512 devices in a mesh: grp: 8 (over x, core), dev: 64 (over y, z).
Axes of the slice: x: 4, y: 8, z: 8, core: 2. Of those that a mesh axis runs over, the one named last changes fastest.
Arguments:
- coords: float32 [262144, 64], P(('grp', 'dev')), may hold values from -6 to 6
- right_side: float32 [262144, 256], P(('grp', 'dev')), may hold values from -6 to 6
- leaf_perm: int32 [512, 512], P(('grp', 'dev')), may hold values from 0 to 511, each once within a row
- near_list: int32 [512, 4], P(('grp', 'dev')), may hold values from -1 to 511, as said below
- far_leaves: int32 [512, 4], P(('grp', 'dev')), may hold values from 0 to 511, as said below
- couplings: bfloat16 [512, 4, 128, 128], P(('grp', 'dev')), may hold values from -0.5 to 0.5
- transfer: bfloat16 [512, 128, 128], P(('grp', 'dev')), may hold values from -0.5 to 0.5
- leaf_basis: bfloat16 [262144, 128], P(('grp', 'dev')), may hold values from -0.25 to 0.25
- cluster_of: int32 [512], P(('grp', 'dev')), may hold values from 0 to 31, as said below
- far_clusters: int32 [32, 4], P('grp'), may hold values from 0 to 31, as said below
- cluster_couplings: bfloat16 [32, 4, 128, 128], P('grp'), may hold values from -0.125 to 0.125
- ridge_weight: float32 [], replicated, may hold values from 0.5 to 2
Outputs:
- solution: float32 [262144, 256], P(('grp', 'dev'))
- residual: float32 [262144, 256], P(('grp', 'dev'))
The draws below stay inside these ranges and needn't reach their ends.
Inputs may be any that keep to these rules, and one draw needn't show every extreme that they name: `near_list`: each row lists leaves of the row's group whose position within the group differs from the row's leaf by 1 to 2, each at most once, in any slot order; -1 marks an empty slot. The number of listed leaves varies from leaf to leaf. `far_leaves`: each row names 4 different leaves of the row's group whose position within the group differs from the row's leaf by more than 2 and at most 8. `cluster_of`: leaves of group g belong to clusters g * 4 to g * 4 + 3, and every cluster holds exactly 16 leaves. `far_clusters`: each row names 4 different clusters, none of them in the row's own group.
All inputs are finite; a program needn't handle non-finite values.
Results may differ from the reference program's by a relative error of at most 0.0033.
Values may be sent and summed in bfloat16 or wider, within the bound.
No kernel may reach another device: no remote copies, remote signals or barrier semaphores. Data moves between devices by JAX's collectives and lax.ppermute only.
A program may use at most 64 MiB of HBM per device.

```python
import jax
import jax.numpy as jnp
from jax import lax

LEAF = 512
DIM = 64
OUT = 256
RANK = 128
REACH = 2
FARREACH = 8
FAR1 = 4
FAR2 = 4
CPG = 4
ITERS = 2
LEAVES = 512
POINTS = 262144
CLUS = 32
LPC = 16
N_GRP = 8
N_DEV = 64


def draw_near_list(key, part):
    count_all = N_GRP * N_DEV
    offset_table = jnp.concatenate([jnp.arange(-REACH, 0), jnp.arange(1, REACH + 1)]).astype(jnp.int32)
    subkeys = jax.random.split(key, 3)
    orders = jax.vmap(lambda single: jax.random.permutation(single, 2 * REACH))(jax.random.split(subkeys[0], count_all))
    offsets = offset_table[orders]
    keep_level = jax.random.randint(subkeys[1], (count_all, 1), 1, 5)
    coin_draws = jax.random.randint(subkeys[2], (count_all, 2 * REACH), 0, 4)
    leaf_index = jnp.arange(count_all, dtype=jnp.int32)[:, None]
    position = leaf_index % N_DEV + offsets
    retained = (coin_draws < keep_level) & (position >= 0) & (position < N_DEV)
    return jnp.where(retained, leaf_index + offsets, -1).astype(jnp.int32)


def draw_far_leaves(key, part):
    count_all = N_GRP * N_DEV
    orders = jax.vmap(lambda single: jax.random.permutation(single, N_DEV))(jax.random.split(jax.random.fold_in(key, 11), count_all))
    leaf_index = jnp.arange(count_all, dtype=jnp.int32)[:, None]
    offset = orders - leaf_index % N_DEV
    allowed = (jnp.abs(offset) > REACH) & (jnp.abs(offset) <= FARREACH)
    ranking = jnp.where(allowed, 0, N_DEV) + jnp.arange(N_DEV, dtype=jnp.int32)[None, :]
    chosen = jnp.argsort(ranking, axis=1)[:, :FAR1]
    picked = jnp.take_along_axis(orders, chosen, axis=1)
    return (leaf_index // N_DEV * N_DEV + picked).astype(jnp.int32)


def draw_cluster_of(key, part):
    per_cluster = N_DEV // CPG
    orders = jax.vmap(lambda single: jax.random.permutation(single, N_DEV))(jax.random.split(jax.random.fold_in(key, 23), N_GRP))
    group_index = jnp.arange(N_GRP, dtype=jnp.int32)[:, None]
    return (group_index * CPG + orders // per_cluster).reshape(N_GRP * N_DEV).astype(jnp.int32)


def draw_far_clusters(key, part):
    count_all = N_GRP * CPG
    orders = jax.vmap(lambda single: jax.random.permutation(single, count_all))(jax.random.split(jax.random.fold_in(key, 37), count_all))
    cluster_index = jnp.arange(count_all, dtype=jnp.int32)[:, None]
    allowed = orders // CPG != cluster_index // CPG
    ranking = jnp.where(allowed, 0, count_all) + jnp.arange(count_all, dtype=jnp.int32)[None, :]
    chosen = jnp.argsort(ranking, axis=1)[:, :FAR2]
    return jnp.take_along_axis(orders, chosen, axis=1).astype(jnp.int32)


def shard_levels(stream_key, extent, cuts, low, largest):
    def one(axis_at, blocks):
        draws = jax.random.uniform(jax.random.fold_in(jax.random.fold_in(stream_key, 6), axis_at), (blocks,), jnp.float32, low / len(cuts), largest / len(cuts))
        return jnp.repeat(jnp.exp(draws), extent[axis_at] // blocks).reshape((-1,) + (1,) * (len(extent) - axis_at - 1))

    level = one(*cuts[0])
    for cut in cuts[1:]:
        level = level * one(*cut)
    return level


def gaussian(key, shape, width, limit, shards=(), held_as=jnp.bfloat16):
    drawn = jax.random.normal(key, shape, jnp.float32) * width
    if len(shards) > 0:
        drawn = shard_levels(key, shape, shards, -0.22, 0.18) * drawn
    return jnp.clip(drawn, min=-limit, max=limit).astype(held_as)


def setup_inputs(seed: int = 0) -> dict:
    streams_of = jax.random.split(jax.random.key(seed), 13)
    return {
        "coords": gaussian(streams_of[0], (POINTS, DIM), 1.0, 6.0, ((0, 512),), jnp.float32),
        "right_side": gaussian(streams_of[1], (POINTS, OUT), 1.0, 6.0, ((0, 512),), jnp.float32),
        "leaf_perm": jax.vmap(lambda own: jax.random.permutation(own, LEAF))(jax.random.split(streams_of[2], LEAVES)).reshape((LEAVES, LEAF)).astype(jnp.int32),
        "near_list": draw_near_list(jax.random.fold_in(streams_of[12], 71), 0),
        "far_leaves": draw_far_leaves(jax.random.fold_in(streams_of[12], 71), 0),
        "couplings": gaussian(streams_of[5], (LEAVES, FAR1, RANK, RANK), RANK ** -0.5, 0.5, ((0, 512),)),
        "transfer": gaussian(streams_of[6], (LEAVES, RANK, RANK), RANK ** -0.5, 0.5, ((0, 512),)),
        "leaf_basis": gaussian(streams_of[7], (POINTS, RANK), LEAF ** -0.5, 0.25, ((0, 512),)),
        "cluster_of": draw_cluster_of(jax.random.fold_in(streams_of[12], 71), 0),
        "far_clusters": draw_far_clusters(jax.random.fold_in(streams_of[12], 71), 0),
        "cluster_couplings": gaussian(streams_of[10], (CLUS, FAR2, RANK, RANK), (RANK * LPC) ** -0.5, 0.125, ((0, 8),)),
        "ridge_weight": jnp.clip(jax.random.uniform(streams_of[11], (), jnp.float32, 0.5, 2.0), 0.5, 2.0),
    }


kernel_scale = 1.0 / 32.0
spectrum_gap = 0.5
spectrum_top = 8.0


def kernel_block(left_points, right_points):
    inner_products = jnp.dot(left_points, right_points.T, precision=lax.Precision.HIGHEST, preferred_element_type=jnp.float32)
    distance = jnp.sum(left_points * left_points, axis=1)[:, None] + jnp.sum(right_points * right_points, axis=1)[None, :] - 2.0 * inner_products
    return jnp.exp(-kernel_scale * distance).astype(jnp.bfloat16)


def place_back(tree_rows, ordering):
    return jnp.zeros_like(tree_rows).at[ordering].set(tree_rows)


def apply_operator(direction, coords, leaf_perm, near_list, far_leaves, couplings, transfer, leaf_basis, cluster_of, far_clusters, cluster_couplings, ridge_weight):
    values = direction.astype(jnp.bfloat16).reshape(LEAVES, LEAF, OUT)
    points = coords.reshape(LEAVES, LEAF, DIM)

    def near_leaf(leaf_id):
        own_points = points[leaf_id]
        accumulated = jnp.dot(kernel_block(own_points, own_points), values[leaf_id], preferred_element_type=jnp.float32)
        for offset in list(range(-REACH, 0)) + list(range(1, REACH + 1)):
            neighbour = jnp.clip(leaf_id + offset, 0, LEAVES - 1)
            listed = jnp.any((near_list[leaf_id] == leaf_id + offset) & (near_list[leaf_id] >= 0)).astype(jnp.float32)
            accumulated = accumulated + listed * jnp.dot(kernel_block(own_points, points[neighbour]), values[neighbour], preferred_element_type=jnp.float32)
        return accumulated

    near_field = lax.map(near_leaf, jnp.arange(LEAVES, dtype=jnp.int32))
    ordered = jnp.take_along_axis(values, leaf_perm[:, :, None], axis=1)
    leaf_bases = leaf_basis.reshape(LEAVES, LEAF, RANK).astype(jnp.float32)
    skeleton = jnp.einsum('lpa,lpo->lao', leaf_bases, ordered.astype(jnp.float32)).astype(jnp.bfloat16)
    transfer_wide = transfer.astype(jnp.float32)
    uplift = jnp.einsum('lba,lbo->lao', transfer_wide, skeleton.astype(jnp.float32))
    cluster_sums = jnp.zeros((CLUS, RANK, OUT), jnp.float32).at[cluster_of].add(uplift).astype(jnp.bfloat16)
    picked = cluster_sums[far_clusters]
    coupled = jnp.einsum('ckab,ckbo->cao', cluster_couplings.astype(jnp.float32), picked.astype(jnp.float32)).astype(jnp.bfloat16)
    partners = skeleton[far_leaves]
    level_one = jnp.einsum('lkab,lkbo->lao', couplings.astype(jnp.float32), partners.astype(jnp.float32))
    local_sum = level_one + jnp.einsum('lab,lbo->lao', transfer_wide, coupled[cluster_of].astype(jnp.float32))
    tree_rows = jnp.einsum('lpa,lao->lpo', leaf_bases, local_sum.astype(jnp.bfloat16).astype(jnp.float32))
    far_field = jax.vmap(place_back)(tree_rows, leaf_perm)
    return ridge_weight * direction + (near_field + far_field).reshape(LEAVES * LEAF, OUT)


def reference(coords, right_side, leaf_perm, near_list, far_leaves, couplings, transfer, leaf_basis, cluster_of, far_clusters, cluster_couplings, ridge_weight):
    bottom_edge = ridge_weight + spectrum_gap
    top_edge = ridge_weight + spectrum_top
    centre = (top_edge + bottom_edge) / 2.0
    spread = (top_edge - bottom_edge) / 2.0
    sigma_ratio = centre / spread
    contraction = 1.0 / sigma_ratio
    direction = right_side / centre
    solution = direction
    residual = right_side
    for rounds in range(ITERS):
        residual = residual - apply_operator(direction, coords, leaf_perm, near_list, far_leaves, couplings, transfer, leaf_basis, cluster_of, far_clusters, cluster_couplings, ridge_weight)
        rho_next = 1.0 / (2.0 * sigma_ratio - contraction)
        direction = rho_next * contraction * direction + (2.0 * rho_next / spread) * residual
        solution = solution + direction
        contraction = rho_next
    return solution, residual
```

```python
import jax
import jax.numpy as jnp
from jax import lax
from jax.experimental import pallas as pl
from jax.experimental.pallas import tpu as pltpu
from jax.sharding import PartitionSpec as P

LEAF, DIM, OUT, RANK = 512, 64, 256, 128
N_GRP, N_DEV, CPG = 8, 64, 4
FAR1, FAR2 = 4, 4
COLS = OUT // N_DEV
NEAR = (-1, 1, -2, 2)

KERNEL_LOG2 = -1.4426950408889634 / 32.0
GAP, TOP = 0.5, 8.0

F32, BF16 = jnp.float32, jnp.bfloat16
VMEM = pl.BlockSpec(memory_space=pltpu.VMEM)
SMEM = pl.BlockSpec(memory_space=pltpu.SMEM)
LIMIT = 48 * 2**20


def dot(a, b, dims=((1,), (0,))):
    return lax.dot_general(a, b, (dims, ((), ())), preferred_element_type=F32)


def call(kernel, name, outs, ins, args, scratch=(), flops=0):
    shapes = [jax.ShapeDtypeStruct(s, t) for s, t in outs]
    return pl.pallas_call(
        kernel,
        name=name,
        out_shape=shapes,
        in_specs=ins,
        out_specs=[VMEM] * len(outs),
        scratch_shapes=list(scratch),
        compiler_params=pltpu.CompilerParams(vmem_limit_bytes=LIMIT),
        cost_estimate=pl.CostEstimate(flops=flops, bytes_accessed=0, transcendentals=0),
    )(*args)


def chebyshev(ridge):
    ridge = jnp.full((1, 1), ridge, F32)
    bottom, top = ridge + GAP, ridge + TOP
    centre, spread = (top + bottom) / 2.0, (top - bottom) / 2.0
    sigma = centre / spread
    rho0 = 1.0 / sigma
    rho1 = 1.0 / (2.0 * sigma - rho0)
    rho2 = 1.0 / (2.0 * sigma - rho1)
    first = (rho1 * rho0, 2.0 * rho1 / spread)
    second = (rho2 * rho1, 2.0 * rho2 / spread)
    return ridge, centre, first, second


def to_owners(values, basis, transfer, staged, rows):
    skeleton = dot(values, basis, ((0,), (0,))).astype(BF16)
    uplift = dot(skeleton, transfer)
    skeleton = skeleton.astype(F32)
    for i in range(COLS):
        part = slice(N_DEV * i, N_DEV * (i + 1))
        staged[pl.ds(i, N_DEV, stride=rows), :] = skeleton[part]
        staged[pl.ds(COLS + i, N_DEV, stride=rows), :] = uplift[part]


def start_kernel(ridge, far, cluster, rs, coords, perm, basis, transfer, wc, sent, placed, staged):
    _, centre, _, _ = chebyshev(ridge[0])
    values = (rs[...] / centre).astype(BF16)
    point = lax.broadcasted_iota(jnp.int32, (LEAF, LEAF), 0)
    pick = jnp.where(point == perm[...], 1.0, 0.0).astype(BF16)
    basis_here = dot(pick, basis[...]).astype(BF16)
    placed[...] = basis_here
    staged[...] = jnp.zeros_like(staged)
    to_owners(values, basis_here, transfer[0], staged, 16)
    lane = lax.broadcasted_iota(jnp.int32, (N_DEV, RANK), 1)
    told = jnp.where(lane == FAR1, (cluster[0] % CPG).astype(F32), 0.0)
    for k in range(FAR1):
        told = jnp.where(lane == k, (far[0, k] % N_DEV).astype(F32), told)
    staged[pl.ds(8, N_DEV, stride=16), :] = told
    sent[...] = staged[...].astype(BF16).reshape(N_DEV, 16, RANK)
    wc[:, :OUT] = values
    high = coords[...].astype(BF16)
    low = (coords[...] - high.astype(F32)).astype(BF16)
    wc[:, OUT : OUT + 2 * DIM] = jnp.concatenate([high, low], axis=1)


def owner_sums(staged, rows, told, sums, narrow):
    lane = lax.broadcasted_iota(jnp.int32, (N_DEV, RANK), 1).astype(F32)
    member = jnp.where(lane == told[:, FAR1 : FAR1 + 1], 1.0, 0.0).astype(BF16)
    uplifts = jnp.concatenate(
        [staged[pl.ds(COLS + i, N_DEV, stride=rows), :] for i in range(COLS)], axis=1
    ).astype(BF16)
    total = dot(member, uplifts, ((0,), (0,)))
    for i in range(COLS):
        narrow[pl.ds(CPG * i, CPG), :] = total[:CPG, RANK * i : RANK * (i + 1)]
    out = narrow[...].astype(BF16)
    for g in range(N_GRP):
        sums[g] = out


def sums_first_kernel(arrived, sums, told, skeletons, staged, narrow):
    staged[...] = arrived[...].astype(F32).reshape(N_DEV * 16, RANK)
    told[...] = staged[pl.ds(8, N_DEV, stride=16), :]
    owner_sums(staged, 16, told[...], sums, narrow)
    skeletons[...] = jnp.concatenate(
        [staged[pl.ds(i, N_DEV, stride=16), :] for i in range(COLS)], axis=1
    ).astype(BF16)


def sums_kernel(arrived, told, sums, skeletons, staged, narrow):
    staged[...] = arrived[...].astype(F32).reshape(N_DEV * 8, RANK)
    owner_sums(staged, 8, told[...], sums, narrow)
    skeletons[...] = jnp.concatenate(
        [staged[pl.ds(i, N_DEV, stride=8), :] for i in range(COLS)], axis=1
    ).astype(BF16)


def partners_kernel(skeletons, told, sent, staged):
    lane = lax.broadcasted_iota(jnp.int32, (N_DEV, N_DEV), 1).astype(F32)
    pick = jnp.concatenate(
        [jnp.where(lane == told[:, k : k + 1], 1.0, 0.0) for k in range(FAR1)], axis=0
    ).astype(BF16)
    picked = dot(pick, skeletons[...])
    for k in range(FAR1):
        for i in range(COLS):
            staged[pl.ds(COLS * k + i, N_DEV, stride=16), :] = picked[
                N_DEV * k : N_DEV * (k + 1), RANK * i : RANK * (i + 1)
            ]
    sent[...] = staged[...].astype(BF16).reshape(N_DEV, 16, RANK)


def couple_kernel(far_clusters, all_sums, blocks, told, sent):
    rows = COLS * CPG
    sums = all_sums[...].reshape(N_GRP * rows, RANK)
    row = lax.broadcasted_iota(jnp.int32, (rows, N_GRP * rows), 0)
    lane = lax.broadcasted_iota(jnp.int32, (rows, N_GRP * rows), 1)
    column, cluster = row // CPG, row % CPG
    total = jnp.zeros((rows, CPG * RANK), F32)
    for k in range(FAR2):
        target = CPG * column
        for c in range(CPG):
            f = far_clusters[c, k]
            target += jnp.where(cluster == c, rows * (f // CPG) + f % CPG, 0)
        pick = jnp.where(lane == target, 1.0, 0.0).astype(BF16)
        picked = dot(pick, sums).astype(BF16)
        block = blocks[:, k].reshape(CPG * RANK, RANK)
        total += dot(picked, block, ((1,), (1,)))
    coupled = jnp.zeros((rows, RANK), F32)
    own = cluster[:, :RANK]
    for c in range(CPG):
        coupled += jnp.where(own == c, total[:, RANK * c : RANK * (c + 1)], 0.0)
    coupled = coupled.astype(BF16)
    lane = lax.broadcasted_iota(jnp.int32, (N_DEV, rows), 1).astype(F32)
    pick = jnp.concatenate(
        [jnp.where(lane == told[:, FAR1 : FAR1 + 1] + CPG * i, 1.0, 0.0) for i in range(COLS)], axis=0
    ).astype(BF16)
    out = dot(pick, coupled)
    for i in range(COLS):
        sent[:, i, :] = out[N_DEV * i : N_DEV * (i + 1)]


def far_field(partners, coupled, couplings, transfer, basis, staged):
    staged[...] = partners[...].astype(F32).reshape(N_DEV * 16, RANK)
    local = jnp.zeros((RANK, OUT), F32)
    for k in range(FAR1):
        skeleton = jnp.concatenate(
            [staged[pl.ds(COLS * k + i, N_DEV, stride=16), :] for i in range(COLS)], axis=0
        ).astype(BF16)
        local += dot(couplings[0, k], skeleton, ((1,), (1,)))
    downward = jnp.concatenate([coupled[:, i, :] for i in range(COLS)], axis=0).astype(BF16)
    local += dot(transfer[0], downward, ((1,), (1,)))
    return dot(basis[...], local.astype(BF16))


def middle_kernel(ridge, partners, coupled, couplings, transfer, basis, near, rs, w, sent, d2, r1, staged, staged_out):
    ridge, centre, (mul, add), _ = chebyshev(ridge[0])
    far = far_field(partners, coupled, couplings, transfer, basis, staged)
    d1 = rs[...] / centre
    residual = rs[...] - (ridge * d1 + (near[...] + far))
    direction = mul * d1 + add * residual
    r1[...] = residual
    d2[...] = direction
    values = direction.astype(BF16)
    w[...] = values
    to_owners(values, basis[...], transfer[0], staged_out, 8)
    sent[...] = staged_out[...].astype(BF16).reshape(N_DEV, 8, RANK)


def end_kernel(ridge, partners, coupled, couplings, transfer, basis, near, rs, d2, r1, solution, residual, staged):
    ridge, centre, _, (mul, add) = chebyshev(ridge[0])
    far = far_field(partners, coupled, couplings, transfer, basis, staged)
    r2 = r1[...] - (ridge * d2[...] + (near[...] + far))
    residual[...] = r2
    d3 = mul * d2[...] + add * r2
    solution[...] = rs[...] / centre + d2[...] + d3


def norms(points):
    square = jnp.sum(points * points, axis=1, keepdims=True) * KERNEL_LOG2
    return square, jnp.broadcast_to(square, (LEAF, RANK)).T[:1]


def listed(near_list, offset):
    leaf = lax.axis_index("grp") * N_DEV + lax.axis_index("dev")
    hit = near_list[0, 0] == leaf + offset
    for k in range(1, len(NEAR)):
        hit = hit | (near_list[0, k] == leaf + offset)
    return hit


def block_times(here, there, block, total, fresh):
    high, low = here[:, OUT : OUT + DIM], here[:, OUT + DIM : OUT + 2 * DIM]
    left = jnp.concatenate([high, high, low, low], axis=1)
    column, _ = norms(high.astype(F32) + low.astype(F32))
    high, low = there[:, OUT : OUT + DIM], there[:, OUT + DIM : OUT + 2 * DIM]
    right = jnp.concatenate([high, low, high, low], axis=1)
    _, across = norms(high.astype(F32) + low.astype(F32))
    step = 128
    for r in range(0, LEAF, step):
        part = slice(r, r + step)
        inner = dot(left[part], right, ((1,), (1,)))
        entries = jnp.exp2((column[part] + across) - (2.0 * KERNEL_LOG2) * inner).astype(BF16)
        block[part] = entries
        product = dot(entries, there[:, :OUT])
        total[part] = product if fresh else total[part] + product


def near_own_kernel(here, block, total):
    block_times(here, here, block, total, True)


def near_pair_kernel(offsets, near_list, here, before, first, second, block1, block2, total):
    total[...] = before[...]
    for offset, there, block in zip(offsets, (first, second), (block1, block2)):

        @pl.when(listed(near_list, offset))
        def _():
            block_times(here, there, block, total, False)


def again_own_kernel(w, block, total):
    total[...] = dot(block[...], w[...])


def again_pair_kernel(offsets, near_list, before, first, second, block1, block2, total):
    total[...] = before[...]
    for offset, there, block in zip(offsets, (first, second), (block1, block2)):

        @pl.when(listed(near_list, offset))
        def _():
            total[...] += dot(block[...], there[...])


def from_behind(shard, by):
    pairs = [(i, i + by) for i in range(N_DEV) if 0 <= i + by < N_DEV]
    return lax.ppermute(shard, "dev", pairs)


def exchanged(blocks, axis):
    return lax.all_to_all(blocks, axis, split_axis=0, concat_axis=0, tiled=True)


def body(
    coords,
    right_side,
    leaf_perm,
    near_list,
    far_leaves,
    couplings,
    transfer,
    leaf_basis,
    cluster_of,
    far_clusters,
    cluster_couplings,
    ridge_weight,
):
    ridge = ridge_weight.reshape(1)
    field = ((LEAF, OUT), F32)
    block = ((LEAF, LEAF), BF16)
    rows16 = pltpu.VMEM((N_DEV * 16, RANK), F32)
    rows8 = pltpu.VMEM((N_DEV * 8, RANK), F32)
    narrow = pltpu.VMEM((COLS * CPG, RANK), F32)
    pair_outs = [block, block, field]
    gmul = 2 * LEAF * LEAF * OUT

    wc, sent, basis = call(
        start_kernel,
        "start",
        [((LEAF, OUT + 2 * DIM), BF16), ((N_DEV, 16, RANK), BF16), ((LEAF, RANK), BF16)],
        [SMEM, SMEM, SMEM] + [VMEM] * 5,
        (ridge, far_leaves, cluster_of, right_side, coords, leaf_perm, leaf_basis, transfer),
        [rows16],
        gmul,
    )
    arrived = exchanged(sent, "dev")
    neighbours = [from_behind(wc, -offset) for offset in NEAR]
    own_block, near = call(near_own_kernel, "near_own", [block, field], [VMEM], (wc,), flops=2 * gmul)

    sums, told, skeletons = call(
        sums_first_kernel,
        "sums_first",
        [((N_GRP, 16, RANK), BF16), ((N_DEV, RANK), F32), ((N_DEV, COLS * RANK), BF16)],
        [VMEM],
        (arrived,),
        [rows16, narrow],
        gmul // 4,
    )

    def through_owners(sums, skeletons):
        all_sums = exchanged(sums, "grp")
        (partners,) = call(
            partners_kernel, "partners", [((N_DEV, 16, RANK), BF16)], [VMEM] * 2, (skeletons, told), [rows16], gmul // 4
        )
        partners = exchanged(partners, "dev")
        (coupled,) = call(
            couple_kernel,
            "couple",
            [((N_DEV, COLS, RANK), F32)],
            [SMEM] + [VMEM] * 3,
            (far_clusters, all_sums, cluster_couplings, told),
            flops=gmul // 4,
        )
        return partners, exchanged(coupled, "dev")

    partners, coupled = through_owners(sums, skeletons)
    blocks = []
    for at in (0, 2):
        b1, b2, near = call(
            lambda *refs, at=at: near_pair_kernel(NEAR[at : at + 2], *refs),
            f"near_pair_{at}",
            pair_outs,
            [SMEM] + [VMEM] * 4,
            (near_list, wc, near, neighbours[at], neighbours[at + 1]),
            flops=4 * gmul,
        )
        blocks += [b1, b2]

    w, sent, d2, r1 = call(
        middle_kernel,
        "middle",
        [((LEAF, OUT), BF16), ((N_DEV, 8, RANK), BF16), field, field],
        [SMEM] + [VMEM] * 7,
        (ridge, partners, coupled, couplings, transfer, basis, near, right_side),
        [rows16, rows8],
        gmul,
    )
    arrived = exchanged(sent, "dev")
    neighbours = [from_behind(w, -offset) for offset in NEAR]
    (near,) = call(again_own_kernel, "again_own", [field], [VMEM] * 2, (w, own_block), flops=gmul)
    sums, skeletons = call(
        sums_kernel,
        "sums",
        [((N_GRP, 16, RANK), BF16), ((N_DEV, COLS * RANK), BF16)],
        [VMEM] * 2,
        (arrived, told),
        [rows8, narrow],
        gmul // 4,
    )
    partners, coupled = through_owners(sums, skeletons)
    for at in (0, 2):
        (near,) = call(
            lambda *refs, at=at: again_pair_kernel(NEAR[at : at + 2], *refs),
            f"again_pair_{at}",
            [field],
            [SMEM] + [VMEM] * 5,
            (near_list, near, neighbours[at], neighbours[at + 1], blocks[at], blocks[at + 1]),
            flops=2 * gmul,
        )
    return tuple(
        call(
            end_kernel,
            "end",
            [field, field],
            [SMEM] + [VMEM] * 9,
            (ridge, partners, coupled, couplings, transfer, basis, near, right_side, d2, r1),
            [rows16],
            gmul,
        )
    )


def solution(mesh):
    placed = (
        P(("grp", "dev"), None),
        P(("grp", "dev"), None),
        P(("grp", "dev"), None),
        P(("grp", "dev"), None),
        P(("grp", "dev"), None),
        P(("grp", "dev"), None, None, None),
        P(("grp", "dev"), None, None),
        P(("grp", "dev"), None),
        P(("grp", "dev")),
        P("grp", None),
        P("grp", None, None, None),
        P(),
    )
    return jax.shard_map(
        body,
        mesh=mesh,
        in_specs=placed,
        out_specs=(P(("grp", "dev"), None), P(("grp", "dev"), None)),
        check_vma=False,
    )
```

```python
import jax
import jax.numpy as jnp
from jax import lax
from jax.experimental import pallas as pl
from jax.experimental.pallas import tpu as pltpu
from jax.sharding import PartitionSpec as P

LEAF, DIM, OUT, RANK = 512, 64, 256, 128
N_GRP, N_DEV, CPG = 8, 64, 4
FAR1, FAR2 = 4, 4
COLS = OUT // N_DEV
NEAR = (-1, 1, -2, 2)

KERNEL_LOG2 = -1.4426950408889634 / 32.0
GAP, TOP = 0.5, 8.0

F32, BF16 = jnp.float32, jnp.bfloat16
VMEM = pl.BlockSpec(memory_space=pltpu.VMEM)
SMEM = pl.BlockSpec(memory_space=pltpu.SMEM)
ANY = pl.BlockSpec(memory_space=pl.ANY)
LIMIT = 48 * 2**20


def dot(a, b, dims=((1,), (0,))):
    return lax.dot_general(a, b, (dims, ((), ())), preferred_element_type=F32)


def call(kernel, name, outs, ins, args, scratch=(), flops=0):
    shapes = [jax.ShapeDtypeStruct(s, t) for s, t in outs]
    return pl.pallas_call(
        kernel,
        name=name,
        out_shape=shapes,
        in_specs=ins,
        out_specs=[VMEM] * len(outs),
        scratch_shapes=list(scratch),
        compiler_params=pltpu.CompilerParams(vmem_limit_bytes=LIMIT),
        cost_estimate=pl.CostEstimate(flops=flops, bytes_accessed=0, transcendentals=0),
    )(*args)


def chebyshev(ridge):
    ridge = jnp.full((1, 1), ridge, F32)
    bottom, top = ridge + GAP, ridge + TOP
    centre, spread = (top + bottom) / 2.0, (top - bottom) / 2.0
    sigma = centre / spread
    rho0 = 1.0 / sigma
    rho1 = 1.0 / (2.0 * sigma - rho0)
    rho2 = 1.0 / (2.0 * sigma - rho1)
    first = (rho1 * rho0, 2.0 * rho1 / spread)
    second = (rho2 * rho1, 2.0 * rho2 / spread)
    return ridge, centre, first, second


def to_owners(values, basis, transfer, staged, rows):
    skeleton = dot(values, basis, ((0,), (0,))).astype(BF16)
    uplift = dot(skeleton, transfer)
    skeleton = skeleton.astype(F32)
    for i in range(COLS):
        part = slice(N_DEV * i, N_DEV * (i + 1))
        staged[pl.ds(i, N_DEV, stride=rows), :] = skeleton[part]
        staged[pl.ds(COLS + i, N_DEV, stride=rows), :] = uplift[part]


def start_kernel(ridge, far, cluster, rs, coords, perm, basis, transfer, wc, sent, placed, staged):
    _, centre, _, _ = chebyshev(ridge[0])
    values = (rs[...] / centre).astype(BF16)
    point = lax.broadcasted_iota(jnp.int32, (LEAF, LEAF), 0)
    pick = jnp.where(point == perm[...], 1.0, 0.0).astype(BF16)
    basis_here = dot(pick, basis[...]).astype(BF16)
    placed[...] = basis_here
    staged[...] = jnp.zeros_like(staged)
    to_owners(values, basis_here, transfer[0], staged, 16)
    lane = lax.broadcasted_iota(jnp.int32, (N_DEV, RANK), 1)
    told = jnp.where(lane == FAR1, (cluster[0] % CPG).astype(F32), 0.0)
    for k in range(FAR1):
        told = jnp.where(lane == k, (far[0, k] % N_DEV).astype(F32), told)
    staged[pl.ds(8, N_DEV, stride=16), :] = told
    sent[...] = staged[...].astype(BF16).reshape(N_DEV, 16, RANK)
    wc[:LEAF] = values
    high = coords[...].astype(BF16)
    low = (coords[...] - high.astype(F32)).astype(BF16)
    parts = jnp.concatenate([high, low], axis=0)
    wc[LEAF : LEAF + 2 * DIM] = parts[:, :OUT]
    wc[LEAF + 2 * DIM :] = parts[:, OUT:]


def owner_sums(staged, rows, told, sums, narrow):
    lane = lax.broadcasted_iota(jnp.int32, (N_DEV, RANK), 1).astype(F32)
    member = jnp.where(lane == told[:, FAR1 : FAR1 + 1], 1.0, 0.0).astype(BF16)
    uplifts = jnp.concatenate(
        [staged[pl.ds(COLS + i, N_DEV, stride=rows), :] for i in range(COLS)], axis=1
    ).astype(BF16)
    total = dot(member, uplifts, ((0,), (0,)))
    for i in range(COLS):
        narrow[pl.ds(CPG * i, CPG), :] = total[:CPG, RANK * i : RANK * (i + 1)]
    out = narrow[...].astype(BF16)
    for g in range(N_GRP):
        sums[g] = out


def sums_first_kernel(arrived, _, sums, told, skeletons, staged, narrow):
    staged[...] = arrived[...].astype(F32).reshape(N_DEV * 16, RANK)
    told[...] = staged[pl.ds(8, N_DEV, stride=16), :]
    owner_sums(staged, 16, told[...], sums, narrow)
    skeletons[...] = jnp.concatenate(
        [staged[pl.ds(i, N_DEV, stride=16), :] for i in range(COLS)], axis=1
    ).astype(BF16)


def sums_kernel(arrived, told, _, sums, skeletons, staged, narrow):
    staged[...] = arrived[...].astype(F32).reshape(N_DEV * 8, RANK)
    owner_sums(staged, 8, told[...], sums, narrow)
    skeletons[...] = jnp.concatenate(
        [staged[pl.ds(i, N_DEV, stride=8), :] for i in range(COLS)], axis=1
    ).astype(BF16)


def partners_kernel(skeletons, told, sent, staged):
    lane = lax.broadcasted_iota(jnp.int32, (N_DEV, N_DEV), 1).astype(F32)
    pick = jnp.concatenate(
        [jnp.where(lane == told[:, k : k + 1], 1.0, 0.0) for k in range(FAR1)], axis=0
    ).astype(BF16)
    picked = dot(pick, skeletons[...])
    for k in range(FAR1):
        for i in range(COLS):
            staged[pl.ds(COLS * k + i, N_DEV, stride=16), :] = picked[
                N_DEV * k : N_DEV * (k + 1), RANK * i : RANK * (i + 1)
            ]
    sent[...] = staged[...].astype(BF16).reshape(N_DEV, 16, RANK)


def couple_kernel(far_clusters, all_sums, blocks, told, partners, _, sent, staged):
    rows = COLS * CPG
    sums = all_sums[...].reshape(N_GRP * rows, RANK)
    row = lax.broadcasted_iota(jnp.int32, (rows, N_GRP * rows), 0)
    lane = lax.broadcasted_iota(jnp.int32, (rows, N_GRP * rows), 1)
    column, cluster = row // CPG, row % CPG
    total = jnp.zeros((rows, CPG * RANK), F32)
    for k in range(FAR2):
        target = CPG * column
        for c in range(CPG):
            f = far_clusters[c, k]
            target += jnp.where(cluster == c, rows * (f // CPG) + f % CPG, 0)
        pick = jnp.where(lane == target, 1.0, 0.0).astype(BF16)
        picked = dot(pick, sums).astype(BF16)
        block = blocks[:, k].reshape(CPG * RANK, RANK)
        total += dot(picked, block, ((1,), (1,)))
    coupled = jnp.zeros((rows, RANK), F32)
    own = cluster[:, :RANK]
    for c in range(CPG):
        coupled += jnp.where(own == c, total[:, RANK * c : RANK * (c + 1)], 0.0)
    coupled = coupled.astype(BF16)
    lane = lax.broadcasted_iota(jnp.int32, (N_DEV, rows), 1).astype(F32)
    pick = jnp.concatenate(
        [jnp.where(lane == told[:, FAR1 : FAR1 + 1] + CPG * i, 1.0, 0.0) for i in range(COLS)], axis=0
    ).astype(BF16)
    out = dot(pick, coupled)
    staged[:, :16, :] = partners[...].astype(F32)
    staged[:, 16:, :] = jnp.zeros((N_DEV, 8, RANK), F32)
    for i in range(COLS):
        staged[:, 16 + i, :] = out[N_DEV * i : N_DEV * (i + 1)]
    sent[...] = staged[...].astype(BF16)


def far_field(arrived, couplings, transfer, basis, staged):
    staged[...] = arrived[...].astype(F32).reshape(N_DEV * 24, RANK)
    local = jnp.zeros((RANK, OUT), F32)
    for k in range(FAR1 + 1):
        skeleton = jnp.concatenate(
            [staged[pl.ds(COLS * k + i, N_DEV, stride=24), :] for i in range(COLS)], axis=0
        ).astype(BF16)
        local += dot(couplings[0, k] if k < FAR1 else transfer[0], skeleton, ((1,), (1,)))
    return dot(basis[...], local.astype(BF16))


def middle_kernel(ridge, arrived, couplings, transfer, basis, near, rs, w, sent, d2, r1, staged, staged_out):
    ridge, centre, (mul, add), _ = chebyshev(ridge[0])
    far = far_field(arrived, couplings, transfer, basis, staged)
    d1 = rs[...] / centre
    residual = rs[...] - (ridge * d1 + (near[...] + far))
    direction = mul * d1 + add * residual
    r1[...] = residual
    d2[...] = direction
    values = direction.astype(BF16)
    w[...] = values
    to_owners(values, basis[...], transfer[0], staged_out, 8)
    sent[...] = staged_out[...].astype(BF16).reshape(N_DEV, 8, RANK)


def end_kernel(ridge, arrived, couplings, transfer, basis, near, rs, d2, r1, solution, residual, staged):
    ridge, centre, _, (mul, add) = chebyshev(ridge[0])
    far = far_field(arrived, couplings, transfer, basis, staged)
    r2 = r1[...] - (ridge * d2[...] + (near[...] + far))
    residual[...] = r2
    d3 = mul * d2[...] + add * r2
    solution[...] = rs[...] / centre + d2[...] + d3


def coordinates(wc):
    parts = jnp.concatenate([wc[LEAF : LEAF + 2 * DIM], wc[LEAF + 2 * DIM :]], axis=1)
    high, low = parts[:DIM], parts[DIM:]
    points = high.astype(F32) + low.astype(F32)
    return high, low, jnp.sum(points * points, axis=0, keepdims=True) * KERNEL_LOG2


def listed(near_list, offset):
    leaf = lax.axis_index("grp") * N_DEV + lax.axis_index("dev")
    hit = near_list[0, 0] == leaf + offset
    for k in range(1, len(NEAR)):
        hit = hit | (near_list[0, k] == leaf + offset)
    return hit


def block_times(here, there, block, total, fresh):
    high, low, norm = coordinates(here)
    left = jnp.concatenate([high, high, low, low], axis=0)
    column = jnp.broadcast_to(norm, (RANK, LEAF)).T[:, :1]
    high, low, across = coordinates(there)
    right = jnp.concatenate([high, low, high, low], axis=0)
    step = 128
    for r in range(0, LEAF, step):
        part = slice(r, r + step)
        inner = dot(left[:, part], right, ((0,), (0,)))
        entries = jnp.exp2((column[part] + across) - (2.0 * KERNEL_LOG2) * inner).astype(BF16)
        block[part] = entries
        product = dot(entries, there[:LEAF])
        total[part] = product if fresh else total[part] + product


def near_own_kernel(here, block, total):
    block_times(here, here, block, total, True)


def near_pair_kernel(offsets, near_list, here, before, first, second, block1, block2, total):
    total[...] = before[...]
    for offset, there, block in zip(offsets, (first, second), (block1, block2)):

        @pl.when(listed(near_list, offset))
        def _():
            block_times(here, there, block, total, False)


def again_own_kernel(w, block, total):
    total[...] = dot(block[...], w[...])


def again_pair_kernel(offsets, near_list, before, first, second, block1, block2, total):
    total[...] = before[...]
    for offset, there, block in zip(offsets, (first, second), (block1, block2)):

        @pl.when(listed(near_list, offset))
        def _():
            total[...] += dot(block[...], there[...])


def from_behind(shard, by):
    pairs = [(i, i + by) for i in range(N_DEV) if 0 <= i + by < N_DEV]
    return lax.ppermute(shard, "dev", pairs)


def exchanged(blocks, axis):
    return lax.all_to_all(blocks, axis, split_axis=0, concat_axis=0, tiled=True)


def body(
    coords,
    right_side,
    leaf_perm,
    near_list,
    far_leaves,
    couplings,
    transfer,
    leaf_basis,
    cluster_of,
    far_clusters,
    cluster_couplings,
    ridge_weight,
):
    ridge = ridge_weight.reshape(1)
    field = ((LEAF, OUT), F32)
    block = ((LEAF, LEAF), BF16)
    rows24 = pltpu.VMEM((N_DEV * 24, RANK), F32)
    rows16 = pltpu.VMEM((N_DEV * 16, RANK), F32)
    rows8 = pltpu.VMEM((N_DEV * 8, RANK), F32)
    narrow = pltpu.VMEM((COLS * CPG, RANK), F32)
    gmul = 2 * LEAF * LEAF * OUT

    wc, sent, basis = call(
        start_kernel,
        "start",
        [((LEAF + 4 * DIM, OUT), BF16), ((N_DEV, 16, RANK), BF16), ((LEAF, RANK), BF16)],
        [SMEM, SMEM, SMEM] + [VMEM] * 5,
        (ridge, far_leaves, cluster_of, right_side, coords.T, leaf_perm, leaf_basis, transfer),
        [rows16],
        gmul,
    )
    arrived = exchanged(sent, "dev")
    behind, ahead = from_behind(wc, 1), from_behind(wc, -1)
    own_block, near = call(near_own_kernel, "near_own", [block, field], [VMEM], (wc,), flops=2 * gmul)
    sums, told, skeletons = call(
        sums_first_kernel,
        "sums_first",
        [((N_GRP, 16, RANK), BF16), ((N_DEV, RANK), F32), ((N_DEV, COLS * RANK), BF16)],
        [VMEM, ANY],
        (arrived, near),
        [rows16, narrow],
        gmul // 4,
    )

    def near_first(at, near, first, second):
        return call(
            lambda *refs: near_pair_kernel(NEAR[at : at + 2], *refs),
            f"near_pair_{at}",
            [block, block, field],
            [SMEM] + [VMEM] * 4,
            (near_list, wc, near, first, second),
            flops=4 * gmul,
        )

    def near_again(at, near, first, second):
        return call(
            lambda *refs: again_pair_kernel(NEAR[at : at + 2], *refs),
            f"again_pair_{at}",
            [field],
            [SMEM] + [VMEM] * 5,
            (near_list, near, first, second, blocks[at], blocks[at + 1]),
            flops=2 * gmul,
        )

    def partners_of(skeletons):
        (partners,) = call(
            partners_kernel, "partners", [((N_DEV, 16, RANK), BF16)], [VMEM] * 2, (skeletons, told), [rows16], gmul // 4
        )
        return partners

    def through_owners(all_sums, partners, near):
        (sent,) = call(
            couple_kernel,
            "couple",
            [((N_DEV, 24, RANK), BF16)],
            [SMEM] + [VMEM] * 4 + [ANY],
            (far_clusters, all_sums, cluster_couplings, told, partners, near),
            [pltpu.VMEM((N_DEV, 24, RANK), F32)],
            gmul // 4,
        )
        return exchanged(sent, "dev")

    all_sums = exchanged(sums, "grp")
    partners = partners_of(skeletons)
    blocks = [None] * len(NEAR)
    blocks[0], blocks[1], near = near_first(0, near, behind, ahead)
    arrived = through_owners(all_sums, partners, near)
    behind, ahead = from_behind(behind, 1), from_behind(ahead, -1)
    blocks[2], blocks[3], near = near_first(2, near, behind, ahead)

    w, sent, d2, r1 = call(
        middle_kernel,
        "middle",
        [((LEAF, OUT), BF16), ((N_DEV, 8, RANK), BF16), field, field],
        [SMEM] + [VMEM] * 6,
        (ridge, arrived, couplings, transfer, basis, near, right_side),
        [rows24, rows8],
        gmul,
    )
    arrived = exchanged(sent, "dev")
    behind, ahead = from_behind(w, 1), from_behind(w, -1)
    (near,) = call(again_own_kernel, "again_own", [field], [VMEM] * 2, (w, own_block), flops=gmul)
    sums, skeletons = call(
        sums_kernel,
        "sums",
        [((N_GRP, 16, RANK), BF16), ((N_DEV, COLS * RANK), BF16)],
        [VMEM, VMEM, ANY],
        (arrived, told, near),
        [rows8, narrow],
        gmul // 4,
    )
    all_sums = exchanged(sums, "grp")
    partners = partners_of(skeletons)
    (near,) = near_again(0, near, behind, ahead)
    arrived = through_owners(all_sums, partners, near)
    behind, ahead = from_behind(behind, 1), from_behind(ahead, -1)
    (near,) = near_again(2, near, behind, ahead)
    return tuple(
        call(
            end_kernel,
            "end",
            [field, field],
            [SMEM] + [VMEM] * 8,
            (ridge, arrived, couplings, transfer, basis, near, right_side, d2, r1),
            [rows24],
            gmul,
        )
    )


def solution(mesh):
    placed = (
        P(("grp", "dev"), None),
        P(("grp", "dev"), None),
        P(("grp", "dev"), None),
        P(("grp", "dev"), None),
        P(("grp", "dev"), None),
        P(("grp", "dev"), None, None, None),
        P(("grp", "dev"), None, None),
        P(("grp", "dev"), None),
        P(("grp", "dev")),
        P("grp", None),
        P("grp", None, None, None),
        P(),
    )
    return jax.shard_map(
        body,
        mesh=mesh,
        in_specs=placed,
        out_specs=(P(("grp", "dev"), None), P(("grp", "dev"), None)),
        check_vma=False,
    )
```

```python
import jax
import jax.numpy as jnp
from jax import lax
from jax.experimental import pallas as pl
from jax.experimental.pallas import tpu as pltpu
from jax.sharding import PartitionSpec as P

LEAF, DIM, OUT, RANK = 512, 64, 256, 128
N_GRP, N_DEV, CPG = 8, 64, 4
FAR1, FAR2 = 4, 4
COLS = OUT // N_DEV
NEAR = (-1, 1, -2, 2)

KERNEL_LOG2 = -1.4426950408889634 / 32.0
GAP, TOP = 0.5, 8.0

F32, BF16 = jnp.float32, jnp.bfloat16
VMEM = pl.BlockSpec(memory_space=pltpu.VMEM)
SMEM = pl.BlockSpec(memory_space=pltpu.SMEM)
ANY = pl.BlockSpec(memory_space=pl.ANY)
HBM = pl.BlockSpec(memory_space=pltpu.HBM)
LIMIT = 32 * 2**20
SHORT, LONG = 10**7, 10**10
ROWS = 128


def dot(a, b, dims=((1,), (0,))):
    return lax.dot_general(a, b, (dims, ((), ())), preferred_element_type=F32)


def call(kernel, name, outs, ins, args, scratch=(), flops=0, aliases=None):
    shapes = [(pltpu.HBM if spec is HBM else jax.ShapeDtypeStruct)(shape, kind) for shape, kind, spec in outs]
    args = [
        pltpu.with_memory_space_constraint(arg, pltpu.HBM) if spec is HBM else arg for arg, spec in zip(args, ins)
    ]
    return pl.pallas_call(
        kernel,
        name=name,
        out_shape=shapes,
        in_specs=ins,
        out_specs=[spec for _, _, spec in outs],
        scratch_shapes=list(scratch),
        input_output_aliases=aliases or {},
        compiler_params=pltpu.CompilerParams(vmem_limit_bytes=LIMIT),
        cost_estimate=pl.CostEstimate(flops=flops, bytes_accessed=0, transcendentals=0),
    )(*args)


def started(pairs, sems, first=0):
    copies = [pltpu.make_async_copy(a, b, sems.at[first + i]) for i, (a, b) in enumerate(pairs)]
    for copy in copies:
        copy.start()
    return copies


def wait(copies):
    for copy in copies:
        copy.wait()


def chebyshev(ridge):
    ridge = jnp.full((1, 1), ridge, F32)
    bottom, top = ridge + GAP, ridge + TOP
    centre, spread = (top + bottom) / 2.0, (top - bottom) / 2.0
    sigma = centre / spread
    rho0 = 1.0 / sigma
    rho1 = 1.0 / (2.0 * sigma - rho0)
    rho2 = 1.0 / (2.0 * sigma - rho1)
    first = (rho1 * rho0, 2.0 * rho1 / spread)
    second = (rho2 * rho1, 2.0 * rho2 / spread)
    return ridge, centre, first, second


def to_owners(values, basis, transfer, staged, rows):
    skeleton = dot(values, basis, ((0,), (0,))).astype(BF16)
    uplift = dot(skeleton, transfer)
    skeleton = skeleton.astype(F32)
    for i in range(COLS):
        part = slice(N_DEV * i, N_DEV * (i + 1))
        staged[pl.ds(i, N_DEV, stride=rows), :] = skeleton[part]
        staged[pl.ds(COLS + i, N_DEV, stride=rows), :] = uplift[part]


def start_kernel(
    ridge, cluster, far_in, rs_in, coords_in, perm_in, basis_in, transfer_in, wc_out, sent_out, placed_out,
    far, rs, coords, perm, basis, transfer, wc, sent, placed, staged, sems,
):
    copies = started(
        (
            (perm_in, perm), (basis_in, basis), (rs_in, rs), (coords_in, coords),
            (transfer_in, transfer), (far_in, far),
        ),
        sems,
    )
    staged[...] = jnp.zeros_like(staged)
    _, centre, _, _ = chebyshev(ridge[0])
    wait(copies[:2])
    point = lax.broadcasted_iota(jnp.int32, (LEAF, LEAF), 0)
    pick = jnp.where(point == perm[...], 1.0, 0.0).astype(BF16)
    basis_here = dot(pick, basis[...]).astype(BF16)
    placed[...] = basis_here
    wait(copies[2:4])
    values = (rs[...] / centre).astype(BF16)
    wc[:LEAF] = values
    high = coords[...].astype(BF16)
    low = (coords[...] - high.astype(F32)).astype(BF16)
    parts = jnp.concatenate([high, low], axis=0)
    wc[LEAF : LEAF + 2 * DIM] = parts[:, :OUT]
    wc[LEAF + 2 * DIM :] = parts[:, OUT:]
    outs = started(((wc, wc_out), (placed, placed_out)), sems, 6)
    wait(copies[4:])
    to_owners(values, basis_here, transfer[0], staged, 16)
    lane = lax.broadcasted_iota(jnp.int32, (N_DEV, RANK), 1)
    told = jnp.where(lane == FAR1, (cluster[0] % CPG).astype(F32), 0.0)
    for k in range(FAR1):
        told = jnp.where(lane == k, (far[0, k] % N_DEV).astype(F32), told)
    staged[pl.ds(8, N_DEV, stride=16), :] = told
    sent[...] = staged[...].astype(BF16).reshape(N_DEV, 16, RANK)
    outs += started(((sent, sent_out),), sems, 8)
    wait(outs)


def owner_sums(staged, rows, told, sums, narrow):
    lane = lax.broadcasted_iota(jnp.int32, (N_DEV, RANK), 1).astype(F32)
    member = jnp.where(lane == told[:, FAR1 : FAR1 + 1], 1.0, 0.0).astype(BF16)
    uplifts = jnp.concatenate(
        [staged[pl.ds(COLS + i, N_DEV, stride=rows), :] for i in range(COLS)], axis=1
    ).astype(BF16)
    total = dot(member, uplifts, ((0,), (0,)))
    for i in range(COLS):
        narrow[pl.ds(CPG * i, CPG), :] = total[:CPG, RANK * i : RANK * (i + 1)]
    out = narrow[...].astype(BF16)
    for g in range(N_GRP):
        sums[g] = out


def sums_first_kernel(arrived, _, sums, told, skeletons, staged, narrow):
    staged[...] = arrived[...].astype(F32).reshape(N_DEV * 16, RANK)
    told[...] = staged[pl.ds(8, N_DEV, stride=16), :]
    owner_sums(staged, 16, told[...], sums, narrow)
    skeletons[...] = jnp.concatenate(
        [staged[pl.ds(i, N_DEV, stride=16), :] for i in range(COLS)], axis=1
    ).astype(BF16)


def sums_kernel(arrived, told, _, sums, skeletons, staged, narrow):
    staged[...] = arrived[...].astype(F32).reshape(N_DEV * 8, RANK)
    owner_sums(staged, 8, told[...], sums, narrow)
    skeletons[...] = jnp.concatenate(
        [staged[pl.ds(i, N_DEV, stride=8), :] for i in range(COLS)], axis=1
    ).astype(BF16)


def partners_kernel(skeletons, told, sent_out, staged, sent, sems):
    lane = lax.broadcasted_iota(jnp.int32, (N_DEV, N_DEV), 1).astype(F32)
    pick = jnp.concatenate(
        [jnp.where(lane == told[:, k : k + 1], 1.0, 0.0) for k in range(FAR1)], axis=0
    ).astype(BF16)
    picked = dot(pick, skeletons[...])
    for k in range(FAR1):
        for i in range(COLS):
            staged[pl.ds(COLS * k + i, N_DEV, stride=16), :] = picked[
                N_DEV * k : N_DEV * (k + 1), RANK * i : RANK * (i + 1)
            ]
    sent[...] = staged[...].reshape(N_DEV, 2, 8, RANK).astype(BF16)
    wait(started(((sent, sent_out.at[:, :2]),), sems))


def couple_kernel(far_clusters, all_sums, blocks, told, _, sent_out, staged, sent, sems):
    rows = COLS * CPG
    sums = all_sums[...].reshape(N_GRP * rows, RANK)
    row = lax.broadcasted_iota(jnp.int32, (rows, N_GRP * rows), 0)
    lane = lax.broadcasted_iota(jnp.int32, (rows, N_GRP * rows), 1)
    column, cluster = row // CPG, row % CPG
    total = jnp.zeros((rows, CPG * RANK), F32)
    for k in range(FAR2):
        target = CPG * column
        for c in range(CPG):
            f = far_clusters[c, k]
            target += jnp.where(cluster == c, rows * (f // CPG) + f % CPG, 0)
        pick = jnp.where(lane == target, 1.0, 0.0).astype(BF16)
        picked = dot(pick, sums).astype(BF16)
        block = blocks[:, k].reshape(CPG * RANK, RANK)
        total += dot(picked, block, ((1,), (1,)))
    coupled = jnp.zeros((rows, RANK), F32)
    own = cluster[:, :RANK]
    for c in range(CPG):
        coupled += jnp.where(own == c, total[:, RANK * c : RANK * (c + 1)], 0.0)
    coupled = coupled.astype(BF16)
    lane = lax.broadcasted_iota(jnp.int32, (N_DEV, rows), 1).astype(F32)
    pick = jnp.concatenate(
        [jnp.where(lane == told[:, FAR1 : FAR1 + 1] + CPG * i, 1.0, 0.0) for i in range(COLS)], axis=0
    ).astype(BF16)
    out = dot(pick, coupled)
    staged[...] = jnp.zeros_like(staged)
    for i in range(COLS):
        staged[pl.ds(i, N_DEV, stride=8), :] = out[N_DEV * i : N_DEV * (i + 1)]
    sent[...] = staged[...].reshape(N_DEV, 8, RANK).astype(BF16)
    wait(started(((sent, sent_out.at[:, 2]),), sems))


def local_field(arrived, couplings, transfer, staged):
    staged[...] = arrived[...].astype(F32).reshape(N_DEV * 24, RANK)
    local = jnp.zeros((RANK, OUT), F32)
    for k in range(FAR1 + 1):
        skeleton = jnp.concatenate(
            [staged[pl.ds(COLS * k + i, N_DEV, stride=24), :] for i in range(COLS)], axis=0
        ).astype(BF16)
        local += dot(couplings[0, k] if k < FAR1 else transfer[0], skeleton, ((1,), (1,)))
    return local.astype(BF16)


def middle_kernel(
    ridge, arrived, couplings, transfer, basis, near, rs_in, w_out, sent_out, r1_out,
    rs, w, sent, r1, staged, staged_out, sems,
):
    copies = started(((rs_in, rs),), sems)
    ridge, centre, (mul, add), _ = chebyshev(ridge[0])
    local = local_field(arrived, couplings, transfer, staged)
    wait(copies)
    outs = []
    for n, r in enumerate(range(0, LEAF, ROWS)):
        part = slice(r, r + ROWS)
        here = rs[part]
        d1 = here / centre
        residual = here - (ridge * d1 + (near[part] + dot(basis[part], local)))
        r1[part] = residual
        w[part] = (mul * d1 + add * residual).astype(BF16)
        at = pl.ds(r, ROWS)
        outs += started(((r1.at[at], r1_out.at[at]), (w.at[at], w_out.at[at])), sems, 1 + 2 * n)
    to_owners(w[...], basis[...], transfer[0], staged_out, 8)
    sent[...] = staged_out[...].astype(BF16).reshape(N_DEV, 8, RANK)
    outs += started(((sent, sent_out),), sems, 9)
    wait(outs)


def end_kernel(
    ridge, arrived, couplings, transfer, basis, near, rs_in, r1_in, solution_out, residual_out,
    rs, r1, solution, residual, staged, sems,
):
    copies = started(((rs_in, rs), (r1_in, r1)), sems)
    ridge, centre, (mul1, add1), (mul, add) = chebyshev(ridge[0])
    local = local_field(arrived, couplings, transfer, staged)
    wait(copies)
    outs = []
    for n, r in enumerate(range(0, LEAF, ROWS)):
        part = slice(r, r + ROWS)
        d1 = rs[part] / centre
        d2 = mul1 * d1 + add1 * r1[part]
        r2 = r1[part] - (ridge * d2 + (near[part] + dot(basis[part], local)))
        residual[part] = r2
        solution[part] = d1 + d2 + (mul * d2 + add * r2)
        at = pl.ds(r, ROWS)
        outs += started(
            ((residual.at[at], residual_out.at[at]), (solution.at[at], solution_out.at[at])), sems, 2 + 2 * n
        )
    wait(outs)


def coordinates(held):
    parts = jnp.concatenate([held[: 2 * DIM], held[2 * DIM :]], axis=1)
    high, low = parts[:DIM], parts[DIM:]
    points = high.astype(F32) + low.astype(F32)
    return high, low, jnp.sum(points * points, axis=0, keepdims=True) * KERNEL_LOG2


def listed(near_list, offset):
    leaf = lax.axis_index("grp") * N_DEV + lax.axis_index("dev")
    hit = near_list[0, 0] == leaf + offset
    for k in range(1, len(NEAR)):
        hit = hit | (near_list[0, k] == leaf + offset)
    return hit


def block_times(here, there, values, total, fresh):
    high, low, norm = here
    left = jnp.concatenate([high, high, low, low], axis=0)
    column = jnp.broadcast_to(norm, (RANK, LEAF)).T[:, :1]
    high, low, across = there
    right = jnp.concatenate([high, low, high, low], axis=0)
    step = 128
    for r in range(0, LEAF, step):
        part = slice(r, r + step)
        inner = dot(left[:, part], right, ((0,), (0,)))
        entries = jnp.exp2((column[part] + across) - (2.0 * KERNEL_LOG2) * inner).astype(BF16)
        product = dot(entries, values)
        total[part] = product if fresh else total[part] + product


def near_own_kernel(places_in, values_in, total, places, values, sems):
    wait(started(((places_in.at[pl.ds(LEAF, 4 * DIM)], places), (values_in.at[pl.ds(0, LEAF)], values)), sems))
    mine = coordinates(places[...])
    block_times(mine, mine, values[...], total, True)


def near_pair_kernel(offsets, near_list, places_in, before, p1, v1, p2, v2, _, total, places, values, sems):
    copies = started([(p.at[pl.ds(LEAF, 4 * DIM)], places.at[i]) for i, p in enumerate((places_in, p1, p2))], sems)
    copies += started([(v.at[pl.ds(0, LEAF)], values.at[i]) for i, v in enumerate((v1, v2))], sems, 3)
    total[...] = before[...]
    wait(copies)
    mine = coordinates(places[0])
    for i, offset in enumerate(offsets):

        @pl.when(listed(near_list, offset))
        def _():
            block_times(mine, coordinates(places[1 + i]), values[i], total, False)


def from_behind(shard, by):
    pairs = [(i, i + by) for i in range(N_DEV) if 0 <= i + by < N_DEV]
    return lax.ppermute(shard, "dev", pairs)


def from_near(shard, after):
    shard, _ = lax.optimization_barrier((shard, after))
    return [from_behind(shard, -offset) for offset in NEAR]


def exchanged(blocks, axis):
    return lax.all_to_all(blocks, axis, split_axis=0, concat_axis=0, tiled=True)


def body(
    coords,
    right_side,
    leaf_perm,
    near_list,
    far_leaves,
    couplings,
    transfer,
    leaf_basis,
    cluster_of,
    far_clusters,
    cluster_couplings,
    ridge_weight,
):
    ridge = ridge_weight.reshape(1)
    field, dma = (LEAF, OUT), pltpu.SemaphoreType.DMA
    rows24 = pltpu.VMEM((N_DEV * 24, RANK), F32)
    rows16 = pltpu.VMEM((N_DEV * 16, RANK), F32)
    rows8 = pltpu.VMEM((N_DEV * 8, RANK), F32)
    narrow = pltpu.VMEM((COLS * CPG, RANK), F32)
    places = pltpu.VMEM((4 * DIM, OUT), BF16)

    wc, sent, basis = call(
        start_kernel,
        "start",
        [
            ((LEAF + 4 * DIM, OUT), BF16, HBM),
            ((N_DEV, 16, RANK), BF16, HBM),
            ((LEAF, RANK), BF16, HBM),
        ],
        [SMEM] * 2 + [HBM] * 6,
        (ridge, cluster_of, far_leaves, right_side, coords.T, leaf_perm, leaf_basis, transfer),
        [
            pltpu.SMEM((1, FAR1), jnp.int32),
            pltpu.VMEM(field, F32),
            pltpu.VMEM((DIM, LEAF), F32),
            pltpu.VMEM((1, LEAF), jnp.int32),
            pltpu.VMEM((LEAF, RANK), BF16),
            pltpu.VMEM((1, RANK, RANK), BF16),
            pltpu.VMEM((LEAF + 4 * DIM, OUT), BF16),
            pltpu.VMEM((N_DEV, 16, RANK), BF16),
            pltpu.VMEM((LEAF, RANK), BF16),
            rows16,
            dma((9,)),
        ],
        SHORT,
    )

    def near_own(values):
        (near,) = call(
            near_own_kernel,
            "near_own",
            [(field, F32, VMEM)],
            [HBM] * 2,
            (wc, values),
            [places, pltpu.VMEM(field, BF16), dma((2,))],
            SHORT,
        )
        return near

    def near_pair(at, near, first, fields, after, flops):
        (near,) = call(
            lambda *refs: near_pair_kernel(NEAR[at : at + 2], *refs),
            f"near_pair_{at}",
            [(field, F32, VMEM)],
            [SMEM, HBM, VMEM] + [ANY] * 5,
            (near_list, wc, near, first[at], fields[at], first[at + 1], fields[at + 1], after),
            [pltpu.VMEM((3, 4 * DIM, OUT), BF16), pltpu.VMEM((2, *field), BF16), dma((5,))],
            flops,
        )
        return near

    def through_owners(sums, skeletons):
        all_sums = exchanged(sums, "grp")
        (partners,) = call(
            partners_kernel,
            "partners",
            [((N_DEV, 3, 8, RANK), BF16, HBM)],
            [VMEM] * 2,
            (skeletons, told),
            [rows16, pltpu.VMEM((N_DEV, 2, 8, RANK), BF16), dma((1,))],
            SHORT,
        )
        (sent,) = call(
            couple_kernel,
            "couple",
            [((N_DEV, 3, 8, RANK), BF16, HBM)],
            [SMEM] + [VMEM] * 3 + [HBM],
            (far_clusters, all_sums, cluster_couplings, told, partners),
            [rows8, pltpu.VMEM((N_DEV, 8, RANK), BF16), dma((1,))],
            SHORT,
            {4: 0},
        )
        return sent, exchanged(sent, "dev")

    arrived = exchanged(sent, "dev")
    near = near_own(wc)
    first = from_near(wc, near)
    sums, told, skeletons = call(
        sums_first_kernel,
        "sums_first",
        [((N_GRP, 16, RANK), BF16, VMEM), ((N_DEV, RANK), F32, VMEM), ((N_DEV, COLS * RANK), BF16, VMEM)],
        [VMEM, ANY],
        (arrived, near),
        [rows16, narrow],
        SHORT,
    )
    sent, arrived = through_owners(sums, skeletons)
    near = near_pair(0, near, first, first, sent, SHORT)
    near = near_pair(2, near, first, first, sent, LONG)
    w, sent, r1 = call(
        middle_kernel,
        "middle",
        [(field, BF16, HBM), ((N_DEV, 8, RANK), BF16, HBM), (field, F32, HBM)],
        [SMEM] + [VMEM] * 5 + [HBM],
        (ridge, arrived, couplings, transfer, basis, near, right_side),
        [
            pltpu.VMEM(field, F32),
            pltpu.VMEM(field, BF16),
            pltpu.VMEM((N_DEV, 8, RANK), BF16),
            pltpu.VMEM(field, F32),
            rows24,
            rows8,
            dma((10,)),
        ],
        SHORT,
    )
    arrived = exchanged(sent, "dev")
    near = near_own(w)
    fields = from_near(w, near)
    sums, skeletons = call(
        sums_kernel,
        "sums",
        [((N_GRP, 16, RANK), BF16, VMEM), ((N_DEV, COLS * RANK), BF16, VMEM)],
        [VMEM, VMEM, ANY],
        (arrived, told, near),
        [rows8, narrow],
        SHORT,
    )
    sent, arrived = through_owners(sums, skeletons)
    near = near_pair(0, near, first, fields, sent, SHORT)
    near = near_pair(2, near, first, fields, sent, LONG)
    return tuple(
        call(
            end_kernel,
            "end",
            [(field, F32, HBM), (field, F32, HBM)],
            [SMEM] + [VMEM] * 5 + [HBM] * 2,
            (ridge, arrived, couplings, transfer, basis, near, right_side, r1),
            [pltpu.VMEM(field, F32)] * 4 + [rows24, dma((10,))],
            SHORT,
        )
    )


def solution(mesh):
    placed = (
        P(("grp", "dev"), None),
        P(("grp", "dev"), None),
        P(("grp", "dev"), None),
        P(("grp", "dev"), None),
        P(("grp", "dev"), None),
        P(("grp", "dev"), None, None, None),
        P(("grp", "dev"), None, None),
        P(("grp", "dev"), None),
        P(("grp", "dev")),
        P("grp", None),
        P("grp", None, None, None),
        P(),
    )
    return jax.shard_map(
        body,
        mesh=mesh,
        in_specs=placed,
        out_specs=(P(("grp", "dev"), None), P(("grp", "dev"), None)),
        check_vma=False,
    )
```

```python
import jax
import jax.numpy as jnp
from jax import lax
from jax.experimental import pallas as pl
from jax.experimental.pallas import tpu as pltpu
from jax.sharding import PartitionSpec as P

LEAF, DIM, OUT, RANK = 512, 64, 256, 128
N_GRP, N_DEV, CPG = 8, 64, 4
FAR1, FAR2 = 4, 4
COLS = OUT // N_DEV
NEAR = 4

KERNEL_LOG2 = -1.4426950408889634 / 32.0
GAP, TOP = 0.5, 8.0

F32, BF16 = jnp.float32, jnp.bfloat16
VMEM = pl.BlockSpec(memory_space=pltpu.VMEM)
SMEM = pl.BlockSpec(memory_space=pltpu.SMEM)
ANY = pl.BlockSpec(memory_space=pl.ANY)
HBM = pl.BlockSpec(memory_space=pltpu.HBM)
LIMIT = 32 * 2**20
SHORT, MID, LONG = 10**7, 10**10, 10**9
ROWS = 128


def dot(a, b, dims=((1,), (0,))):
    return lax.dot_general(a, b, (dims, ((), ())), preferred_element_type=F32)


def call(kernel, name, outs, ins, args, scratch=(), flops=0, aliases=None):
    shapes = [(pltpu.HBM if spec is HBM else jax.ShapeDtypeStruct)(shape, kind) for shape, kind, spec in outs]
    args = [
        pltpu.with_memory_space_constraint(arg, pltpu.HBM) if spec is HBM else arg for arg, spec in zip(args, ins)
    ]
    return pl.pallas_call(
        kernel,
        name=name,
        out_shape=shapes,
        in_specs=ins,
        out_specs=[spec for _, _, spec in outs],
        scratch_shapes=list(scratch),
        input_output_aliases=aliases or {},
        compiler_params=pltpu.CompilerParams(vmem_limit_bytes=LIMIT),
        cost_estimate=pl.CostEstimate(flops=flops, bytes_accessed=0, transcendentals=0),
    )(*args)


def started(pairs, sems, first=0):
    copies = [pltpu.make_async_copy(a, b, sems.at[first + i]) for i, (a, b) in enumerate(pairs)]
    for copy in copies:
        copy.start()
    return copies


def wait(copies):
    for copy in copies:
        copy.wait()


def chebyshev(ridge):
    ridge = jnp.full((1, 1), ridge, F32)
    bottom, top = ridge + GAP, ridge + TOP
    centre, spread = (top + bottom) / 2.0, (top - bottom) / 2.0
    sigma = centre / spread
    rho0 = 1.0 / sigma
    rho1 = 1.0 / (2.0 * sigma - rho0)
    rho2 = 1.0 / (2.0 * sigma - rho1)
    first = (rho1 * rho0, 2.0 * rho1 / spread)
    second = (rho2 * rho1, 2.0 * rho2 / spread)
    return ridge, centre, first, second


def to_owners(values, basis, transfer, staged, rows):
    skeleton = dot(values, basis, ((0,), (0,))).astype(BF16)
    uplift = dot(skeleton, transfer)
    skeleton = skeleton.astype(F32)
    for i in range(COLS):
        part = slice(N_DEV * i, N_DEV * (i + 1))
        staged[pl.ds(i, N_DEV, stride=rows), :] = skeleton[part]
        staged[pl.ds(COLS + i, N_DEV, stride=rows), :] = uplift[part]


def start_kernel(
    ridge, cluster, far_in, rs_in, coords_in, perm_in, basis_in, transfer_in, wc_out, sent_out, placed_out,
    far, rs, coords, perm, basis, transfer, wc, sent, placed, staged, sems,
):
    copies = started(
        (
            (perm_in, perm), (basis_in, basis), (rs_in, rs), (coords_in, coords),
            (transfer_in, transfer), (far_in, far),
        ),
        sems,
    )
    staged[...] = jnp.zeros_like(staged)
    _, centre, _, _ = chebyshev(ridge[0])
    wait(copies[:2])
    point = lax.broadcasted_iota(jnp.int32, (LEAF, LEAF), 0)
    pick = jnp.where(point == perm[...], 1.0, 0.0).astype(BF16)
    basis_here = dot(pick, basis[...]).astype(BF16)
    placed[...] = basis_here
    wait(copies[2:4])
    values = (rs[...] / centre).astype(BF16)
    wc[:LEAF] = values
    high = coords[...].astype(BF16)
    low = (coords[...] - high.astype(F32)).astype(BF16)
    parts = jnp.concatenate([high, low], axis=0)
    wc[LEAF : LEAF + 2 * DIM] = parts[:, :OUT]
    wc[LEAF + 2 * DIM :] = parts[:, OUT:]
    outs = started(((wc, wc_out), (placed, placed_out)), sems, 6)
    wait(copies[4:])
    to_owners(values, basis_here, transfer[0], staged, 16)
    lane = lax.broadcasted_iota(jnp.int32, (N_DEV, RANK), 1)
    told = jnp.where(lane == FAR1, (cluster[0] % CPG).astype(F32), 0.0)
    for k in range(FAR1):
        told = jnp.where(lane == k, (far[0, k] % N_DEV).astype(F32), told)
    staged[pl.ds(8, N_DEV, stride=16), :] = told
    sent[...] = staged[...].astype(BF16).reshape(N_DEV, 16, RANK)
    outs += started(((sent, sent_out),), sems, 8)
    wait(outs)


def owner_sums(staged, rows, told, sums, narrow):
    lane = lax.broadcasted_iota(jnp.int32, (N_DEV, RANK), 1).astype(F32)
    member = jnp.where(lane == told[:, FAR1 : FAR1 + 1], 1.0, 0.0).astype(BF16)
    uplifts = jnp.concatenate(
        [staged[pl.ds(COLS + i, N_DEV, stride=rows), :] for i in range(COLS)], axis=1
    ).astype(BF16)
    total = dot(member, uplifts, ((0,), (0,)))
    for i in range(COLS):
        narrow[pl.ds(CPG * i, CPG), :] = total[:CPG, RANK * i : RANK * (i + 1)]
    out = narrow[...].astype(BF16)
    for g in range(N_GRP):
        sums[g] = out


def sums_first_kernel(arrived, _, sums, told, skeletons, staged, narrow):
    staged[...] = arrived[...].astype(F32).reshape(N_DEV * 16, RANK)
    told[...] = staged[pl.ds(8, N_DEV, stride=16), :]
    owner_sums(staged, 16, told[...], sums, narrow)
    skeletons[...] = jnp.concatenate(
        [staged[pl.ds(i, N_DEV, stride=16), :] for i in range(COLS)], axis=1
    ).astype(BF16)


def sums_kernel(arrived, told, _, sums, skeletons, staged, narrow):
    staged[...] = arrived[...].astype(F32).reshape(N_DEV * 8, RANK)
    owner_sums(staged, 8, told[...], sums, narrow)
    skeletons[...] = jnp.concatenate(
        [staged[pl.ds(i, N_DEV, stride=8), :] for i in range(COLS)], axis=1
    ).astype(BF16)


def partners_kernel(skeletons, told, sent_out, done, staged, sent, sems):
    lane = lax.broadcasted_iota(jnp.int32, (N_DEV, N_DEV), 1).astype(F32)
    pick = jnp.concatenate(
        [jnp.where(lane == told[:, k : k + 1], 1.0, 0.0) for k in range(FAR1)], axis=0
    ).astype(BF16)
    picked = dot(pick, skeletons[...])
    for k in range(FAR1):
        for i in range(COLS):
            staged[pl.ds(COLS * k + i, N_DEV, stride=16), :] = picked[
                N_DEV * k : N_DEV * (k + 1), RANK * i : RANK * (i + 1)
            ]
    sent[...] = staged[...].reshape(N_DEV, 2, 8, RANK).astype(BF16)
    done[...] = jnp.zeros_like(done)
    wait(started(((sent, sent_out.at[:, :2]),), sems))


def couple_kernel(far_clusters, all_sums, blocks, told, _, sent_out, staged, sent, sems):
    rows = COLS * CPG
    sums = all_sums[...].reshape(N_GRP * rows, RANK)
    row = lax.broadcasted_iota(jnp.int32, (rows, N_GRP * rows), 0)
    lane = lax.broadcasted_iota(jnp.int32, (rows, N_GRP * rows), 1)
    column, cluster = row // CPG, row % CPG
    total = jnp.zeros((CPG * RANK, rows), F32)
    for k in range(FAR2):
        target = CPG * column
        for c in range(CPG):
            f = far_clusters[c, k]
            target += jnp.where(cluster == c, rows * (f // CPG) + f % CPG, 0)
        pick = jnp.where(lane == target, 1.0, 0.0).astype(BF16)
        picked = dot(pick, sums).astype(BF16)
        total += dot(blocks[:, k].reshape(CPG * RANK, RANK), picked, ((1,), (1,)))
    own = lax.broadcasted_iota(jnp.int32, (RANK, rows), 1) % CPG
    coupled = jnp.zeros((RANK, rows), F32)
    for c in range(CPG):
        coupled += jnp.where(own == c, total[RANK * c : RANK * (c + 1)], 0.0)
    coupled = coupled.T
    coupled = coupled.astype(BF16)
    lane = lax.broadcasted_iota(jnp.int32, (N_DEV, rows), 1).astype(F32)
    pick = jnp.concatenate(
        [jnp.where(lane == told[:, FAR1 : FAR1 + 1] + CPG * i, 1.0, 0.0) for i in range(COLS)], axis=0
    ).astype(BF16)
    out = dot(pick, coupled)
    staged[...] = jnp.zeros_like(staged)
    for i in range(COLS):
        staged[pl.ds(i, N_DEV, stride=8), :] = out[N_DEV * i : N_DEV * (i + 1)]
    sent[...] = staged[...].reshape(N_DEV, 8, RANK).astype(BF16)
    wait(started(((sent, sent_out.at[:, 2]),), sems))


def local_field(arrived, couplings, transfer, staged):
    staged[...] = arrived[...].astype(F32).reshape(N_DEV * 24, RANK)
    local = jnp.zeros((OUT, RANK), F32)
    for k in range(FAR1 + 1):
        skeleton = jnp.concatenate(
            [staged[pl.ds(COLS * k + i, N_DEV, stride=24), :] for i in range(COLS)], axis=0
        ).astype(BF16)
        local += dot(skeleton, couplings[0, k] if k < FAR1 else transfer[0], ((1,), (1,)))
    return local.T.astype(BF16)


def middle_kernel(
    ridge, arrived, couplings, transfer, basis, near, rs_in, w_out, sent_out, r1_out,
    rs, w, sent, r1, staged, staged_out, sems,
):
    copies = started(((rs_in, rs),), sems)
    ridge, centre, (mul, add), _ = chebyshev(ridge[0])
    local = local_field(arrived, couplings, transfer, staged)
    wait(copies)
    outs = []
    for n, r in enumerate(range(0, LEAF, ROWS)):
        part = slice(r, r + ROWS)
        here = rs[part]
        d1 = here / centre
        residual = here - (ridge * d1 + (near[part] + dot(basis[part], local)))
        r1[part] = residual
        w[part] = (mul * d1 + add * residual).astype(BF16)
        at = pl.ds(r, ROWS)
        outs += started(((r1.at[at], r1_out.at[at]), (w.at[at], w_out.at[at])), sems, 1 + 2 * n)
    to_owners(w[...], basis[...], transfer[0], staged_out, 8)
    sent[...] = staged_out[...].astype(BF16).reshape(N_DEV, 8, RANK)
    outs += started(((sent, sent_out),), sems, 9)
    wait(outs)


def end_kernel(
    ridge, arrived, couplings, transfer, basis, near, rs_in, r1_in, solution_out, residual_out,
    rs, r1, solution, residual, staged, sems,
):
    copies = started(((rs_in, rs), (r1_in, r1)), sems)
    ridge, centre, (mul1, add1), (mul, add) = chebyshev(ridge[0])
    local = local_field(arrived, couplings, transfer, staged)
    wait(copies)
    outs = []
    for n, r in enumerate(range(0, LEAF, ROWS)):
        part = slice(r, r + ROWS)
        d1 = rs[part] / centre
        d2 = mul1 * d1 + add1 * r1[part]
        r2 = r1[part] - (ridge * d2 + (near[part] + dot(basis[part], local)))
        residual[part] = r2
        solution[part] = d1 + d2 + (mul * d2 + add * r2)
        at = pl.ds(r, ROWS)
        outs += started(
            ((residual.at[at], residual_out.at[at]), (solution.at[at], solution_out.at[at])), sems, 2 + 2 * n
        )
    wait(outs)


def coordinates(held):
    parts = jnp.concatenate([held[: 2 * DIM], held[2 * DIM :]], axis=1)
    high, low = parts[:DIM], parts[DIM:]
    points = high.astype(F32) + low.astype(F32)
    return high, low, jnp.sum(points * points, axis=0, keepdims=True) * KERNEL_LOG2


def listed(near_list, offset):
    leaf = lax.axis_index("grp") * N_DEV + lax.axis_index("dev")
    hit = near_list[0, 0] == leaf + offset
    for k in range(1, NEAR):
        hit = hit | (near_list[0, k] == leaf + offset)
    return hit


def block_times(here, there, values, total, fresh):
    high, low, norm = here
    left = jnp.concatenate([high, high, low, low], axis=0)
    column = jnp.broadcast_to(norm, (RANK, LEAF)).T[:, :1]
    high, low, across = there
    right = jnp.concatenate([high, low, high, low], axis=0)
    step = 128
    for r in range(0, LEAF, step):
        part = slice(r, r + step)
        inner = dot(left[:, part], right, ((0,), (0,)))
        entries = jnp.exp2((column[part] + across) - (2.0 * KERNEL_LOG2) * inner).astype(BF16)
        product = dot(entries, values)
        total[part] = product if fresh else total[part] + product


def near_own_kernel(places_in, values_in, total, places, values, sems):
    wait(started(((places_in.at[pl.ds(LEAF, 4 * DIM)], places), (values_in.at[pl.ds(0, LEAF)], values)), sems))
    mine = coordinates(places[...])
    block_times(mine, mine, values[...], total, True)


def near_pair_kernel(offsets, near_list, places_in, before, p1, v1, p2, v2, _, total, places, values, sems):
    copies = started([(p.at[pl.ds(LEAF, 4 * DIM)], places.at[i]) for i, p in enumerate((places_in, p1, p2))], sems)
    copies += started([(v.at[pl.ds(0, LEAF)], values.at[i]) for i, v in enumerate((v1, v2))], sems, 3)
    total[...] = before[...]
    wait(copies)
    mine = coordinates(places[0])
    for i, offset in enumerate(offsets):

        @pl.when(listed(near_list, offset))
        def _():
            block_times(mine, coordinates(places[1 + i]), values[i], total, False)


def from_behind(shard, by):
    pairs = [(i, i + by) for i in range(N_DEV) if 0 <= i + by < N_DEV]
    return lax.ppermute(shard, "dev", pairs)


def from_pair(shard, distance, after):
    shard, _ = lax.optimization_barrier((shard, after))
    return from_behind(shard, distance), from_behind(shard, -distance)


def exchanged(blocks, axis):
    return lax.all_to_all(blocks, axis, split_axis=0, concat_axis=0, tiled=True)


def body(
    coords,
    right_side,
    leaf_perm,
    near_list,
    far_leaves,
    couplings,
    transfer,
    leaf_basis,
    cluster_of,
    far_clusters,
    cluster_couplings,
    ridge_weight,
):
    ridge = ridge_weight.reshape(1)
    field, dma = (LEAF, OUT), pltpu.SemaphoreType.DMA
    rows24 = pltpu.VMEM((N_DEV * 24, RANK), F32)
    rows16 = pltpu.VMEM((N_DEV * 16, RANK), F32)
    rows8 = pltpu.VMEM((N_DEV * 8, RANK), F32)
    narrow = pltpu.VMEM((COLS * CPG, RANK), F32)
    places = pltpu.VMEM((4 * DIM, OUT), BF16)

    wc, sent, basis = call(
        start_kernel,
        "start",
        [
            ((LEAF + 4 * DIM, OUT), BF16, HBM),
            ((N_DEV, 16, RANK), BF16, HBM),
            ((LEAF, RANK), BF16, HBM),
        ],
        [SMEM] * 2 + [HBM] * 6,
        (ridge, cluster_of, far_leaves, right_side, coords.T, leaf_perm, leaf_basis, transfer),
        [
            pltpu.SMEM((1, FAR1), jnp.int32),
            pltpu.VMEM(field, F32),
            pltpu.VMEM((DIM, LEAF), F32),
            pltpu.VMEM((1, LEAF), jnp.int32),
            pltpu.VMEM((LEAF, RANK), BF16),
            pltpu.VMEM((1, RANK, RANK), BF16),
            pltpu.VMEM((LEAF + 4 * DIM, OUT), BF16),
            pltpu.VMEM((N_DEV, 16, RANK), BF16),
            pltpu.VMEM((LEAF, RANK), BF16),
            rows16,
            dma((9,)),
        ],
        SHORT,
    )

    def near_own(values):
        (near,) = call(
            near_own_kernel,
            "near_own",
            [(field, F32, VMEM)],
            [HBM] * 2,
            (wc, values),
            [places, pltpu.VMEM(field, BF16), dma((2,))],
            SHORT,
        )
        return near

    def near_pair(distance, near, first, fields, after, flops):
        (near,) = call(
            lambda *refs: near_pair_kernel((-distance, distance), *refs),
            f"near_pair_{distance}",
            [(field, F32, VMEM)],
            [SMEM, HBM, VMEM] + [ANY] * 5,
            (near_list, wc, near, first[0], fields[0], first[1], fields[1], after),
            [pltpu.VMEM((3, 4 * DIM, OUT), BF16), pltpu.VMEM((2, *field), BF16), dma((5,))],
            flops,
        )
        return near

    def through_owners(sums, skeletons):
        all_sums = exchanged(sums, "grp")
        partners, done = call(
            partners_kernel,
            "partners",
            [((N_DEV, 3, 8, RANK), BF16, HBM), ((8, RANK), F32, VMEM)],
            [VMEM] * 2,
            (skeletons, told),
            [rows16, pltpu.VMEM((N_DEV, 2, 8, RANK), BF16), dma((1,))],
            SHORT,
        )
        (sent,) = call(
            couple_kernel,
            "couple",
            [((N_DEV, 3, 8, RANK), BF16, HBM)],
            [SMEM] + [VMEM] * 3 + [HBM],
            (far_clusters, all_sums, cluster_couplings, told, partners),
            [rows8, pltpu.VMEM((N_DEV, 8, RANK), BF16), dma((1,))],
            SHORT,
            {4: 0},
        )
        return sent, exchanged(sent, "dev"), done

    arrived = exchanged(sent, "dev")
    near = near_own(wc)
    first2 = from_pair(wc, 2, near)
    sums, told, skeletons = call(
        sums_first_kernel,
        "sums_first",
        [((N_GRP, 16, RANK), BF16, VMEM), ((N_DEV, RANK), F32, VMEM), ((N_DEV, COLS * RANK), BF16, VMEM)],
        [VMEM, ANY],
        (arrived, near),
        [rows16, narrow],
        SHORT,
    )
    sent, arrived, done = through_owners(sums, skeletons)
    first1 = from_pair(wc, 1, done)
    near = near_pair(2, near, first2, first2, sent, MID)
    near = near_pair(1, near, first1, first1, sent, LONG)
    w, sent, r1 = call(
        middle_kernel,
        "middle",
        [(field, BF16, HBM), ((N_DEV, 8, RANK), BF16, HBM), (field, F32, HBM)],
        [SMEM] + [VMEM] * 5 + [HBM],
        (ridge, arrived, couplings, transfer, basis, near, right_side),
        [
            pltpu.VMEM(field, F32),
            pltpu.VMEM(field, BF16),
            pltpu.VMEM((N_DEV, 8, RANK), BF16),
            pltpu.VMEM(field, F32),
            rows24,
            rows8,
            dma((10,)),
        ],
        SHORT,
    )
    arrived = exchanged(sent, "dev")
    near = near_own(w)
    fields2 = from_pair(w, 2, near)
    sums, skeletons = call(
        sums_kernel,
        "sums",
        [((N_GRP, 16, RANK), BF16, VMEM), ((N_DEV, COLS * RANK), BF16, VMEM)],
        [VMEM, VMEM, ANY],
        (arrived, told, near),
        [rows8, narrow],
        SHORT,
    )
    sent, arrived, done = through_owners(sums, skeletons)
    fields1 = from_pair(w, 1, done)
    near = near_pair(2, near, first2, fields2, sent, MID)
    near = near_pair(1, near, first1, fields1, sent, LONG)
    return tuple(
        call(
            end_kernel,
            "end",
            [(field, F32, HBM), (field, F32, HBM)],
            [SMEM] + [VMEM] * 5 + [HBM] * 2,
            (ridge, arrived, couplings, transfer, basis, near, right_side, r1),
            [pltpu.VMEM(field, F32)] * 4 + [rows24, dma((10,))],
            SHORT,
        )
    )


def solution(mesh):
    placed = (
        P(("grp", "dev"), None),
        P(("grp", "dev"), None),
        P(("grp", "dev"), None),
        P(("grp", "dev"), None),
        P(("grp", "dev"), None),
        P(("grp", "dev"), None, None, None),
        P(("grp", "dev"), None, None),
        P(("grp", "dev"), None),
        P(("grp", "dev")),
        P("grp", None),
        P("grp", None, None, None),
        P(),
    )
    return jax.shard_map(
        body,
        mesh=mesh,
        in_specs=placed,
        out_specs=(P(("grp", "dev"), None), P(("grp", "dev"), None)),
        check_vma=False,
    )
```

```python
import jax
import jax.numpy as jnp
from jax import lax
from jax.experimental import pallas as pl
from jax.experimental.pallas import tpu as pltpu
from jax.sharding import PartitionSpec as P

LEAF, DIM, OUT, RANK = 512, 64, 256, 128
N_GRP, N_DEV, CPG = 8, 64, 4
FAR1, FAR2 = 4, 4
COLS = OUT // N_DEV
NEAR = 4

KERNEL_LOG2 = -1.4426950408889634 / 32.0
GAP, TOP = 0.5, 8.0

F32, BF16 = jnp.float32, jnp.bfloat16
VMEM = pl.BlockSpec(memory_space=pltpu.VMEM)
SMEM = pl.BlockSpec(memory_space=pltpu.SMEM)
ANY = pl.BlockSpec(memory_space=pl.ANY)
HBM = pl.BlockSpec(memory_space=pltpu.HBM)
LIMIT = 32 * 2**20
SHORT, MID, LONG = 10**7, 10**10, 10**9
ROWS = 128


def dot(a, b, dims=((1,), (0,))):
    return lax.dot_general(a, b, (dims, ((), ())), preferred_element_type=F32)


def call(kernel, name, outs, ins, args, scratch=(), flops=0, aliases=None):
    shapes = [(pltpu.HBM if spec is HBM else jax.ShapeDtypeStruct)(shape, kind) for shape, kind, spec in outs]
    args = [
        pltpu.with_memory_space_constraint(arg, pltpu.HBM) if spec is HBM else arg for arg, spec in zip(args, ins)
    ]
    return pl.pallas_call(
        kernel,
        name=name,
        out_shape=shapes,
        in_specs=ins,
        out_specs=[spec for _, _, spec in outs],
        scratch_shapes=list(scratch),
        input_output_aliases=aliases or {},
        compiler_params=pltpu.CompilerParams(vmem_limit_bytes=LIMIT),
        cost_estimate=pl.CostEstimate(flops=flops, bytes_accessed=0, transcendentals=0),
    )(*args)


def started(pairs, sems, first=0):
    copies = [pltpu.make_async_copy(a, b, sems.at[first + i]) for i, (a, b) in enumerate(pairs)]
    for copy in copies:
        copy.start()
    return copies


def wait(copies):
    for copy in copies:
        copy.wait()


def chebyshev(ridge):
    ridge = jnp.full((1, 1), ridge, F32)
    bottom, top = ridge + GAP, ridge + TOP
    centre, spread = (top + bottom) / 2.0, (top - bottom) / 2.0
    sigma = centre / spread
    rho0 = 1.0 / sigma
    rho1 = 1.0 / (2.0 * sigma - rho0)
    rho2 = 1.0 / (2.0 * sigma - rho1)
    first = (rho1 * rho0, 2.0 * rho1 / spread)
    second = (rho2 * rho1, 2.0 * rho2 / spread)
    return ridge, centre, first, second


def to_owners(values, basis, transfer, staged, rows):
    skeleton = dot(values, basis, ((0,), (0,))).astype(BF16)
    uplift = dot(skeleton, transfer)
    skeleton = skeleton.astype(F32)
    for i in range(COLS):
        part = slice(N_DEV * i, N_DEV * (i + 1))
        staged[pl.ds(i, N_DEV, stride=rows), :] = skeleton[part]
        staged[pl.ds(COLS + i, N_DEV, stride=rows), :] = uplift[part]


def start_kernel(
    ridge, cluster, far_in, rs_in, coords_in, perm_in, basis_in, transfer_in, wc_out, sent_out, placed_out,
    far, rs, coords, perm, basis, transfer, wc, sent, placed, staged, sems,
):
    copies = started(
        (
            (perm_in, perm), (basis_in, basis), (rs_in, rs), (coords_in, coords),
            (transfer_in, transfer), (far_in, far),
        ),
        sems,
    )
    staged[...] = jnp.zeros_like(staged)
    _, centre, _, _ = chebyshev(ridge[0])
    wait(copies[:2])
    point = lax.broadcasted_iota(jnp.int32, (LEAF, LEAF), 0)
    pick = jnp.where(point == perm[...], 1.0, 0.0).astype(BF16)
    basis_here = dot(pick, basis[...]).astype(BF16)
    placed[...] = basis_here
    wait(copies[2:4])
    values = (rs[...] / centre).astype(BF16)
    wc[:LEAF] = values
    high = coords[...].astype(BF16)
    low = (coords[...] - high.astype(F32)).astype(BF16)
    parts = jnp.concatenate([high, low], axis=0)
    wc[LEAF : LEAF + 2 * DIM] = parts[:, :OUT]
    wc[LEAF + 2 * DIM :] = parts[:, OUT:]
    outs = started(((wc, wc_out), (placed, placed_out)), sems, 6)
    wait(copies[4:])
    to_owners(values, basis_here, transfer[0], staged, 16)
    lane = lax.broadcasted_iota(jnp.int32, (N_DEV, RANK), 1)
    told = jnp.where(lane == FAR1, (cluster[0] % CPG).astype(F32), 0.0)
    for k in range(FAR1):
        told = jnp.where(lane == k, (far[0, k] % N_DEV).astype(F32), told)
    staged[pl.ds(8, N_DEV, stride=16), :] = told
    sent[...] = staged[...].astype(BF16).reshape(N_DEV, 16, RANK)
    outs += started(((sent, sent_out),), sems, 8)
    wait(outs)


def owner_sums(staged, rows, told, sums, narrow):
    lane = lax.broadcasted_iota(jnp.int32, (N_DEV, RANK), 1).astype(F32)
    member = jnp.where(lane == told[:, FAR1 : FAR1 + 1], 1.0, 0.0).astype(BF16)
    uplifts = jnp.concatenate(
        [staged[pl.ds(COLS + i, N_DEV, stride=rows), :] for i in range(COLS)], axis=1
    ).astype(BF16)
    total = dot(member, uplifts, ((0,), (0,)))
    for i in range(COLS):
        narrow[pl.ds(CPG * i, CPG), :] = total[:CPG, RANK * i : RANK * (i + 1)]
    out = narrow[...].astype(BF16)
    for g in range(N_GRP):
        sums[g] = out


def sums_first_kernel(arrived, _, sums, told, skeletons, staged, narrow):
    staged[...] = arrived[...].astype(F32).reshape(N_DEV * 16, RANK)
    told[...] = staged[pl.ds(8, N_DEV, stride=16), :]
    owner_sums(staged, 16, told[...], sums, narrow)
    skeletons[...] = jnp.concatenate(
        [staged[pl.ds(i, N_DEV, stride=16), :] for i in range(COLS)], axis=1
    ).astype(BF16)


def sums_kernel(arrived, told, _, sums, skeletons, staged, narrow):
    staged[...] = arrived[...].astype(F32).reshape(N_DEV * 8, RANK)
    owner_sums(staged, 8, told[...], sums, narrow)
    skeletons[...] = jnp.concatenate(
        [staged[pl.ds(i, N_DEV, stride=8), :] for i in range(COLS)], axis=1
    ).astype(BF16)


def partners_kernel(skeletons, told, sent_out, staged, sent, sems):
    lane = lax.broadcasted_iota(jnp.int32, (N_DEV, N_DEV), 1).astype(F32)
    pick = jnp.concatenate(
        [jnp.where(lane == told[:, k : k + 1], 1.0, 0.0) for k in range(FAR1)], axis=0
    ).astype(BF16)
    picked = dot(pick, skeletons[...])
    for k in range(FAR1):
        for i in range(COLS):
            staged[pl.ds(COLS * k + i, N_DEV, stride=16), :] = picked[
                N_DEV * k : N_DEV * (k + 1), RANK * i : RANK * (i + 1)
            ]
    sent[...] = staged[...].reshape(N_DEV, 2, 8, RANK).astype(BF16)
    wait(started(((sent, sent_out.at[:, :2]),), sems))


def couple_kernel(far_clusters, all_sums, blocks, told, _, sent_out, staged, sent, sems):
    rows = COLS * CPG
    sums = all_sums[...].reshape(N_GRP * rows, RANK)
    row = lax.broadcasted_iota(jnp.int32, (rows, N_GRP * rows), 0)
    lane = lax.broadcasted_iota(jnp.int32, (rows, N_GRP * rows), 1)
    column, cluster = row // CPG, row % CPG
    total = jnp.zeros((CPG * RANK, rows), F32)
    for k in range(FAR2):
        target = CPG * column
        for c in range(CPG):
            f = far_clusters[c, k]
            target += jnp.where(cluster == c, rows * (f // CPG) + f % CPG, 0)
        pick = jnp.where(lane == target, 1.0, 0.0).astype(BF16)
        picked = dot(pick, sums).astype(BF16)
        total += dot(blocks[:, k].reshape(CPG * RANK, RANK), picked, ((1,), (1,)))
    own = lax.broadcasted_iota(jnp.int32, (RANK, rows), 1) % CPG
    coupled = jnp.zeros((RANK, rows), F32)
    for c in range(CPG):
        coupled += jnp.where(own == c, total[RANK * c : RANK * (c + 1)], 0.0)
    coupled = coupled.T
    coupled = coupled.astype(BF16)
    lane = lax.broadcasted_iota(jnp.int32, (N_DEV, rows), 1).astype(F32)
    pick = jnp.concatenate(
        [jnp.where(lane == told[:, FAR1 : FAR1 + 1] + CPG * i, 1.0, 0.0) for i in range(COLS)], axis=0
    ).astype(BF16)
    out = dot(pick, coupled)
    staged[...] = jnp.zeros_like(staged)
    for i in range(COLS):
        staged[pl.ds(i, N_DEV, stride=8), :] = out[N_DEV * i : N_DEV * (i + 1)]
    sent[...] = staged[...].reshape(N_DEV, 8, RANK).astype(BF16)
    wait(started(((sent, sent_out.at[:, 2]),), sems))


def local_field(arrived, couplings, transfer, staged):
    staged[...] = arrived[...].astype(F32).reshape(N_DEV * 24, RANK)
    local = jnp.zeros((OUT, RANK), F32)
    for k in range(FAR1 + 1):
        skeleton = jnp.concatenate(
            [staged[pl.ds(COLS * k + i, N_DEV, stride=24), :] for i in range(COLS)], axis=0
        ).astype(BF16)
        local += dot(skeleton, couplings[0, k] if k < FAR1 else transfer[0], ((1,), (1,)))
    return local.T.astype(BF16)


def middle_kernel(
    ridge, arrived, couplings, transfer, basis, near, rs_in, w_out, sent_out, r1_out,
    rs, w, sent, r1, staged, staged_out, sems,
):
    copies = started(((rs_in, rs),), sems)
    ridge, centre, (mul, add), _ = chebyshev(ridge[0])
    local = local_field(arrived, couplings, transfer, staged)
    wait(copies)
    outs = []
    for n, r in enumerate(range(0, LEAF, ROWS)):
        part = slice(r, r + ROWS)
        here = rs[part]
        d1 = here / centre
        residual = here - (ridge * d1 + (near[part] + dot(basis[part], local)))
        r1[part] = residual
        w[part] = (mul * d1 + add * residual).astype(BF16)
        at = pl.ds(r, ROWS)
        outs += started(((r1.at[at], r1_out.at[at]), (w.at[at], w_out.at[at])), sems, 1 + 2 * n)
    to_owners(w[...], basis[...], transfer[0], staged_out, 8)
    sent[...] = staged_out[...].astype(BF16).reshape(N_DEV, 8, RANK)
    outs += started(((sent, sent_out),), sems, 9)
    wait(outs)


def end_kernel(
    ridge, arrived, couplings, transfer, basis, near, rs_in, r1_in, solution_out, residual_out,
    rs, r1, solution, residual, staged, sems,
):
    copies = started(((rs_in, rs), (r1_in, r1)), sems)
    ridge, centre, (mul1, add1), (mul, add) = chebyshev(ridge[0])
    local = local_field(arrived, couplings, transfer, staged)
    wait(copies)
    outs = []
    for n, r in enumerate(range(0, LEAF, ROWS)):
        part = slice(r, r + ROWS)
        d1 = rs[part] / centre
        d2 = mul1 * d1 + add1 * r1[part]
        r2 = r1[part] - (ridge * d2 + (near[part] + dot(basis[part], local)))
        residual[part] = r2
        solution[part] = d1 + d2 + (mul * d2 + add * r2)
        at = pl.ds(r, ROWS)
        outs += started(
            ((residual.at[at], residual_out.at[at]), (solution.at[at], solution_out.at[at])), sems, 2 + 2 * n
        )
    wait(outs)


def coordinates(held):
    parts = jnp.concatenate([held[: 2 * DIM], held[2 * DIM :]], axis=1)
    high, low = parts[:DIM], parts[DIM:]
    points = high.astype(F32) + low.astype(F32)
    return high, low, jnp.sum(points * points, axis=0, keepdims=True) * KERNEL_LOG2


def listed(near_list, offset):
    leaf = lax.axis_index("grp") * N_DEV + lax.axis_index("dev")
    hit = near_list[0, 0] == leaf + offset
    for k in range(1, NEAR):
        hit = hit | (near_list[0, k] == leaf + offset)
    return hit


def block_times(here, there, values, total, fresh):
    high, low, norm = here
    left = jnp.concatenate([high, high, low, low], axis=0)
    column = jnp.broadcast_to(norm, (RANK, LEAF)).T[:, :1]
    high, low, across = there
    right = jnp.concatenate([high, low, high, low], axis=0)
    step = 128
    for r in range(0, LEAF, step):
        part = slice(r, r + step)
        inner = dot(left[:, part], right, ((0,), (0,)))
        entries = jnp.exp2((column[part] + across) - (2.0 * KERNEL_LOG2) * inner).astype(BF16)
        product = dot(entries, values)
        total[part] = product if fresh else total[part] + product


def near_own_kernel(places_in, values_in, total, places, values, sems):
    wait(started(((places_in.at[pl.ds(LEAF, 4 * DIM)], places), (values_in.at[pl.ds(0, LEAF)], values)), sems))
    mine = coordinates(places[...])
    block_times(mine, mine, values[...], total, True)


def near_pair_kernel(offsets, near_list, places_in, before, p1, v1, p2, v2, _, total, places, values, sems):
    copies = started([(p.at[pl.ds(LEAF, 4 * DIM)], places.at[i]) for i, p in enumerate((places_in, p1, p2))], sems)
    copies += started([(v.at[pl.ds(0, LEAF)], values.at[i]) for i, v in enumerate((v1, v2))], sems, 3)
    total[...] = before[...]
    wait(copies)
    mine = coordinates(places[0])
    for i, offset in enumerate(offsets):

        @pl.when(listed(near_list, offset))
        def _():
            block_times(mine, coordinates(places[1 + i]), values[i], total, False)


def from_behind(shard, by):
    pairs = [(i, i + by) for i in range(N_DEV) if 0 <= i + by < N_DEV]
    return lax.ppermute(shard, "dev", pairs)


def from_pair(shard, distance, after):
    shard, _ = lax.optimization_barrier((shard, after))
    return from_behind(shard, distance), from_behind(shard, -distance)


def exchanged(blocks, axis):
    return lax.all_to_all(blocks, axis, split_axis=0, concat_axis=0, tiled=True)


def body(
    coords,
    right_side,
    leaf_perm,
    near_list,
    far_leaves,
    couplings,
    transfer,
    leaf_basis,
    cluster_of,
    far_clusters,
    cluster_couplings,
    ridge_weight,
):
    ridge = ridge_weight.reshape(1)
    field, dma = (LEAF, OUT), pltpu.SemaphoreType.DMA
    rows24 = pltpu.VMEM((N_DEV * 24, RANK), F32)
    rows16 = pltpu.VMEM((N_DEV * 16, RANK), F32)
    rows8 = pltpu.VMEM((N_DEV * 8, RANK), F32)
    narrow = pltpu.VMEM((COLS * CPG, RANK), F32)
    places = pltpu.VMEM((4 * DIM, OUT), BF16)

    wc, sent, basis = call(
        start_kernel,
        "start",
        [
            ((LEAF + 4 * DIM, OUT), BF16, HBM),
            ((N_DEV, 16, RANK), BF16, HBM),
            ((LEAF, RANK), BF16, HBM),
        ],
        [SMEM] * 2 + [HBM] * 6,
        (ridge, cluster_of, far_leaves, right_side, coords.T, leaf_perm, leaf_basis, transfer),
        [
            pltpu.SMEM((1, FAR1), jnp.int32),
            pltpu.VMEM(field, F32),
            pltpu.VMEM((DIM, LEAF), F32),
            pltpu.VMEM((1, LEAF), jnp.int32),
            pltpu.VMEM((LEAF, RANK), BF16),
            pltpu.VMEM((1, RANK, RANK), BF16),
            pltpu.VMEM((LEAF + 4 * DIM, OUT), BF16),
            pltpu.VMEM((N_DEV, 16, RANK), BF16),
            pltpu.VMEM((LEAF, RANK), BF16),
            rows16,
            dma((9,)),
        ],
        SHORT,
    )

    def near_own(values):
        (near,) = call(
            near_own_kernel,
            "near_own",
            [(field, F32, VMEM)],
            [HBM] * 2,
            (wc, values),
            [places, pltpu.VMEM(field, BF16), dma((2,))],
            SHORT,
        )
        return near

    def near_pair(distance, near, first, fields, after, flops):
        (near,) = call(
            lambda *refs: near_pair_kernel((-distance, distance), *refs),
            f"near_pair_{distance}",
            [(field, F32, VMEM)],
            [SMEM, HBM, VMEM] + [ANY] * 5,
            (near_list, wc, near, first[0], fields[0], first[1], fields[1], after),
            [pltpu.VMEM((3, 4 * DIM, OUT), BF16), pltpu.VMEM((2, *field), BF16), dma((5,))],
            flops,
        )
        return near

    def through_owners(sums, skeletons):
        all_sums = exchanged(sums, "grp")
        (partners,) = call(
            partners_kernel,
            "partners",
            [((N_DEV, 3, 8, RANK), BF16, HBM)],
            [VMEM] * 2,
            (skeletons, told),
            [rows16, pltpu.VMEM((N_DEV, 2, 8, RANK), BF16), dma((1,))],
            SHORT,
        )
        (sent,) = call(
            couple_kernel,
            "couple",
            [((N_DEV, 3, 8, RANK), BF16, HBM)],
            [SMEM] + [VMEM] * 3 + [HBM],
            (far_clusters, all_sums, cluster_couplings, told, partners),
            [rows8, pltpu.VMEM((N_DEV, 8, RANK), BF16), dma((1,))],
            SHORT,
            {4: 0},
        )
        return sent, exchanged(sent, "dev")

    arrived = exchanged(sent, "dev")
    near = near_own(wc)
    first2 = from_pair(wc, 2, near)
    sums, told, skeletons = call(
        sums_first_kernel,
        "sums_first",
        [((N_GRP, 16, RANK), BF16, VMEM), ((N_DEV, RANK), F32, VMEM), ((N_DEV, COLS * RANK), BF16, VMEM)],
        [VMEM, ANY],
        (arrived, near),
        [rows16, narrow],
        SHORT,
    )
    sent, arrived = through_owners(sums, skeletons)
    first1 = from_pair(wc, 1, sent)
    near = near_pair(2, near, first2, first2, sent, MID)
    near = near_pair(1, near, first1, first1, sent, LONG)
    w, sent, r1 = call(
        middle_kernel,
        "middle",
        [(field, BF16, HBM), ((N_DEV, 8, RANK), BF16, HBM), (field, F32, HBM)],
        [SMEM] + [VMEM] * 5 + [HBM],
        (ridge, arrived, couplings, transfer, basis, near, right_side),
        [
            pltpu.VMEM(field, F32),
            pltpu.VMEM(field, BF16),
            pltpu.VMEM((N_DEV, 8, RANK), BF16),
            pltpu.VMEM(field, F32),
            rows24,
            rows8,
            dma((10,)),
        ],
        SHORT,
    )
    arrived = exchanged(sent, "dev")
    near = near_own(w)
    fields2 = from_pair(w, 2, near)
    sums, skeletons = call(
        sums_kernel,
        "sums",
        [((N_GRP, 16, RANK), BF16, VMEM), ((N_DEV, COLS * RANK), BF16, VMEM)],
        [VMEM, VMEM, ANY],
        (arrived, told, near),
        [rows8, narrow],
        SHORT,
    )
    sent, arrived = through_owners(sums, skeletons)
    fields1 = from_pair(w, 1, sent)
    near = near_pair(2, near, first2, fields2, sent, MID)
    near = near_pair(1, near, first1, fields1, sent, LONG)
    return tuple(
        call(
            end_kernel,
            "end",
            [(field, F32, HBM), (field, F32, HBM)],
            [SMEM] + [VMEM] * 5 + [HBM] * 2,
            (ridge, arrived, couplings, transfer, basis, near, right_side, r1),
            [pltpu.VMEM(field, F32)] * 4 + [rows24, dma((10,))],
            SHORT,
        )
    )


def solution(mesh):
    placed = (
        P(("grp", "dev"), None),
        P(("grp", "dev"), None),
        P(("grp", "dev"), None),
        P(("grp", "dev"), None),
        P(("grp", "dev"), None),
        P(("grp", "dev"), None, None, None),
        P(("grp", "dev"), None, None),
        P(("grp", "dev"), None),
        P(("grp", "dev")),
        P("grp", None),
        P("grp", None, None, None),
        P(),
    )
    return jax.shard_map(
        body,
        mesh=mesh,
        in_specs=placed,
        out_specs=(P(("grp", "dev"), None), P(("grp", "dev"), None)),
        check_vma=False,
    )
```

```python
import jax
import jax.numpy as jnp
from jax import lax
from jax.experimental import pallas as pl
from jax.experimental.pallas import tpu as pltpu
from jax.sharding import PartitionSpec as P

LEAF, DIM, OUT, RANK = 512, 64, 256, 128
N_GRP, N_DEV, CPG = 8, 64, 4
FAR1, FAR2 = 4, 4
COLS = OUT // N_DEV
NEAR = 4

KERNEL_LOG2 = -1.4426950408889634 / 32.0
GAP, TOP = 0.5, 8.0

F32, BF16 = jnp.float32, jnp.bfloat16
VMEM = pl.BlockSpec(memory_space=pltpu.VMEM)
SMEM = pl.BlockSpec(memory_space=pltpu.SMEM)
ANY = pl.BlockSpec(memory_space=pl.ANY)
HBM = pl.BlockSpec(memory_space=pltpu.HBM)
LIMIT = 32 * 2**20
SHORT, MID, LONG = 10**7, 10**10, 10**9
ROWS = 128


def dot(a, b, dims=((1,), (0,))):
    return lax.dot_general(a, b, (dims, ((), ())), preferred_element_type=F32)


def call(kernel, name, outs, ins, args, scratch=(), flops=0, aliases=None):
    shapes = [(pltpu.HBM if spec is HBM else jax.ShapeDtypeStruct)(shape, kind) for shape, kind, spec in outs]
    args = [
        pltpu.with_memory_space_constraint(arg, pltpu.HBM) if spec is HBM else arg for arg, spec in zip(args, ins)
    ]
    return pl.pallas_call(
        kernel,
        name=name,
        out_shape=shapes,
        in_specs=ins,
        out_specs=[spec for _, _, spec in outs],
        scratch_shapes=list(scratch),
        input_output_aliases=aliases or {},
        compiler_params=pltpu.CompilerParams(vmem_limit_bytes=LIMIT),
        cost_estimate=pl.CostEstimate(flops=flops, bytes_accessed=0, transcendentals=0),
    )(*args)


def started(pairs, sems, first=0):
    copies = [pltpu.make_async_copy(a, b, sems.at[first + i]) for i, (a, b) in enumerate(pairs)]
    for copy in copies:
        copy.start()
    return copies


def wait(copies):
    for copy in copies:
        copy.wait()


def chebyshev(ridge):
    ridge = jnp.full((1, 1), ridge, F32)
    bottom, top = ridge + GAP, ridge + TOP
    centre, spread = (top + bottom) / 2.0, (top - bottom) / 2.0
    sigma = centre / spread
    rho0 = 1.0 / sigma
    rho1 = 1.0 / (2.0 * sigma - rho0)
    rho2 = 1.0 / (2.0 * sigma - rho1)
    first = (rho1 * rho0, 2.0 * rho1 / spread)
    second = (rho2 * rho1, 2.0 * rho2 / spread)
    return ridge, centre, first, second


def to_owners(values, basis, transfer, staged, rows):
    skeleton = dot(values, basis, ((0,), (0,))).astype(BF16)
    uplift = dot(skeleton, transfer)
    skeleton = skeleton.astype(F32)
    for i in range(COLS):
        part = slice(N_DEV * i, N_DEV * (i + 1))
        staged[pl.ds(i, N_DEV, stride=rows), :] = skeleton[part]
        staged[pl.ds(COLS + i, N_DEV, stride=rows), :] = uplift[part]


def start_kernel(
    ridge, cluster, far_in, rs_in, coords_in, perm_in, basis_in, transfer_in, wc_out, sent_out, placed_out,
    far, rs, coords, perm, basis, transfer, wc, sent, placed, staged, sems,
):
    copies = started(
        (
            (perm_in, perm), (basis_in, basis), (rs_in, rs), (coords_in, coords),
            (transfer_in, transfer), (far_in, far),
        ),
        sems,
    )
    staged[...] = jnp.zeros_like(staged)
    _, centre, _, _ = chebyshev(ridge[0])
    wait(copies[:2])
    point = lax.broadcasted_iota(jnp.int32, (LEAF, LEAF), 0)
    pick = jnp.where(point == perm[...], 1.0, 0.0).astype(BF16)
    basis_here = dot(pick, basis[...]).astype(BF16)
    placed[...] = basis_here
    wait(copies[2:4])
    values = (rs[...] / centre).astype(BF16)
    wc[:LEAF] = values
    high = coords[...].astype(BF16)
    low = (coords[...] - high.astype(F32)).astype(BF16)
    parts = jnp.concatenate([high, low], axis=0)
    wc[LEAF : LEAF + 2 * DIM] = parts[:, :OUT]
    wc[LEAF + 2 * DIM :] = parts[:, OUT:]
    outs = started(((wc, wc_out), (placed, placed_out)), sems, 6)
    wait(copies[4:])
    to_owners(values, basis_here, transfer[0], staged, 16)
    lane = lax.broadcasted_iota(jnp.int32, (N_DEV, RANK), 1)
    told = jnp.where(lane == FAR1, (cluster[0] % CPG).astype(F32), 0.0)
    for k in range(FAR1):
        told = jnp.where(lane == k, (far[0, k] % N_DEV).astype(F32), told)
    staged[pl.ds(8, N_DEV, stride=16), :] = told
    sent[...] = staged[...].astype(BF16).reshape(N_DEV, 16, RANK)
    outs += started(((sent, sent_out),), sems, 8)
    wait(outs)


def owner_sums(staged, rows, told, sums, narrow):
    lane = lax.broadcasted_iota(jnp.int32, (N_DEV, RANK), 1).astype(F32)
    member = jnp.where(lane == told[:, FAR1 : FAR1 + 1], 1.0, 0.0).astype(BF16)
    uplifts = jnp.concatenate(
        [staged[pl.ds(COLS + i, N_DEV, stride=rows), :] for i in range(COLS)], axis=1
    ).astype(BF16)
    total = dot(member, uplifts, ((0,), (0,)))
    for i in range(COLS):
        narrow[pl.ds(CPG * i, CPG), :] = total[:CPG, RANK * i : RANK * (i + 1)]
    out = narrow[...].astype(BF16)
    for g in range(N_GRP):
        sums[g] = out


def sums_first_kernel(arrived, _, sums, told, skeletons, staged, narrow):
    staged[...] = arrived[...].astype(F32).reshape(N_DEV * 16, RANK)
    told[...] = staged[pl.ds(8, N_DEV, stride=16), :]
    owner_sums(staged, 16, told[...], sums, narrow)
    skeletons[...] = jnp.concatenate(
        [staged[pl.ds(i, N_DEV, stride=16), :] for i in range(COLS)], axis=1
    ).astype(BF16)


def sums_kernel(arrived, told, _, sums, skeletons, staged, narrow):
    staged[...] = arrived[...].astype(F32).reshape(N_DEV * 8, RANK)
    owner_sums(staged, 8, told[...], sums, narrow)
    skeletons[...] = jnp.concatenate(
        [staged[pl.ds(i, N_DEV, stride=8), :] for i in range(COLS)], axis=1
    ).astype(BF16)


def partners_kernel(skeletons, told, sent_out, done, staged, sent, sems):
    lane = lax.broadcasted_iota(jnp.int32, (N_DEV, N_DEV), 1).astype(F32)
    pick = jnp.concatenate(
        [jnp.where(lane == told[:, k : k + 1], 1.0, 0.0) for k in range(FAR1)], axis=0
    ).astype(BF16)
    picked = dot(pick, skeletons[...])
    for k in range(FAR1):
        for i in range(COLS):
            staged[pl.ds(COLS * k + i, N_DEV, stride=16), :] = picked[
                N_DEV * k : N_DEV * (k + 1), RANK * i : RANK * (i + 1)
            ]
    sent[...] = staged[...].reshape(N_DEV, 2, 8, RANK).astype(BF16)
    done[...] = jnp.zeros_like(done)
    wait(started(((sent, sent_out.at[:, :2]),), sems))


def couple_kernel(far_clusters, all_sums, blocks, told, _, sent_out, staged, sent, sems):
    rows = COLS * CPG
    sums = all_sums[...].reshape(N_GRP * rows, RANK)
    row = lax.broadcasted_iota(jnp.int32, (rows, N_GRP * rows), 0)
    lane = lax.broadcasted_iota(jnp.int32, (rows, N_GRP * rows), 1)
    column, cluster = row // CPG, row % CPG
    total = jnp.zeros((CPG * RANK, rows), F32)
    for k in range(FAR2):
        target = CPG * column
        for c in range(CPG):
            f = far_clusters[c, k]
            target += jnp.where(cluster == c, rows * (f // CPG) + f % CPG, 0)
        pick = jnp.where(lane == target, 1.0, 0.0).astype(BF16)
        picked = dot(pick, sums).astype(BF16)
        total += dot(blocks[:, k].reshape(CPG * RANK, RANK), picked, ((1,), (1,)))
    own = lax.broadcasted_iota(jnp.int32, (RANK, rows), 1) % CPG
    coupled = jnp.zeros((RANK, rows), F32)
    for c in range(CPG):
        coupled += jnp.where(own == c, total[RANK * c : RANK * (c + 1)], 0.0)
    coupled = coupled.T
    coupled = coupled.astype(BF16)
    lane = lax.broadcasted_iota(jnp.int32, (N_DEV, rows), 1).astype(F32)
    pick = jnp.concatenate(
        [jnp.where(lane == told[:, FAR1 : FAR1 + 1] + CPG * i, 1.0, 0.0) for i in range(COLS)], axis=0
    ).astype(BF16)
    out = dot(pick, coupled)
    staged[...] = jnp.zeros_like(staged)
    for i in range(COLS):
        staged[pl.ds(i, N_DEV, stride=8), :] = out[N_DEV * i : N_DEV * (i + 1)]
    sent[...] = staged[...].reshape(N_DEV, 8, RANK).astype(BF16)
    wait(started(((sent, sent_out.at[:, 2]),), sems))


def local_field(arrived, couplings, transfer, staged):
    staged[...] = arrived[...].astype(F32).reshape(N_DEV * 24, RANK)
    local = jnp.zeros((OUT, RANK), F32)
    for k in range(FAR1 + 1):
        skeleton = jnp.concatenate(
            [staged[pl.ds(COLS * k + i, N_DEV, stride=24), :] for i in range(COLS)], axis=0
        ).astype(BF16)
        local += dot(skeleton, couplings[0, k] if k < FAR1 else transfer[0], ((1,), (1,)))
    return local.T.astype(BF16)


def middle_kernel(
    ridge, arrived, couplings, transfer, basis, near, rs_in, w_out, sent_out, r1_out,
    rs, w, sent, r1, staged, staged_out, sems,
):
    copies = started(((rs_in, rs),), sems)
    ridge, centre, (mul, add), _ = chebyshev(ridge[0])
    local = local_field(arrived, couplings, transfer, staged)
    wait(copies)
    outs = []
    for n, r in enumerate(range(0, LEAF, ROWS)):
        part = slice(r, r + ROWS)
        here = rs[part]
        d1 = here / centre
        residual = here - (ridge * d1 + (near[part] + dot(basis[part], local)))
        r1[part] = residual
        w[part] = (mul * d1 + add * residual).astype(BF16)
        at = pl.ds(r, ROWS)
        outs += started(((r1.at[at], r1_out.at[at]), (w.at[at], w_out.at[at])), sems, 1 + 2 * n)
    to_owners(w[...], basis[...], transfer[0], staged_out, 8)
    sent[...] = staged_out[...].astype(BF16).reshape(N_DEV, 8, RANK)
    outs += started(((sent, sent_out),), sems, 9)
    wait(outs)


def end_kernel(
    ridge, arrived, couplings, transfer, basis, near, rs_in, r1_in, solution_out, residual_out,
    rs, r1, solution, residual, staged, sems,
):
    copies = started(((rs_in, rs), (r1_in, r1)), sems)
    ridge, centre, (mul1, add1), (mul, add) = chebyshev(ridge[0])
    local = local_field(arrived, couplings, transfer, staged)
    wait(copies)
    outs = []
    for n, r in enumerate(range(0, LEAF, ROWS)):
        part = slice(r, r + ROWS)
        d1 = rs[part] / centre
        d2 = mul1 * d1 + add1 * r1[part]
        r2 = r1[part] - (ridge * d2 + (near[part] + dot(basis[part], local)))
        residual[part] = r2
        solution[part] = d1 + d2 + (mul * d2 + add * r2)
        at = pl.ds(r, ROWS)
        outs += started(
            ((residual.at[at], residual_out.at[at]), (solution.at[at], solution_out.at[at])), sems, 2 + 2 * n
        )
    wait(outs)


def coordinates(held):
    parts = jnp.concatenate([held[: 2 * DIM], held[2 * DIM :]], axis=1)
    high, low = parts[:DIM], parts[DIM:]
    points = high.astype(F32) + low.astype(F32)
    return high, low, jnp.sum(points * points, axis=0, keepdims=True) * KERNEL_LOG2


def listed(near_list, offset):
    leaf = lax.axis_index("grp") * N_DEV + lax.axis_index("dev")
    hit = near_list[0, 0] == leaf + offset
    for k in range(1, NEAR):
        hit = hit | (near_list[0, k] == leaf + offset)
    return hit


def block_times(here, there, values, total, fresh):
    high, low, norm = here
    left = jnp.concatenate([high, high, low, low], axis=0)
    column = jnp.broadcast_to(norm, (RANK, LEAF)).T[:, :1]
    high, low, across = there
    right = jnp.concatenate([high, low, high, low], axis=0)
    step = 128
    for r in range(0, LEAF, step):
        part = slice(r, r + step)
        inner = dot(left[:, part], right, ((0,), (0,)))
        entries = jnp.exp2((column[part] + across) - (2.0 * KERNEL_LOG2) * inner).astype(BF16)
        product = dot(entries, values)
        total[part] = product if fresh else total[part] + product


def near_kernel(offsets, own, near_list, places_in, before, p1, v1, p2, v2, _, total, places, values, sems):
    pairs = [(p.at[pl.ds(LEAF, 4 * DIM)], places.at[i]) for i, p in enumerate((places_in, p1, p2))]
    pairs += [(v.at[pl.ds(0, LEAF)], values.at[i]) for i, v in enumerate((v1, v2))]
    if own:
        pairs.append((before.at[pl.ds(0, LEAF)], values.at[2]))
    else:
        pairs.append((before, total))
    copies = started(pairs, sems)
    wait(copies)
    mine = coordinates(places[0])
    if own:
        block_times(mine, mine, values[2], total, True)
    for i, offset in enumerate(offsets):

        @pl.when(listed(near_list, offset))
        def _():
            block_times(mine, coordinates(places[1 + i]), values[i], total, False)


def mark_kernel(_, mark):
    mark[...] = jnp.zeros_like(mark)


def from_behind(shard, by):
    pairs = [(i, i + by) for i in range(N_DEV) if 0 <= i + by < N_DEV]
    return lax.ppermute(shard, "dev", pairs)


def passed_on(pair, after):
    behind, ahead, _ = lax.optimization_barrier((*pair, after))
    return from_behind(behind, 1), from_behind(ahead, -1)


def exchanged(blocks, axis):
    return lax.all_to_all(blocks, axis, split_axis=0, concat_axis=0, tiled=True)


def body(
    coords,
    right_side,
    leaf_perm,
    near_list,
    far_leaves,
    couplings,
    transfer,
    leaf_basis,
    cluster_of,
    far_clusters,
    cluster_couplings,
    ridge_weight,
):
    ridge = ridge_weight.reshape(1)
    field, dma = (LEAF, OUT), pltpu.SemaphoreType.DMA
    rows24 = pltpu.VMEM((N_DEV * 24, RANK), F32)
    rows16 = pltpu.VMEM((N_DEV * 16, RANK), F32)
    rows8 = pltpu.VMEM((N_DEV * 8, RANK), F32)
    narrow = pltpu.VMEM((COLS * CPG, RANK), F32)

    wc, sent, basis = call(
        start_kernel,
        "start",
        [
            ((LEAF + 4 * DIM, OUT), BF16, HBM),
            ((N_DEV, 16, RANK), BF16, HBM),
            ((LEAF, RANK), BF16, HBM),
        ],
        [SMEM] * 2 + [HBM] * 6,
        (ridge, cluster_of, far_leaves, right_side, coords.T, leaf_perm, leaf_basis, transfer),
        [
            pltpu.SMEM((1, FAR1), jnp.int32),
            pltpu.VMEM(field, F32),
            pltpu.VMEM((DIM, LEAF), F32),
            pltpu.VMEM((1, LEAF), jnp.int32),
            pltpu.VMEM((LEAF, RANK), BF16),
            pltpu.VMEM((1, RANK, RANK), BF16),
            pltpu.VMEM((LEAF + 4 * DIM, OUT), BF16),
            pltpu.VMEM((N_DEV, 16, RANK), BF16),
            pltpu.VMEM((LEAF, RANK), BF16),
            rows16,
            dma((9,)),
        ],
        SHORT,
    )

    def near_with(distance, own, before, first, fields, after, flops):
        (near,) = call(
            lambda *refs: near_kernel((-distance, distance), own, *refs),
            f"near_{distance}",
            [(field, F32, VMEM)],
            [SMEM, HBM] + [ANY] * 6,
            (near_list, wc, before, first[0], fields[0], first[1], fields[1], after),
            [pltpu.VMEM((3, 4 * DIM, OUT), BF16), pltpu.VMEM((3, *field), BF16), dma((6,))],
            flops,
        )
        return near

    def marked(shard):
        (mark,) = call(mark_kernel, "mark", [((8, RANK), F32, VMEM)], [ANY], (shard,), flops=SHORT)
        return mark

    def through_owners(sums, skeletons):
        all_sums = exchanged(sums, "grp")
        partners, done = call(
            partners_kernel,
            "partners",
            [((N_DEV, 3, 8, RANK), BF16, HBM), ((8, RANK), F32, VMEM)],
            [VMEM] * 2,
            (skeletons, told),
            [rows16, pltpu.VMEM((N_DEV, 2, 8, RANK), BF16), dma((1,))],
            SHORT,
        )
        (sent,) = call(
            couple_kernel,
            "couple",
            [((N_DEV, 3, 8, RANK), BF16, HBM)],
            [SMEM] + [VMEM] * 3 + [HBM],
            (far_clusters, all_sums, cluster_couplings, told, partners),
            [rows8, pltpu.VMEM((N_DEV, 8, RANK), BF16), dma((1,))],
            SHORT,
            {4: 0},
        )
        return sent, exchanged(sent, "dev"), done

    arrived = exchanged(sent, "dev")
    mark = marked(wc)
    first1 = passed_on((wc, wc), mark)
    sums, told, skeletons = call(
        sums_first_kernel,
        "sums_first",
        [((N_GRP, 16, RANK), BF16, VMEM), ((N_DEV, RANK), F32, VMEM), ((N_DEV, COLS * RANK), BF16, VMEM)],
        [VMEM, ANY],
        (arrived, mark),
        [rows16, narrow],
        SHORT,
    )
    sent, arrived, done = through_owners(sums, skeletons)
    first2 = passed_on(first1, done)
    near = near_with(1, True, wc, first1, first1, sent, MID)
    near = near_with(2, False, near, first2, first2, sent, LONG)
    w, sent, r1 = call(
        middle_kernel,
        "middle",
        [(field, BF16, HBM), ((N_DEV, 8, RANK), BF16, HBM), (field, F32, HBM)],
        [SMEM] + [VMEM] * 5 + [HBM],
        (ridge, arrived, couplings, transfer, basis, near, right_side),
        [
            pltpu.VMEM(field, F32),
            pltpu.VMEM(field, BF16),
            pltpu.VMEM((N_DEV, 8, RANK), BF16),
            pltpu.VMEM(field, F32),
            rows24,
            rows8,
            dma((10,)),
        ],
        SHORT,
    )
    arrived = exchanged(sent, "dev")
    mark = marked(w)
    fields1 = passed_on((w, w), mark)
    sums, skeletons = call(
        sums_kernel,
        "sums",
        [((N_GRP, 16, RANK), BF16, VMEM), ((N_DEV, COLS * RANK), BF16, VMEM)],
        [VMEM, VMEM, ANY],
        (arrived, told, mark),
        [rows8, narrow],
        SHORT,
    )
    sent, arrived, done = through_owners(sums, skeletons)
    fields2 = passed_on(fields1, done)
    near = near_with(1, True, w, first1, fields1, sent, MID)
    near = near_with(2, False, near, first2, fields2, sent, LONG)
    return tuple(
        call(
            end_kernel,
            "end",
            [(field, F32, HBM), (field, F32, HBM)],
            [SMEM] + [VMEM] * 5 + [HBM] * 2,
            (ridge, arrived, couplings, transfer, basis, near, right_side, r1),
            [pltpu.VMEM(field, F32)] * 4 + [rows24, dma((10,))],
            SHORT,
        )
    )


def solution(mesh):
    placed = (
        P(("grp", "dev"), None),
        P(("grp", "dev"), None),
        P(("grp", "dev"), None),
        P(("grp", "dev"), None),
        P(("grp", "dev"), None),
        P(("grp", "dev"), None, None, None),
        P(("grp", "dev"), None, None),
        P(("grp", "dev"), None),
        P(("grp", "dev")),
        P("grp", None),
        P("grp", None, None, None),
        P(),
    )
    return jax.shard_map(
        body,
        mesh=mesh,
        in_specs=placed,
        out_specs=(P(("grp", "dev"), None), P(("grp", "dev"), None)),
        check_vma=False,
    )
```

```python
import jax
import jax.numpy as jnp
from jax import lax
from jax.experimental import pallas as pl
from jax.experimental.pallas import tpu as pltpu
from jax.sharding import PartitionSpec as P

LEAF, DIM, OUT, RANK = 512, 64, 256, 128
N_GRP, N_DEV, CPG = 8, 64, 4
FAR1, FAR2 = 4, 4
COLS = OUT // N_DEV
NEAR = 4

KERNEL_LOG2 = -1.4426950408889634 / 32.0
GAP, TOP = 0.5, 8.0

F32, BF16 = jnp.float32, jnp.bfloat16
VMEM = pl.BlockSpec(memory_space=pltpu.VMEM)
SMEM = pl.BlockSpec(memory_space=pltpu.SMEM)
ANY = pl.BlockSpec(memory_space=pl.ANY)
HBM = pl.BlockSpec(memory_space=pltpu.HBM)
LIMIT = 32 * 2**20
SHORT, MID, LONG = 10**7, 10**10, 10**9
ROWS = 128


def dot(a, b, dims=((1,), (0,))):
    return lax.dot_general(a, b, (dims, ((), ())), preferred_element_type=F32)


def call(kernel, name, outs, ins, args, scratch=(), flops=0, aliases=None):
    shapes = [(pltpu.HBM if spec is HBM else jax.ShapeDtypeStruct)(shape, kind) for shape, kind, spec in outs]
    args = [
        pltpu.with_memory_space_constraint(arg, pltpu.HBM) if spec is HBM else arg for arg, spec in zip(args, ins)
    ]
    return pl.pallas_call(
        kernel,
        name=name,
        out_shape=shapes,
        in_specs=ins,
        out_specs=[spec for _, _, spec in outs],
        scratch_shapes=list(scratch),
        input_output_aliases=aliases or {},
        compiler_params=pltpu.CompilerParams(vmem_limit_bytes=LIMIT),
        cost_estimate=pl.CostEstimate(flops=flops, bytes_accessed=0, transcendentals=0),
    )(*args)


def started(pairs, sems, first=0):
    copies = [pltpu.make_async_copy(a, b, sems.at[first + i]) for i, (a, b) in enumerate(pairs)]
    for copy in copies:
        copy.start()
    return copies


def wait(copies):
    for copy in copies:
        copy.wait()


def chebyshev(ridge):
    ridge = jnp.full((1, 1), ridge, F32)
    bottom, top = ridge + GAP, ridge + TOP
    centre, spread = (top + bottom) / 2.0, (top - bottom) / 2.0
    sigma = centre / spread
    rho0 = 1.0 / sigma
    rho1 = 1.0 / (2.0 * sigma - rho0)
    rho2 = 1.0 / (2.0 * sigma - rho1)
    first = (rho1 * rho0, 2.0 * rho1 / spread)
    second = (rho2 * rho1, 2.0 * rho2 / spread)
    return ridge, centre, first, second


def to_owners(values, basis, transfer, staged, rows):
    skeleton = dot(values, basis, ((0,), (0,))).astype(BF16)
    uplift = dot(skeleton, transfer)
    skeleton = skeleton.astype(F32)
    for i in range(COLS):
        part = slice(N_DEV * i, N_DEV * (i + 1))
        staged[pl.ds(i, N_DEV, stride=rows), :] = skeleton[part]
        staged[pl.ds(COLS + i, N_DEV, stride=rows), :] = uplift[part]


def start_kernel(
    ridge, cluster, far_in, rs_in, coords_in, perm_in, basis_in, transfer_in, wc_out, sent_out, placed,
    far, rs, coords, perm, basis, transfer, wc, sent, staged, sems,
):
    copies = started(
        (
            (perm_in, perm), (basis_in, basis), (rs_in, rs), (coords_in, coords),
            (transfer_in, transfer), (far_in, far),
        ),
        sems,
    )
    staged[...] = jnp.zeros_like(staged)
    _, centre, _, _ = chebyshev(ridge[0])
    wait(copies[:2])
    point = lax.broadcasted_iota(jnp.int32, (LEAF, LEAF), 0)
    pick = jnp.where(point == perm[...], 1.0, 0.0).astype(BF16)
    basis_here = dot(pick, basis[...]).astype(BF16)
    placed[...] = basis_here
    wait(copies[2:4])
    values = (rs[...] / centre).astype(BF16)
    wc[:LEAF] = values
    high = coords[...].astype(BF16)
    low = (coords[...] - high.astype(F32)).astype(BF16)
    parts = jnp.concatenate([high, low], axis=0)
    wc[LEAF : LEAF + 2 * DIM] = parts[:, :OUT]
    wc[LEAF + 2 * DIM :] = parts[:, OUT:]
    outs = started(((wc, wc_out),), sems, 6)
    wait(copies[4:])
    to_owners(values, basis_here, transfer[0], staged, 16)
    lane = lax.broadcasted_iota(jnp.int32, (N_DEV, RANK), 1)
    told = jnp.where(lane == FAR1, (cluster[0] % CPG).astype(F32), 0.0)
    for k in range(FAR1):
        told = jnp.where(lane == k, (far[0, k] % N_DEV).astype(F32), told)
    staged[pl.ds(8, N_DEV, stride=16), :] = told
    sent[...] = staged[...].astype(BF16).reshape(N_DEV, 16, RANK)
    outs += started(((sent, sent_out),), sems, 8)
    wait(outs)


def owner_sums(staged, rows, told, sums, narrow):
    lane = lax.broadcasted_iota(jnp.int32, (N_DEV, RANK), 1).astype(F32)
    member = jnp.where(lane == told[:, FAR1 : FAR1 + 1], 1.0, 0.0).astype(BF16)
    uplifts = jnp.concatenate(
        [staged[pl.ds(COLS + i, N_DEV, stride=rows), :] for i in range(COLS)], axis=1
    ).astype(BF16)
    total = dot(member, uplifts, ((0,), (0,)))
    for i in range(COLS):
        narrow[pl.ds(CPG * i, CPG), :] = total[:CPG, RANK * i : RANK * (i + 1)]
    out = narrow[...].astype(BF16)
    for g in range(N_GRP):
        sums[g] = out


def sums_first_kernel(arrived, _, sums, told, skeletons, staged, narrow):
    staged[...] = arrived[...].astype(F32).reshape(N_DEV * 16, RANK)
    told[...] = staged[pl.ds(8, N_DEV, stride=16), :]
    owner_sums(staged, 16, told[...], sums, narrow)
    skeletons[...] = jnp.concatenate(
        [staged[pl.ds(i, N_DEV, stride=16), :] for i in range(COLS)], axis=1
    ).astype(BF16)


def sums_kernel(arrived, told, _, sums, skeletons, staged, narrow):
    staged[...] = arrived[...].astype(F32).reshape(N_DEV * 8, RANK)
    owner_sums(staged, 8, told[...], sums, narrow)
    skeletons[...] = jnp.concatenate(
        [staged[pl.ds(i, N_DEV, stride=8), :] for i in range(COLS)], axis=1
    ).astype(BF16)


def partners_kernel(skeletons, told, sent_out, done, staged, sent, sems):
    lane = lax.broadcasted_iota(jnp.int32, (N_DEV, N_DEV), 1).astype(F32)
    pick = jnp.concatenate(
        [jnp.where(lane == told[:, k : k + 1], 1.0, 0.0) for k in range(FAR1)], axis=0
    ).astype(BF16)
    picked = dot(pick, skeletons[...])
    for k in range(FAR1):
        for i in range(COLS):
            staged[:, i, RANK * k : RANK * (k + 1)] = picked[
                N_DEV * k : N_DEV * (k + 1), RANK * i : RANK * (i + 1)
            ]
    sent[...] = staged[...].astype(BF16)
    done[...] = jnp.zeros_like(done)
    wait(started(((sent, sent_out.at[:, :, pl.ds(0, FAR1 * RANK)]),), sems))


def couple_kernel(picks, all_sums, blocks, told, _, sent_out, staged, sent, sems):
    rows = COLS * CPG
    picked = dot(picks[...], all_sums[...].reshape(N_GRP * rows, RANK)).astype(BF16)
    total = jnp.zeros((CPG * RANK, rows), F32)
    for k in range(FAR2):
        block = blocks[:, k].reshape(CPG * RANK, RANK)
        total += dot(block, picked[rows * k : rows * (k + 1)], ((1,), (1,)))
    own = lax.broadcasted_iota(jnp.int32, (RANK, rows), 1) % CPG
    coupled = jnp.zeros((RANK, rows), F32)
    for c in range(CPG):
        coupled += jnp.where(own == c, total[RANK * c : RANK * (c + 1)], 0.0)
    coupled = coupled.T.astype(BF16)
    lane = lax.broadcasted_iota(jnp.int32, (N_DEV, rows), 1).astype(F32)
    pick = jnp.concatenate(
        [jnp.where(lane == told[:, FAR1 : FAR1 + 1] + CPG * i, 1.0, 0.0) for i in range(COLS)], axis=0
    ).astype(BF16)
    out = dot(pick, coupled)
    for i in range(COLS):
        staged[:, i, :] = out[N_DEV * i : N_DEV * (i + 1)]
    sent[...] = staged[...].astype(BF16)
    wait(started(((sent, sent_out.at[:, :, pl.ds(FAR1 * RANK, RANK)]),), sems))


def local_field(arrived, couplings, transfer, staged):
    staged[...] = arrived[...].astype(F32)
    local = jnp.zeros((OUT, RANK), F32)
    for k in range(FAR1 + 1):
        skeleton = jnp.concatenate(
            [staged[:, i, RANK * k : RANK * (k + 1)] for i in range(COLS)], axis=0
        ).astype(BF16)
        local += dot(skeleton, couplings[0, k] if k < FAR1 else transfer[0], ((1,), (1,)))
    return local.T.astype(BF16)


def middle_kernel(
    arrived, couplings, transfer, basis, residual, direction, factor, w, sent_out, r1, sent, staged, staged_out, sems
):
    local = local_field(arrived, couplings, transfer, staged)
    for r in range(0, LEAF, ROWS):
        part = slice(r, r + ROWS)
        far = dot(basis[part], local)
        r1[part] = residual[part] - far
        w[part] = (direction[part] - factor[:1, :1] * far).astype(BF16)
    to_owners(w[...], basis[...], transfer[0], staged_out, 8)
    sent[...] = staged_out[...].astype(BF16).reshape(N_DEV, 8, RANK)
    wait(started(((sent, sent_out),), sems))


def end_kernel(
    arrived, couplings, transfer, basis, before_r, before_s, factor, solution_out, residual_out,
    solution, residual, staged, sems,
):
    local = local_field(arrived, couplings, transfer, staged)
    outs = []
    for n, r in enumerate(range(0, LEAF, ROWS)):
        part = slice(r, r + ROWS)
        far = dot(basis[part], local)
        residual[part] = before_r[part] - far
        solution[part] = before_s[part] - factor[:1, :1] * far
        at = pl.ds(r, ROWS)
        outs += started(
            ((residual.at[at], residual_out.at[at]), (solution.at[at], solution_out.at[at])), sems, 2 * n
        )
    wait(outs)


def coordinates(held):
    parts = jnp.concatenate([held[: 2 * DIM], held[2 * DIM :]], axis=1)
    high, low = parts[:DIM], parts[DIM:]
    points = high.astype(F32) + low.astype(F32)
    return high, low, jnp.sum(points * points, axis=0, keepdims=True) * KERNEL_LOG2


def listed(near_list, offset):
    leaf = lax.axis_index("grp") * N_DEV + lax.axis_index("dev")
    hit = near_list[0, 0] == leaf + offset
    for k in range(1, NEAR):
        hit = hit | (near_list[0, k] == leaf + offset)
    return hit


def block_times(here, there, values, total, fresh):
    high, low, norm = here
    left = jnp.concatenate([high, high, low, low], axis=0)
    column = jnp.broadcast_to(norm, (RANK, LEAF)).T[:, :1]
    high, low, across = there
    right = jnp.concatenate([high, low, high, low], axis=0)
    step = 128
    for r in range(0, LEAF, step):
        part = slice(r, r + step)
        inner = dot(left[:, part], right, ((0,), (0,)))
        entries = jnp.exp2((column[part] + across) - (2.0 * KERNEL_LOG2) * inner).astype(BF16)
        product = dot(entries, values)
        total[part] = product if fresh else total[part] + product


def near_products(offsets, near_list, mine, places, values, total):
    for i, offset in enumerate(offsets):

        @pl.when(listed(near_list, offset))
        def _():
            block_times(mine, coordinates(places[1 + i]), values[i], total, False)


def near_pairs(places_in, p1, v1, p2, v2, places, values):
    pairs = [(p.at[pl.ds(LEAF, 4 * DIM)], places.at[i]) for i, p in enumerate((places_in, p1, p2))]
    return pairs + [(v.at[pl.ds(0, LEAF)], values.at[i]) for i, v in enumerate((v1, v2))]


def near_1_kernel(near_list, places_in, own, p1, v1, p2, v2, _, total, places, values, sems):
    pairs = near_pairs(places_in, p1, v1, p2, v2, places, values)
    wait(started([*pairs, (own.at[pl.ds(0, LEAF)], values.at[2])], sems))
    mine = coordinates(places[0])
    block_times(mine, mine, values[2], total, True)
    near_products((-1, 1), near_list, mine, places, values, total)


def near_2_kernel(
    last, ridge, near_list, places_in, before, p1, v1, p2, v2, rs_in, r1, residual, other, factor,
    total, places, values, rs, sems,
):
    pairs = near_pairs(places_in, p1, v1, p2, v2, places, values)
    copies = started([*pairs, (before, total), (rs_in, rs)], sems)
    if last:
        copies += started(((r1, residual),), sems, 7)
    wait(copies)
    near_products((-2, 2), near_list, coordinates(places[0]), places, values, total)
    ridge, centre, first, second = chebyshev(ridge[0])
    d1 = rs[...] / centre
    if last:
        d2 = first[0] * d1 + first[1] * residual[...]
        left = residual[...] - (ridge * d2 + total[...])
        other[...] = d1 + d2 + (second[0] * d2 + second[1] * left)
        factor[...] = jnp.broadcast_to(second[1], factor.shape)
    else:
        left = rs[...] - (ridge * d1 + total[...])
        other[...] = first[0] * d1 + first[1] * left
        factor[...] = jnp.broadcast_to(first[1], factor.shape)
    residual[...] = left


def mark_kernel(_, mark):
    mark[...] = jnp.zeros_like(mark)


def prepare_kernel(far_clusters, _, picks):
    rows = COLS * CPG
    row = lax.broadcasted_iota(jnp.int32, (rows, N_GRP * rows), 0)
    lane = lax.broadcasted_iota(jnp.int32, (rows, N_GRP * rows), 1)
    column, cluster = row // CPG, row % CPG
    for k in range(FAR2):
        target = CPG * column
        for c in range(CPG):
            f = far_clusters[c, k]
            target += jnp.where(cluster == c, rows * (f // CPG) + f % CPG, 0)
        picks[rows * k : rows * (k + 1)] = jnp.where(lane == target, 1.0, 0.0).astype(BF16)


def from_behind(shard, by):
    pairs = [(i, i + by) for i in range(N_DEV) if 0 <= i + by < N_DEV]
    return lax.ppermute(shard, "dev", pairs)


def passed_on(pair, after):
    behind, ahead, _ = lax.optimization_barrier((*pair, after))
    return from_behind(behind, 1), from_behind(ahead, -1)


def exchanged(blocks, axis):
    return lax.all_to_all(blocks, axis, split_axis=0, concat_axis=0, tiled=True)


def body(
    coords,
    right_side,
    leaf_perm,
    near_list,
    far_leaves,
    couplings,
    transfer,
    leaf_basis,
    cluster_of,
    far_clusters,
    cluster_couplings,
    ridge_weight,
):
    ridge = ridge_weight.reshape(1)
    field, dma = (LEAF, OUT), pltpu.SemaphoreType.DMA
    payload, partner = (N_DEV, COLS, (FAR1 + 1) * RANK), (N_DEV, COLS, FAR1 * RANK)
    wide = pltpu.VMEM(payload, F32)
    rows16 = pltpu.VMEM((N_DEV * 16, RANK), F32)
    rows8 = pltpu.VMEM((N_DEV * 8, RANK), F32)
    narrow = pltpu.VMEM((COLS * CPG, RANK), F32)

    wc, sent, basis = call(
        start_kernel,
        "start",
        [
            ((LEAF + 4 * DIM, OUT), BF16, HBM),
            ((N_DEV, 16, RANK), BF16, HBM),
            ((LEAF, RANK), BF16, VMEM),
        ],
        [SMEM] * 2 + [HBM] * 6,
        (ridge, cluster_of, far_leaves, right_side, coords.T, leaf_perm, leaf_basis, transfer),
        [
            pltpu.SMEM((1, FAR1), jnp.int32),
            pltpu.VMEM(field, F32),
            pltpu.VMEM((DIM, LEAF), F32),
            pltpu.VMEM((1, LEAF), jnp.int32),
            pltpu.VMEM((LEAF, RANK), BF16),
            pltpu.VMEM((1, RANK, RANK), BF16),
            pltpu.VMEM((LEAF + 4 * DIM, OUT), BF16),
            pltpu.VMEM((N_DEV, 16, RANK), BF16),
            rows16,
            dma((9,)),
        ],
        SHORT,
    )

    def near_1(own, first, fields, after):
        (near,) = call(
            near_1_kernel,
            "near_1",
            [(field, F32, VMEM)],
            [SMEM, HBM] + [ANY] * 6,
            (near_list, wc, own, first[0], fields[0], first[1], fields[1], after),
            [pltpu.VMEM((3, 4 * DIM, OUT), BF16), pltpu.VMEM((3, *field), BF16), dma((6,))],
            MID,
        )
        return near

    def near_2(last, near, first, fields, r1):
        return call(
            lambda *refs: near_2_kernel(last, *refs),
            "near_2",
            [(field, F32, VMEM), (field, F32, VMEM), ((8, RANK), F32, VMEM)],
            [SMEM, SMEM, HBM] + [ANY] * 5 + [HBM, ANY],
            (ridge, near_list, wc, near, first[0], fields[0], first[1], fields[1], right_side, r1),
            [
                pltpu.VMEM(field, F32),
                pltpu.VMEM((3, 4 * DIM, OUT), BF16),
                pltpu.VMEM((2, *field), BF16),
                pltpu.VMEM(field, F32),
                dma((8,)),
            ],
            LONG,
        )

    def marked(shard):
        (mark,) = call(mark_kernel, "mark", [((8, RANK), F32, VMEM)], [ANY], (shard,), flops=SHORT)
        return mark

    def through_owners(sums, skeletons):
        all_sums = exchanged(sums, "grp")
        partners, done = call(
            partners_kernel,
            "partners",
            [(payload, BF16, HBM), ((8, RANK), F32, VMEM)],
            [VMEM] * 2,
            (skeletons, told),
            [pltpu.VMEM(partner, F32), pltpu.VMEM(partner, BF16), dma((1,))],
            SHORT,
        )
        (sent,) = call(
            couple_kernel,
            "couple",
            [(payload, BF16, HBM)],
            [VMEM] * 4 + [HBM],
            (picks, all_sums, cluster_couplings, told, partners),
            [pltpu.VMEM((N_DEV, COLS, RANK), F32), pltpu.VMEM((N_DEV, COLS, RANK), BF16), dma((1,))],
            SHORT,
            {4: 0},
        )
        return sent, exchanged(sent, "dev"), done

    arrived = exchanged(sent, "dev")
    (picks,) = call(
        prepare_kernel,
        "prepare",
        [((FAR2 * COLS * CPG, N_GRP * COLS * CPG), BF16, VMEM)],
        [SMEM, ANY],
        (far_clusters, wc),
        flops=SHORT,
    )
    first1 = passed_on((wc, wc), picks)
    sums, told, skeletons = call(
        sums_first_kernel,
        "sums_first",
        [((N_GRP, 16, RANK), BF16, VMEM), ((N_DEV, RANK), F32, VMEM), ((N_DEV, COLS * RANK), BF16, VMEM)],
        [VMEM, ANY],
        (arrived, picks),
        [rows16, narrow],
        SHORT,
    )
    sent, arrived, done = through_owners(sums, skeletons)
    first2 = passed_on(first1, done)
    near = near_1(wc, first1, first1, sent)
    residual, direction, factor = near_2(False, near, first2, first2, near)
    w, sent, r1 = call(
        middle_kernel,
        "middle",
        [(field, BF16, VMEM), ((N_DEV, 8, RANK), BF16, HBM), (field, F32, VMEM)],
        [VMEM] * 7,
        (arrived, couplings, transfer, basis, residual, direction, factor),
        [pltpu.VMEM((N_DEV, 8, RANK), BF16), wide, rows8, dma((1,))],
        SHORT,
    )
    arrived = exchanged(sent, "dev")
    mark = marked(w)
    fields1 = passed_on((w, w), mark)
    sums, skeletons = call(
        sums_kernel,
        "sums",
        [((N_GRP, 16, RANK), BF16, VMEM), ((N_DEV, COLS * RANK), BF16, VMEM)],
        [VMEM, VMEM, ANY],
        (arrived, told, mark),
        [rows8, narrow],
        SHORT,
    )
    sent, arrived, done = through_owners(sums, skeletons)
    fields2 = passed_on(fields1, done)
    near = near_1(w, first1, fields1, sent)
    residual, total, factor = near_2(True, near, first2, fields2, r1)
    return tuple(
        call(
            end_kernel,
            "end",
            [(field, F32, HBM), (field, F32, HBM)],
            [VMEM] * 7,
            (arrived, couplings, transfer, basis, residual, total, factor),
            [pltpu.VMEM(field, F32)] * 2 + [wide, dma((8,))],
            SHORT,
        )
    )


def solution(mesh):
    placed = (
        P(("grp", "dev"), None),
        P(("grp", "dev"), None),
        P(("grp", "dev"), None),
        P(("grp", "dev"), None),
        P(("grp", "dev"), None),
        P(("grp", "dev"), None, None, None),
        P(("grp", "dev"), None, None),
        P(("grp", "dev"), None),
        P(("grp", "dev")),
        P("grp", None),
        P("grp", None, None, None),
        P(),
    )
    return jax.shard_map(
        body,
        mesh=mesh,
        in_specs=placed,
        out_specs=(P(("grp", "dev"), None), P(("grp", "dev"), None)),
        check_vma=False,
    )
```

```python
import jax
import jax.numpy as jnp
from jax import lax
from jax.experimental import pallas as pl
from jax.experimental.pallas import tpu as pltpu
from jax.sharding import PartitionSpec as P

LEAF, DIM, OUT, RANK = 512, 64, 256, 128
N_GRP, N_DEV, CPG = 8, 64, 4
FAR1, FAR2 = 4, 4
COLS = OUT // N_DEV
NEAR = 4

KERNEL_LOG2 = -1.4426950408889634 / 32.0
GAP, TOP = 0.5, 8.0

F32, BF16 = jnp.float32, jnp.bfloat16
VMEM = pl.BlockSpec(memory_space=pltpu.VMEM)
SMEM = pl.BlockSpec(memory_space=pltpu.SMEM)
ANY = pl.BlockSpec(memory_space=pl.ANY)
HBM = pl.BlockSpec(memory_space=pltpu.HBM)
LIMIT = 32 * 2**20
SHORT, MID, LONG = 10**7, 10**10, 10**9
ROWS = 128


def dot(a, b, dims=((1,), (0,))):
    return lax.dot_general(a, b, (dims, ((), ())), preferred_element_type=F32)


def call(kernel, name, outs, ins, args, scratch=(), flops=0):
    shapes = [(pltpu.HBM if spec is HBM else jax.ShapeDtypeStruct)(shape, kind) for shape, kind, spec in outs]
    args = [
        pltpu.with_memory_space_constraint(arg, pltpu.HBM) if spec is HBM else arg for arg, spec in zip(args, ins)
    ]
    return pl.pallas_call(
        kernel,
        name=name,
        out_shape=shapes,
        in_specs=ins,
        out_specs=[spec for _, _, spec in outs],
        scratch_shapes=list(scratch),
        compiler_params=pltpu.CompilerParams(vmem_limit_bytes=LIMIT),
        cost_estimate=pl.CostEstimate(flops=flops, bytes_accessed=0, transcendentals=0),
    )(*args)


def started(pairs, sems, first=0):
    copies = [pltpu.make_async_copy(a, b, sems.at[first + i]) for i, (a, b) in enumerate(pairs)]
    for copy in copies:
        copy.start()
    return copies


def wait(copies):
    for copy in copies:
        copy.wait()


def chebyshev(ridge):
    ridge = jnp.full((1, 1), ridge, F32)
    bottom, top = ridge + GAP, ridge + TOP
    centre, spread = (top + bottom) / 2.0, (top - bottom) / 2.0
    sigma = centre / spread
    rho0 = 1.0 / sigma
    rho1 = 1.0 / (2.0 * sigma - rho0)
    rho2 = 1.0 / (2.0 * sigma - rho1)
    first = (rho1 * rho0, 2.0 * rho1 / spread)
    second = (rho2 * rho1, 2.0 * rho2 / spread)
    return ridge, centre, first, second


def to_owners(values, basis, transfer, staged, rows):
    skeleton = dot(values, basis, ((0,), (0,))).astype(BF16)
    uplift = dot(skeleton, transfer)
    skeleton = skeleton.astype(F32)
    for i in range(COLS):
        part = slice(N_DEV * i, N_DEV * (i + 1))
        staged[pl.ds(i, N_DEV, stride=rows), :] = skeleton[part]
        staged[pl.ds(COLS + i, N_DEV, stride=rows), :] = uplift[part]


def start_kernel(
    ridge, cluster, far_in, rs_in, coords_in, perm_in, basis_in, transfer_in, wc_out, sent_out, placed,
    far, rs, coords, perm, basis, transfer, wc, sent, staged, sems,
):
    copies = started(
        (
            (perm_in, perm), (basis_in, basis), (rs_in, rs), (coords_in, coords),
            (transfer_in, transfer), (far_in, far),
        ),
        sems,
    )
    staged[...] = jnp.zeros_like(staged)
    _, centre, _, _ = chebyshev(ridge[0])
    wait(copies[:2])
    point = lax.broadcasted_iota(jnp.int32, (LEAF, LEAF), 0)
    pick = jnp.where(point == perm[...], 1.0, 0.0).astype(BF16)
    basis_here = dot(pick, basis[...]).astype(BF16)
    placed[...] = basis_here
    wait(copies[2:4])
    values = (rs[...] / centre).astype(BF16)
    wc[:LEAF] = values
    high = coords[...].astype(BF16)
    low = (coords[...] - high.astype(F32)).astype(BF16)
    parts = jnp.concatenate([high, low], axis=0)
    wc[LEAF : LEAF + 2 * DIM] = parts[:, :OUT]
    wc[LEAF + 2 * DIM :] = parts[:, OUT:]
    outs = started(((wc, wc_out),), sems, 6)
    wait(copies[4:])
    to_owners(values, basis_here, transfer[0], staged, 16)
    lane = lax.broadcasted_iota(jnp.int32, (N_DEV, RANK), 1)
    told = jnp.where(lane == FAR1, (cluster[0] % CPG).astype(F32), 0.0)
    for k in range(FAR1):
        told = jnp.where(lane == k, (far[0, k] % N_DEV).astype(F32), told)
    staged[pl.ds(8, N_DEV, stride=16), :] = told
    sent[...] = staged[...].astype(BF16).reshape(N_DEV, 16, RANK)
    outs += started(((sent, sent_out),), sems, 8)
    wait(outs)


def owner_sums(staged, rows, told, sums, narrow):
    lane = lax.broadcasted_iota(jnp.int32, (N_DEV, RANK), 1).astype(F32)
    member = jnp.where(lane == told[:, FAR1 : FAR1 + 1], 1.0, 0.0).astype(BF16)
    uplifts = jnp.concatenate(
        [staged[pl.ds(COLS + i, N_DEV, stride=rows), :] for i in range(COLS)], axis=1
    ).astype(BF16)
    total = dot(member, uplifts, ((0,), (0,)))
    for i in range(COLS):
        narrow[pl.ds(CPG * i, CPG), :] = total[:CPG, RANK * i : RANK * (i + 1)]
    out = narrow[...].astype(BF16)
    for g in range(N_GRP):
        sums[g] = out


def sums_first_kernel(arrived, _, sums, told, skeletons, staged, narrow):
    staged[...] = arrived[...].astype(F32).reshape(N_DEV * 16, RANK)
    told[...] = staged[pl.ds(8, N_DEV, stride=16), :]
    owner_sums(staged, 16, told[...], sums, narrow)
    skeletons[...] = jnp.concatenate(
        [staged[pl.ds(i, N_DEV, stride=16), :] for i in range(COLS)], axis=1
    ).astype(BF16)


def sums_kernel(arrived, told, _, sums, skeletons, staged, narrow):
    staged[...] = arrived[...].astype(F32).reshape(N_DEV * 8, RANK)
    owner_sums(staged, 8, told[...], sums, narrow)
    skeletons[...] = jnp.concatenate(
        [staged[pl.ds(i, N_DEV, stride=8), :] for i in range(COLS)], axis=1
    ).astype(BF16)


def partners_kernel(skeletons, told, sent, staged):
    lane = lax.broadcasted_iota(jnp.int32, (N_DEV, N_DEV), 1).astype(F32)
    pick = jnp.concatenate(
        [jnp.where(lane == told[:, k : k + 1], 1.0, 0.0) for k in range(FAR1)], axis=0
    ).astype(BF16)
    picked = dot(pick, skeletons[...])
    for k in range(FAR1):
        for i in range(COLS):
            staged[:, i, RANK * k : RANK * (k + 1)] = picked[
                N_DEV * k : N_DEV * (k + 1), RANK * i : RANK * (i + 1)
            ]
    sent[...] = staged[...].astype(BF16)


def couple_kernel(picks, all_sums, blocks, told, partners, sent_out, staged, sent, sems):
    copies = started(((partners, sent_out.at[:, :, pl.ds(0, FAR1 * RANK)]),), sems)
    rows = COLS * CPG
    picked = dot(picks[...], all_sums[...].reshape(N_GRP * rows, RANK)).astype(BF16)
    total = jnp.zeros((CPG * RANK, rows), F32)
    for k in range(FAR2):
        block = blocks[:, k].reshape(CPG * RANK, RANK)
        total += dot(block, picked[rows * k : rows * (k + 1)], ((1,), (1,)))
    own = lax.broadcasted_iota(jnp.int32, (RANK, rows), 1) % CPG
    coupled = jnp.zeros((RANK, rows), F32)
    for c in range(CPG):
        coupled += jnp.where(own == c, total[RANK * c : RANK * (c + 1)], 0.0)
    coupled = coupled.T.astype(BF16)
    lane = lax.broadcasted_iota(jnp.int32, (N_DEV, rows), 1).astype(F32)
    pick = jnp.concatenate(
        [jnp.where(lane == told[:, FAR1 : FAR1 + 1] + CPG * i, 1.0, 0.0) for i in range(COLS)], axis=0
    ).astype(BF16)
    out = dot(pick, coupled)
    for i in range(COLS):
        staged[:, i, :] = out[N_DEV * i : N_DEV * (i + 1)]
    sent[...] = staged[...].astype(BF16)
    wait(copies + started(((sent, sent_out.at[:, :, pl.ds(FAR1 * RANK, RANK)]),), sems, 1))


def local_field(arrived, couplings, transfer, staged):
    staged[...] = arrived[...].astype(F32)
    local = jnp.zeros((OUT, RANK), F32)
    for k in range(FAR1 + 1):
        skeleton = jnp.concatenate(
            [staged[:, i, RANK * k : RANK * (k + 1)] for i in range(COLS)], axis=0
        ).astype(BF16)
        local += dot(skeleton, couplings[0, k] if k < FAR1 else transfer[0], ((1,), (1,)))
    return local.T.astype(BF16)


def middle_kernel(
    arrived, couplings, transfer, basis, residual, direction, factor, w, sent_out, r1, sent, staged, staged_out, sems
):
    local = local_field(arrived, couplings, transfer, staged)
    for r in range(0, LEAF, ROWS):
        part = slice(r, r + ROWS)
        far = dot(basis[part], local)
        r1[part] = residual[part] - far
        w[part] = (direction[part] - factor[:1, :1] * far).astype(BF16)
    to_owners(w[...], basis[...], transfer[0], staged_out, 8)
    sent[...] = staged_out[...].astype(BF16).reshape(N_DEV, 8, RANK)
    wait(started(((sent, sent_out),), sems))


def end_kernel(
    arrived, couplings, transfer, basis, before_r, before_s, factor, solution_out, residual_out,
    solution, residual, staged, sems,
):
    local = local_field(arrived, couplings, transfer, staged)
    outs = []
    for n, r in enumerate(range(0, LEAF, ROWS)):
        part = slice(r, r + ROWS)
        far = dot(basis[part], local)
        residual[part] = before_r[part] - far
        solution[part] = before_s[part] - factor[:1, :1] * far
        at = pl.ds(r, ROWS)
        outs += started(
            ((residual.at[at], residual_out.at[at]), (solution.at[at], solution_out.at[at])), sems, 2 * n
        )
    wait(outs)


def coordinates(held):
    parts = jnp.concatenate([held[: 2 * DIM], held[2 * DIM :]], axis=1)
    high, low = parts[:DIM], parts[DIM:]
    points = high.astype(F32) + low.astype(F32)
    return high, low, jnp.sum(points * points, axis=0, keepdims=True) * KERNEL_LOG2


def listed(near_list, offset):
    leaf = lax.axis_index("grp") * N_DEV + lax.axis_index("dev")
    hit = near_list[0, 0] == leaf + offset
    for k in range(1, NEAR):
        hit = hit | (near_list[0, k] == leaf + offset)
    return hit


def block_times(here, there, values, total, fresh):
    high, low, norm = here
    left = jnp.concatenate([high, high, low, low], axis=0)
    column = jnp.broadcast_to(norm, (RANK, LEAF)).T[:, :1]
    high, low, across = there
    right = jnp.concatenate([high, low, high, low], axis=0)
    step = 128
    for r in range(0, LEAF, step):
        part = slice(r, r + step)
        inner = dot(left[:, part], right, ((0,), (0,)))
        entries = jnp.exp2((column[part] + across) - (2.0 * KERNEL_LOG2) * inner).astype(BF16)
        product = dot(entries, values)
        total[part] = product if fresh else total[part] + product


def near_products(distance, near_list, mine, places, values, total):
    ahead = distance * (1 - 2 * (lax.axis_index("dev") % 2))
    for i, offset in enumerate((ahead, -ahead)):

        @pl.when(listed(near_list, offset))
        def _():
            block_times(mine, coordinates(places[1 + i]), values[i], total, False)


def near_pairs(places_in, p1, v1, p2, v2, places, values):
    pairs = [(p.at[pl.ds(LEAF, 4 * DIM)], places.at[i]) for i, p in enumerate((places_in, p1, p2))]
    return pairs + [(v.at[pl.ds(0, LEAF)], values.at[i]) for i, v in enumerate((v1, v2))]


def near_1_kernel(near_list, places_in, own, p1, v1, p2, v2, _, total, places, values, sems):
    pairs = near_pairs(places_in, p1, v1, p2, v2, places, values)
    wait(started([*pairs, (own.at[pl.ds(0, LEAF)], values.at[2])], sems))
    mine = coordinates(places[0])
    block_times(mine, mine, values[2], total, True)
    near_products(1, near_list, mine, places, values, total)


def near_2_kernel(
    last, ridge, near_list, places_in, before, p1, v1, p2, v2, rs_in, r1, residual, other, factor,
    total, places, values, rs, sems,
):
    pairs = near_pairs(places_in, p1, v1, p2, v2, places, values)
    copies = started([*pairs, (before, total), (rs_in, rs)], sems)
    if last:
        copies += started(((r1, residual),), sems, 7)
    wait(copies)
    near_products(2, near_list, coordinates(places[0]), places, values, total)
    ridge, centre, first, second = chebyshev(ridge[0])
    d1 = rs[...] / centre
    if last:
        d2 = first[0] * d1 + first[1] * residual[...]
        left = residual[...] - (ridge * d2 + total[...])
        other[...] = d1 + d2 + (second[0] * d2 + second[1] * left)
        factor[...] = jnp.broadcast_to(second[1], factor.shape)
    else:
        left = rs[...] - (ridge * d1 + total[...])
        other[...] = first[0] * d1 + first[1] * left
        factor[...] = jnp.broadcast_to(first[1], factor.shape)
    residual[...] = left


def mark_kernel(_, mark):
    mark[...] = jnp.zeros_like(mark)


def prepare_kernel(far_clusters, _, picks):
    rows = COLS * CPG
    row = lax.broadcasted_iota(jnp.int32, (rows, N_GRP * rows), 0)
    lane = lax.broadcasted_iota(jnp.int32, (rows, N_GRP * rows), 1)
    column, cluster = row // CPG, row % CPG
    for k in range(FAR2):
        target = CPG * column
        for c in range(CPG):
            f = far_clusters[c, k]
            target += jnp.where(cluster == c, rows * (f // CPG) + f % CPG, 0)
        picks[rows * k : rows * (k + 1)] = jnp.where(lane == target, 1.0, 0.0).astype(BF16)


def swapped(pair, after):
    one, two, _ = lax.optimization_barrier((*pair, after))
    inner = [(i, i ^ 1) for i in range(N_DEV)]
    outer = [(i, ((i + 1) ^ 1) - 1) for i in range(1, N_DEV - 1)]
    return lax.ppermute(one, "dev", inner), lax.ppermute(two, "dev", outer)


def exchanged(blocks, axis):
    return lax.all_to_all(blocks, axis, split_axis=0, concat_axis=0, tiled=True)


def body(
    coords,
    right_side,
    leaf_perm,
    near_list,
    far_leaves,
    couplings,
    transfer,
    leaf_basis,
    cluster_of,
    far_clusters,
    cluster_couplings,
    ridge_weight,
):
    ridge = ridge_weight.reshape(1)
    field, dma = (LEAF, OUT), pltpu.SemaphoreType.DMA
    payload, partner = (N_DEV, COLS, (FAR1 + 1) * RANK), (N_DEV, COLS, FAR1 * RANK)
    wide = pltpu.VMEM(payload, F32)
    rows16 = pltpu.VMEM((N_DEV * 16, RANK), F32)
    rows8 = pltpu.VMEM((N_DEV * 8, RANK), F32)
    narrow = pltpu.VMEM((COLS * CPG, RANK), F32)

    wc, sent, basis = call(
        start_kernel,
        "start",
        [
            ((LEAF + 4 * DIM, OUT), BF16, HBM),
            ((N_DEV, 16, RANK), BF16, HBM),
            ((LEAF, RANK), BF16, VMEM),
        ],
        [SMEM] * 2 + [HBM] * 6,
        (ridge, cluster_of, far_leaves, right_side, coords.T, leaf_perm, leaf_basis, transfer),
        [
            pltpu.SMEM((1, FAR1), jnp.int32),
            pltpu.VMEM(field, F32),
            pltpu.VMEM((DIM, LEAF), F32),
            pltpu.VMEM((1, LEAF), jnp.int32),
            pltpu.VMEM((LEAF, RANK), BF16),
            pltpu.VMEM((1, RANK, RANK), BF16),
            pltpu.VMEM((LEAF + 4 * DIM, OUT), BF16),
            pltpu.VMEM((N_DEV, 16, RANK), BF16),
            rows16,
            dma((9,)),
        ],
        SHORT,
    )

    def near_1(own, first, fields, after):
        (near,) = call(
            near_1_kernel,
            "near_1",
            [(field, F32, VMEM)],
            [SMEM, HBM] + [ANY] * 6,
            (near_list, wc, own, first[0], fields[0], first[1], fields[1], after),
            [pltpu.VMEM((3, 4 * DIM, OUT), BF16), pltpu.VMEM((3, *field), BF16), dma((6,))],
            MID,
        )
        return near

    def near_2(last, near, first, fields, r1):
        return call(
            lambda *refs: near_2_kernel(last, *refs),
            "near_2",
            [(field, F32, VMEM), (field, F32, VMEM), ((8, RANK), F32, VMEM)],
            [SMEM, SMEM, HBM] + [ANY] * 5 + [HBM, ANY],
            (ridge, near_list, wc, near, first[0], fields[0], first[1], fields[1], right_side, r1),
            [
                pltpu.VMEM(field, F32),
                pltpu.VMEM((3, 4 * DIM, OUT), BF16),
                pltpu.VMEM((2, *field), BF16),
                pltpu.VMEM(field, F32),
                dma((8,)),
            ],
            LONG,
        )

    def marked(shard):
        (mark,) = call(mark_kernel, "mark", [((8, RANK), F32, VMEM)], [ANY], (shard,), flops=SHORT)
        return mark

    def through_owners(sums, skeletons):
        all_sums = exchanged(sums, "grp")
        (partners,) = call(
            partners_kernel,
            "partners",
            [(partner, BF16, VMEM)],
            [VMEM] * 2,
            (skeletons, told),
            [pltpu.VMEM(partner, F32)],
            SHORT,
        )
        (sent,) = call(
            couple_kernel,
            "couple",
            [(payload, BF16, HBM)],
            [VMEM] * 5,
            (picks, all_sums, cluster_couplings, told, partners),
            [pltpu.VMEM((N_DEV, COLS, RANK), F32), pltpu.VMEM((N_DEV, COLS, RANK), BF16), dma((2,))],
            SHORT,
        )
        return sent, exchanged(sent, "dev")

    arrived = exchanged(sent, "dev")
    (picks,) = call(
        prepare_kernel,
        "prepare",
        [((FAR2 * COLS * CPG, N_GRP * COLS * CPG), BF16, VMEM)],
        [SMEM, ANY],
        (far_clusters, wc),
        flops=SHORT,
    )
    first1 = swapped((wc, wc), picks)
    sums, told, skeletons = call(
        sums_first_kernel,
        "sums_first",
        [((N_GRP, 16, RANK), BF16, VMEM), ((N_DEV, RANK), F32, VMEM), ((N_DEV, COLS * RANK), BF16, VMEM)],
        [VMEM, ANY],
        (arrived, picks),
        [rows16, narrow],
        SHORT,
    )
    sent, arrived = through_owners(sums, skeletons)
    first2 = swapped(first1[::-1], sums)
    near = near_1(wc, first1, first1, sent)
    residual, direction, factor = near_2(False, near, first2, first2, near)
    w, sent, r1 = call(
        middle_kernel,
        "middle",
        [(field, BF16, VMEM), ((N_DEV, 8, RANK), BF16, HBM), (field, F32, VMEM)],
        [VMEM] * 7,
        (arrived, couplings, transfer, basis, residual, direction, factor),
        [pltpu.VMEM((N_DEV, 8, RANK), BF16), wide, rows8, dma((1,))],
        SHORT,
    )
    arrived = exchanged(sent, "dev")
    mark = marked(w)
    fields1 = swapped((w, w), mark)
    sums, skeletons = call(
        sums_kernel,
        "sums",
        [((N_GRP, 16, RANK), BF16, VMEM), ((N_DEV, COLS * RANK), BF16, VMEM)],
        [VMEM, VMEM, ANY],
        (arrived, told, mark),
        [rows8, narrow],
        SHORT,
    )
    sent, arrived = through_owners(sums, skeletons)
    fields2 = swapped(fields1[::-1], sums)
    near = near_1(w, first1, fields1, sent)
    residual, total, factor = near_2(True, near, first2, fields2, r1)
    return tuple(
        call(
            end_kernel,
            "end",
            [(field, F32, HBM), (field, F32, HBM)],
            [VMEM] * 7,
            (arrived, couplings, transfer, basis, residual, total, factor),
            [pltpu.VMEM(field, F32)] * 2 + [wide, dma((8,))],
            SHORT,
        )
    )


def solution(mesh):
    placed = (
        P(("grp", "dev"), None),
        P(("grp", "dev"), None),
        P(("grp", "dev"), None),
        P(("grp", "dev"), None),
        P(("grp", "dev"), None),
        P(("grp", "dev"), None, None, None),
        P(("grp", "dev"), None, None),
        P(("grp", "dev"), None),
        P(("grp", "dev")),
        P("grp", None),
        P("grp", None, None, None),
        P(),
    )
    return jax.shard_map(
        body,
        mesh=mesh,
        in_specs=placed,
        out_specs=(P(("grp", "dev"), None), P(("grp", "dev"), None)),
        check_vma=False,
    )
```

```python
import jax
import jax.numpy as jnp
from jax import lax
from jax.experimental import pallas as pl
from jax.experimental.pallas import tpu as pltpu
from jax.sharding import PartitionSpec as P

LEAF, DIM, OUT, RANK = 512, 64, 256, 128
N_GRP, N_DEV, CPG = 8, 64, 4
FAR1, FAR2 = 4, 4
COLS = OUT // N_DEV
NEAR = 4

KERNEL_LOG2 = -1.4426950408889634 / 32.0
GAP, TOP = 0.5, 8.0

F32, BF16 = jnp.float32, jnp.bfloat16
VMEM = pl.BlockSpec(memory_space=pltpu.VMEM)
SMEM = pl.BlockSpec(memory_space=pltpu.SMEM)
ANY = pl.BlockSpec(memory_space=pl.ANY)
HBM = pl.BlockSpec(memory_space=pltpu.HBM)
LIMIT = 32 * 2**20
SHORT, MID, LONG = 10**7, 10**10, 10**9
ROWS = 128


def dot(a, b, dims=((1,), (0,))):
    return lax.dot_general(a, b, (dims, ((), ())), preferred_element_type=F32)


def call(kernel, name, outs, ins, args, scratch=(), flops=0):
    shapes = [(pltpu.HBM if spec is HBM else jax.ShapeDtypeStruct)(shape, kind) for shape, kind, spec in outs]
    args = [
        pltpu.with_memory_space_constraint(arg, pltpu.HBM) if spec is HBM else arg for arg, spec in zip(args, ins)
    ]
    return pl.pallas_call(
        kernel,
        name=name,
        out_shape=shapes,
        in_specs=ins,
        out_specs=[spec for _, _, spec in outs],
        scratch_shapes=list(scratch),
        compiler_params=pltpu.CompilerParams(vmem_limit_bytes=LIMIT),
        cost_estimate=pl.CostEstimate(flops=flops, bytes_accessed=0, transcendentals=0),
    )(*args)


def started(pairs, sems, first=0):
    copies = [pltpu.make_async_copy(a, b, sems.at[first + i]) for i, (a, b) in enumerate(pairs)]
    for copy in copies:
        copy.start()
    return copies


def wait(copies):
    for copy in copies:
        copy.wait()


def chebyshev(ridge):
    ridge = jnp.full((1, 1), ridge, F32)
    bottom, top = ridge + GAP, ridge + TOP
    centre, spread = (top + bottom) / 2.0, (top - bottom) / 2.0
    sigma = centre / spread
    rho0 = 1.0 / sigma
    rho1 = 1.0 / (2.0 * sigma - rho0)
    rho2 = 1.0 / (2.0 * sigma - rho1)
    first = (rho1 * rho0, 2.0 * rho1 / spread)
    second = (rho2 * rho1, 2.0 * rho2 / spread)
    return ridge, centre, first, second


def to_owners(values, basis, transfer, staged):
    skeleton = dot(values, basis, ((0,), (0,))).astype(BF16)
    uplift = dot(skeleton, transfer)
    skeleton = skeleton.astype(F32)
    for i in range(COLS):
        part = slice(N_DEV * i, N_DEV * (i + 1))
        staged[:, i, :RANK] = skeleton[part]
        staged[:, i, RANK : 2 * RANK] = uplift[part]


def start_kernel(
    ridge, cluster, far_in, rs_in, coords_in, perm_in, basis_in, transfer_in, wc_out, sent_out, placed,
    far, rs, coords, perm, basis, transfer, wc, sent, staged, sems,
):
    parts = [pl.ds(r, ROWS) for r in range(0, LEAF, ROWS)]
    copies = started(((perm_in, perm), (basis_in, basis)), sems)
    copies += started([(rs_in.at[part], rs.at[part]) for part in parts], sems, 2)
    copies += started(((transfer_in, transfer), (coords_in, coords), (far_in, far)), sems, 6)
    _, centre, _, _ = chebyshev(ridge[0])
    wait(copies[:2])
    point = lax.broadcasted_iota(jnp.int32, (LEAF, LEAF), 0)
    pick = jnp.where(point == perm[...], 1.0, 0.0).astype(BF16)
    basis_here = dot(pick, basis[...]).astype(BF16)
    placed[...] = basis_here
    wait(copies[2:6])
    values = (rs[...] / centre).astype(BF16)
    wc[:LEAF] = values
    outs = started(((wc.at[pl.ds(0, LEAF)], wc_out.at[pl.ds(0, LEAF)]),), sems, 9)
    wait(copies[6:])
    to_owners(values, basis_here, transfer[0], staged)
    lane = lax.broadcasted_iota(jnp.int32, (N_DEV, RANK), 1)
    told = jnp.where(lane == FAR1, (cluster[0] % CPG).astype(F32), 0.0)
    for k in range(FAR1):
        told = jnp.where(lane == k, (far[0, k] % N_DEV).astype(F32), told)
    for i in range(COLS):
        staged[:, i, 2 * RANK :] = told
    sent[...] = staged[...].astype(BF16)
    outs += started(((sent, sent_out),), sems, 10)
    high = coords[...].astype(BF16)
    low = (coords[...] - high.astype(F32)).astype(BF16)
    both = jnp.concatenate([high, low], axis=0)
    wc[LEAF : LEAF + 2 * DIM] = both[:, :OUT]
    wc[LEAF + 2 * DIM :] = both[:, OUT:]
    rest = pl.ds(LEAF, 4 * DIM)
    outs += started(((wc.at[rest], wc_out.at[rest]),), sems, 11)
    wait(outs)


def owner_sums(staged, told, sums_out, skeletons, narrow, sums, sems):
    lane = lax.broadcasted_iota(jnp.int32, (N_DEV, RANK), 1).astype(F32)
    member = jnp.where(lane == told[:, FAR1 : FAR1 + 1], 1.0, 0.0).astype(BF16)
    uplifts = jnp.concatenate([staged[:, i, RANK : 2 * RANK] for i in range(COLS)], axis=1).astype(BF16)
    total = dot(member, uplifts, ((0,), (0,)))
    for i in range(COLS):
        narrow[pl.ds(CPG * i, CPG), :] = total[:CPG, RANK * i : RANK * (i + 1)]
    out = narrow[...].astype(BF16)
    for g in range(N_GRP):
        sums[g] = out
    copies = started(((sums, sums_out),), sems)
    skeletons[...] = jnp.concatenate([staged[:, i, :RANK] for i in range(COLS)], axis=1).astype(BF16)
    wait(copies)


def sums_first_kernel(arrived, _, sums_out, told, skeletons, staged, narrow, sums, sems):
    staged[...] = arrived[...].astype(F32)
    told[...] = staged[:, 0, 2 * RANK :]
    owner_sums(staged, told[...], sums_out, skeletons, narrow, sums, sems)


def sums_kernel(arrived, told, _, sums_out, skeletons, staged, narrow, sums, sems):
    staged[...] = arrived[...].astype(F32)
    owner_sums(staged, told[...], sums_out, skeletons, narrow, sums, sems)


def partners_kernel(skeletons, told, sent, staged):
    lane = lax.broadcasted_iota(jnp.int32, (N_DEV, N_DEV), 1).astype(F32)
    pick = jnp.concatenate(
        [jnp.where(lane == told[:, k : k + 1], 1.0, 0.0) for k in range(FAR1)], axis=0
    ).astype(BF16)
    picked = dot(pick, skeletons[...])
    for k in range(FAR1):
        for i in range(COLS):
            staged[:, i, RANK * k : RANK * (k + 1)] = picked[
                N_DEV * k : N_DEV * (k + 1), RANK * i : RANK * (i + 1)
            ]
    sent[...] = staged[...].astype(BF16)


def couple_kernel(picks, all_sums, blocks, told, partners, sent_out, staged, sent, sems):
    copies = started(((partners, sent_out.at[:, :, pl.ds(0, FAR1 * RANK)]),), sems)
    rows = COLS * CPG
    picked = dot(picks[...], all_sums[...].reshape(N_GRP * rows, RANK)).astype(BF16)
    total = jnp.zeros((CPG * RANK, rows), F32)
    for k in range(FAR2):
        block = blocks[:, k].reshape(CPG * RANK, RANK)
        total += dot(block, picked[rows * k : rows * (k + 1)], ((1,), (1,)))
    own = lax.broadcasted_iota(jnp.int32, (RANK, rows), 1) % CPG
    coupled = jnp.zeros((RANK, rows), F32)
    for c in range(CPG):
        coupled += jnp.where(own == c, total[RANK * c : RANK * (c + 1)], 0.0)
    coupled = coupled.T.astype(BF16)
    lane = lax.broadcasted_iota(jnp.int32, (N_DEV, rows), 1).astype(F32)
    pick = jnp.concatenate(
        [jnp.where(lane == told[:, FAR1 : FAR1 + 1] + CPG * i, 1.0, 0.0) for i in range(COLS)], axis=0
    ).astype(BF16)
    out = dot(pick, coupled)
    for i in range(COLS):
        staged[:, i, :] = out[N_DEV * i : N_DEV * (i + 1)]
    sent[...] = staged[...].astype(BF16)
    wait(copies + started(((sent, sent_out.at[:, :, pl.ds(FAR1 * RANK, RANK)]),), sems, 1))


def local_field(arrived, couplings, transfer, staged):
    staged[...] = arrived[...].astype(F32)
    local = jnp.zeros((OUT, RANK), F32)
    for k in range(FAR1 + 1):
        skeleton = jnp.concatenate(
            [staged[:, i, RANK * k : RANK * (k + 1)] for i in range(COLS)], axis=0
        ).astype(BF16)
        local += dot(skeleton, couplings[0, k] if k < FAR1 else transfer[0], ((1,), (1,)))
    return local.T.astype(BF16)


def middle_kernel(
    arrived, couplings, transfer, basis, residual, direction, factor, w, sent_out, r1, sent, staged, staged_out, sems
):
    local = local_field(arrived, couplings, transfer, staged)
    for r in range(0, LEAF, ROWS):
        part = slice(r, r + ROWS)
        far = dot(basis[part], local)
        r1[part] = residual[part] - far
        w[part] = (direction[part] - factor[:1, :1] * far).astype(BF16)
    to_owners(w[...], basis[...], transfer[0], staged_out)
    sent[...] = staged_out[...].astype(BF16)
    wait(started(((sent, sent_out),), sems))


def end_kernel(
    arrived, couplings, transfer, basis, before_r, before_s, factor, solution_out, residual_out,
    solution, residual, staged, sems,
):
    local = local_field(arrived, couplings, transfer, staged)
    outs = []
    for n, r in enumerate(range(0, LEAF, ROWS)):
        part = slice(r, r + ROWS)
        far = dot(basis[part], local)
        residual[part] = before_r[part] - far
        solution[part] = before_s[part] - factor[:1, :1] * far
        at = pl.ds(r, ROWS)
        outs += started(
            ((residual.at[at], residual_out.at[at]), (solution.at[at], solution_out.at[at])), sems, 2 * n
        )
    wait(outs)


def coordinates(held):
    parts = jnp.concatenate([held[: 2 * DIM], held[2 * DIM :]], axis=1)
    high, low = parts[:DIM], parts[DIM:]
    points = high.astype(F32) + low.astype(F32)
    return high, low, jnp.sum(points * points, axis=0, keepdims=True) * KERNEL_LOG2


def listed(near_list, offset):
    leaf = lax.axis_index("grp") * N_DEV + lax.axis_index("dev")
    hit = near_list[0, 0] == leaf + offset
    for k in range(1, NEAR):
        hit = hit | (near_list[0, k] == leaf + offset)
    return hit


def block_times(here, there, values, total, fresh):
    high, low, norm = here
    left = jnp.concatenate([high, high, low, low], axis=0)
    column = jnp.broadcast_to(norm, (RANK, LEAF)).T[:, :1]
    high, low, across = there
    right = jnp.concatenate([high, low, high, low], axis=0)
    step = 128
    for r in range(0, LEAF, step):
        part = slice(r, r + step)
        inner = dot(left[:, part], right, ((0,), (0,)))
        entries = jnp.exp2((column[part] + across) - (2.0 * KERNEL_LOG2) * inner).astype(BF16)
        product = dot(entries, values)
        total[part] = product if fresh else total[part] + product


def near_products(distance, near_list, mine, places, values, total):
    ahead = distance * (1 - 2 * (lax.axis_index("dev") % 2))
    for i, offset in enumerate((ahead, -ahead)):

        @pl.when(listed(near_list, offset))
        def _():
            block_times(mine, coordinates(places[1 + i]), values[i], total, False)


def near_pairs(places_in, p1, v1, p2, v2, places, values):
    pairs = [(p.at[pl.ds(LEAF, 4 * DIM)], places.at[i]) for i, p in enumerate((places_in, p1, p2))]
    return pairs + [(v.at[pl.ds(0, LEAF)], values.at[i]) for i, v in enumerate((v1, v2))]


def near_1_kernel(near_list, places_in, own, p1, v1, p2, v2, _, total, places, values, sems):
    pairs = near_pairs(places_in, p1, v1, p2, v2, places, values)
    wait(started([*pairs, (own.at[pl.ds(0, LEAF)], values.at[2])], sems))
    mine = coordinates(places[0])
    block_times(mine, mine, values[2], total, True)
    near_products(1, near_list, mine, places, values, total)


def near_2_kernel(
    last, ridge, near_list, places_in, before, p1, v1, p2, v2, rs_in, r1, residual, other, factor,
    total, places, values, rs, sems,
):
    pairs = near_pairs(places_in, p1, v1, p2, v2, places, values)
    copies = started([*pairs, (before, total), (rs_in, rs)], sems)
    if last:
        copies += started(((r1, residual),), sems, 7)
    wait(copies)
    near_products(2, near_list, coordinates(places[0]), places, values, total)
    ridge, centre, first, second = chebyshev(ridge[0])
    d1 = rs[...] / centre
    if last:
        d2 = first[0] * d1 + first[1] * residual[...]
        left = residual[...] - (ridge * d2 + total[...])
        other[...] = d1 + d2 + (second[0] * d2 + second[1] * left)
        factor[...] = jnp.broadcast_to(second[1], factor.shape)
    else:
        left = rs[...] - (ridge * d1 + total[...])
        other[...] = first[0] * d1 + first[1] * left
        factor[...] = jnp.broadcast_to(first[1], factor.shape)
    residual[...] = left


def mark_kernel(_, mark):
    mark[...] = jnp.zeros_like(mark)


def prepare_kernel(far_clusters, _, picks):
    rows = COLS * CPG
    row = lax.broadcasted_iota(jnp.int32, (rows, N_GRP * rows), 0)
    lane = lax.broadcasted_iota(jnp.int32, (rows, N_GRP * rows), 1)
    column, cluster = row // CPG, row % CPG
    for k in range(FAR2):
        target = CPG * column
        for c in range(CPG):
            f = far_clusters[c, k]
            target += jnp.where(cluster == c, rows * (f // CPG) + f % CPG, 0)
        picks[rows * k : rows * (k + 1)] = jnp.where(lane == target, 1.0, 0.0).astype(BF16)


def swapped(pair, after):
    one, two, _ = lax.optimization_barrier((*pair, after))
    inner = [(i, i ^ 1) for i in range(N_DEV)]
    outer = [(i, ((i + 1) ^ 1) - 1) for i in range(1, N_DEV - 1)]
    return lax.ppermute(one, "dev", inner), lax.ppermute(two, "dev", outer)


def exchanged(blocks, axis):
    return lax.all_to_all(blocks, axis, split_axis=0, concat_axis=0, tiled=True)


def body(
    coords,
    right_side,
    leaf_perm,
    near_list,
    far_leaves,
    couplings,
    transfer,
    leaf_basis,
    cluster_of,
    far_clusters,
    cluster_couplings,
    ridge_weight,
):
    ridge = ridge_weight.reshape(1)
    field, dma = (LEAF, OUT), pltpu.SemaphoreType.DMA
    payload, partner = (N_DEV, COLS, (FAR1 + 1) * RANK), (N_DEV, COLS, FAR1 * RANK)
    wide = pltpu.VMEM(payload, F32)
    told_too, upward = (N_DEV, COLS, 3 * RANK), (N_DEV, COLS, 2 * RANK)
    sums_shape = (N_GRP, COLS * CPG, RANK)
    narrow = [pltpu.VMEM((COLS * CPG, RANK), F32), pltpu.VMEM(sums_shape, BF16), dma((1,))]

    wc, sent, basis = call(
        start_kernel,
        "start",
        [
            ((LEAF + 4 * DIM, OUT), BF16, HBM),
            (told_too, BF16, HBM),
            ((LEAF, RANK), BF16, VMEM),
        ],
        [SMEM] * 2 + [HBM] * 6,
        (ridge, cluster_of, far_leaves, right_side, coords.T, leaf_perm, leaf_basis, transfer),
        [
            pltpu.SMEM((1, FAR1), jnp.int32),
            pltpu.VMEM(field, F32),
            pltpu.VMEM((DIM, LEAF), F32),
            pltpu.VMEM((1, LEAF), jnp.int32),
            pltpu.VMEM((LEAF, RANK), BF16),
            pltpu.VMEM((1, RANK, RANK), BF16),
            pltpu.VMEM((LEAF + 4 * DIM, OUT), BF16),
            pltpu.VMEM(told_too, BF16),
            pltpu.VMEM(told_too, F32),
            dma((12,)),
        ],
        SHORT,
    )

    def near_1(own, first, fields, after):
        (near,) = call(
            near_1_kernel,
            "near_1",
            [(field, F32, VMEM)],
            [SMEM, HBM] + [ANY] * 5 + [HBM],
            (near_list, wc, own, first[0], fields[0], first[1], fields[1], after),
            [pltpu.VMEM((3, 4 * DIM, OUT), BF16), pltpu.VMEM((3, *field), BF16), dma((6,))],
            MID,
        )
        return near

    def near_2(last, near, first, fields, r1):
        return call(
            lambda *refs: near_2_kernel(last, *refs),
            "near_2",
            [(field, F32, VMEM), (field, F32, VMEM), ((8, RANK), F32, VMEM)],
            [SMEM, SMEM, HBM] + [ANY] * 5 + [HBM, ANY],
            (ridge, near_list, wc, near, first[0], fields[0], first[1], fields[1], right_side, r1),
            [
                pltpu.VMEM(field, F32),
                pltpu.VMEM((3, 4 * DIM, OUT), BF16),
                pltpu.VMEM((2, *field), BF16),
                pltpu.VMEM(field, F32),
                dma((8,)),
            ],
            LONG,
        )

    def marked(shard):
        (mark,) = call(mark_kernel, "mark", [((8, RANK), F32, VMEM)], [ANY], (shard,), flops=SHORT)
        return mark

    def through_owners(sums, skeletons):
        all_sums = exchanged(sums, "grp")
        (partners,) = call(
            partners_kernel,
            "partners",
            [(partner, BF16, VMEM)],
            [VMEM] * 2,
            (skeletons, told),
            [pltpu.VMEM(partner, F32)],
            SHORT,
        )
        (sent,) = call(
            couple_kernel,
            "couple",
            [(payload, BF16, HBM)],
            [VMEM] * 5,
            (picks, all_sums, cluster_couplings, told, partners),
            [pltpu.VMEM((N_DEV, COLS, RANK), F32), pltpu.VMEM((N_DEV, COLS, RANK), BF16), dma((2,))],
            SHORT,
        )
        return sent, exchanged(sent, "dev")

    arrived = exchanged(sent, "dev")
    (picks,) = call(
        prepare_kernel,
        "prepare",
        [((FAR2 * COLS * CPG, N_GRP * COLS * CPG), BF16, VMEM)],
        [SMEM, HBM],
        (far_clusters, wc),
        flops=SHORT,
    )
    first1 = swapped((wc, wc), picks)
    sums, told, skeletons = call(
        sums_first_kernel,
        "sums_first",
        [(sums_shape, BF16, HBM), ((N_DEV, RANK), F32, VMEM), ((N_DEV, COLS * RANK), BF16, VMEM)],
        [VMEM, ANY],
        (arrived, picks),
        [pltpu.VMEM(told_too, F32), *narrow],
        SHORT,
    )
    sent, arrived = through_owners(sums, skeletons)
    first2 = swapped(first1[::-1], sums)
    near = near_1(wc, first1, first1, sent)
    residual, direction, factor = near_2(False, near, first2, first2, near)
    w, sent, r1 = call(
        middle_kernel,
        "middle",
        [(field, BF16, VMEM), (upward, BF16, HBM), (field, F32, VMEM)],
        [VMEM] * 7,
        (arrived, couplings, transfer, basis, residual, direction, factor),
        [pltpu.VMEM(upward, BF16), wide, pltpu.VMEM(upward, F32), dma((1,))],
        SHORT,
    )
    arrived = exchanged(sent, "dev")
    mark = marked(w)
    fields1 = swapped((w, w), mark)
    sums, skeletons = call(
        sums_kernel,
        "sums",
        [(sums_shape, BF16, HBM), ((N_DEV, COLS * RANK), BF16, VMEM)],
        [VMEM, VMEM, ANY],
        (arrived, told, mark),
        [pltpu.VMEM(upward, F32), *narrow],
        SHORT,
    )
    sent, arrived = through_owners(sums, skeletons)
    fields2 = swapped(fields1[::-1], sums)
    near = near_1(w, first1, fields1, sent)
    residual, total, factor = near_2(True, near, first2, fields2, r1)
    return tuple(
        call(
            end_kernel,
            "end",
            [(field, F32, HBM), (field, F32, HBM)],
            [VMEM] * 7,
            (arrived, couplings, transfer, basis, residual, total, factor),
            [pltpu.VMEM(field, F32)] * 2 + [wide, dma((8,))],
            SHORT,
        )
    )


def solution(mesh):
    placed = (
        P(("grp", "dev"), None),
        P(("grp", "dev"), None),
        P(("grp", "dev"), None),
        P(("grp", "dev"), None),
        P(("grp", "dev"), None),
        P(("grp", "dev"), None, None, None),
        P(("grp", "dev"), None, None),
        P(("grp", "dev"), None),
        P(("grp", "dev")),
        P("grp", None),
        P("grp", None, None, None),
        P(),
    )
    return jax.shard_map(
        body,
        mesh=mesh,
        in_specs=placed,
        out_specs=(P(("grp", "dev"), None), P(("grp", "dev"), None)),
        check_vma=False,
    )
```

```python
import jax
import jax.numpy as jnp
from jax import lax
from jax.experimental import pallas as pl
from jax.experimental.pallas import tpu as pltpu
from jax.sharding import PartitionSpec as P

LEAF, DIM, OUT, RANK = 512, 64, 256, 128
N_GRP, N_DEV, CPG = 8, 64, 4
FAR1, FAR2 = 4, 4
COLS = OUT // N_DEV
NEAR = 4

KERNEL_LOG2 = -1.4426950408889634 / 32.0
GAP, TOP = 0.5, 8.0

F32, BF16 = jnp.float32, jnp.bfloat16
VMEM = pl.BlockSpec(memory_space=pltpu.VMEM)
SMEM = pl.BlockSpec(memory_space=pltpu.SMEM)
ANY = pl.BlockSpec(memory_space=pl.ANY)
HBM = pl.BlockSpec(memory_space=pltpu.HBM)
LIMIT = 32 * 2**20
SHORT, MID, LONG = 10**7, 10**9, 10**10
ROWS = 128


def dot(a, b, dims=((1,), (0,))):
    return lax.dot_general(a, b, (dims, ((), ())), preferred_element_type=F32)


def call(kernel, name, outs, ins, args, scratch=(), flops=0):
    shapes = [(pltpu.HBM if spec is HBM else jax.ShapeDtypeStruct)(shape, kind) for shape, kind, spec in outs]
    args = [
        pltpu.with_memory_space_constraint(arg, pltpu.HBM) if spec is HBM else arg for arg, spec in zip(args, ins)
    ]
    return pl.pallas_call(
        kernel,
        name=name,
        out_shape=shapes,
        in_specs=ins,
        out_specs=[spec for _, _, spec in outs],
        scratch_shapes=list(scratch),
        compiler_params=pltpu.CompilerParams(vmem_limit_bytes=LIMIT),
        cost_estimate=pl.CostEstimate(flops=flops, bytes_accessed=0, transcendentals=0),
    )(*args)


def started(pairs, sems, first=0):
    copies = [pltpu.make_async_copy(a, b, sems.at[first + i]) for i, (a, b) in enumerate(pairs)]
    for copy in copies:
        copy.start()
    return copies


def wait(copies):
    for copy in copies:
        copy.wait()


def chebyshev(ridge):
    ridge = jnp.full((1, 1), ridge, F32)
    bottom, top = ridge + GAP, ridge + TOP
    centre, spread = (top + bottom) / 2.0, (top - bottom) / 2.0
    sigma = centre / spread
    rho0 = 1.0 / sigma
    rho1 = 1.0 / (2.0 * sigma - rho0)
    rho2 = 1.0 / (2.0 * sigma - rho1)
    first = (rho1 * rho0, 2.0 * rho1 / spread)
    second = (rho2 * rho1, 2.0 * rho2 / spread)
    return ridge, centre, first, second


def to_owners(values, basis, transfer, staged):
    skeleton = dot(values, basis, ((0,), (0,))).astype(BF16)
    uplift = dot(skeleton, transfer)
    skeleton = skeleton.astype(F32)
    for i in range(COLS):
        part = slice(N_DEV * i, N_DEV * (i + 1))
        staged[:, i, :RANK] = skeleton[part]
        staged[:, i, RANK : 2 * RANK] = uplift[part]


def start_kernel(
    ridge, cluster, far_in, rs_in, coords_in, perm_in, basis_in, transfer_in, wc_out, sent_out, placed,
    far, rs, coords, perm, basis, transfer, wc, sent, staged, sems,
):
    copies = started(
        (
            (perm_in, perm), (basis_in, basis), (rs_in, rs), (transfer_in, transfer),
            (coords_in, coords), (far_in, far),
        ),
        sems,
    )
    _, centre, _, _ = chebyshev(ridge[0])
    wait(copies[:2])
    point = lax.broadcasted_iota(jnp.int32, (LEAF, LEAF), 0)
    pick = jnp.where(point == perm[...], 1.0, 0.0).astype(BF16)
    basis_here = dot(pick, basis[...]).astype(BF16)
    placed[...] = basis_here
    wait(copies[2:3])
    values = (rs[...] / centre).astype(BF16)
    wc[:LEAF] = values
    outs = started(((wc.at[pl.ds(0, LEAF)], wc_out.at[pl.ds(0, LEAF)]),), sems, 6)
    wait(copies[3:])
    to_owners(values, basis_here, transfer[0], staged)
    lane = lax.broadcasted_iota(jnp.int32, (N_DEV, RANK), 1)
    told = jnp.where(lane == FAR1, (cluster[0] % CPG).astype(F32), 0.0)
    for k in range(FAR1):
        told = jnp.where(lane == k, (far[0, k] % N_DEV).astype(F32), told)
    for i in range(COLS):
        staged[:, i, 2 * RANK :] = told
    sent[...] = staged[...].astype(BF16)
    outs += started(((sent, sent_out),), sems, 7)
    high = coords[...].astype(BF16)
    low = (coords[...] - high.astype(F32)).astype(BF16)
    both = jnp.concatenate([high, low], axis=0)
    wc[LEAF : LEAF + 2 * DIM] = both[:, :OUT]
    wc[LEAF + 2 * DIM :] = both[:, OUT:]
    rest = pl.ds(LEAF, 4 * DIM)
    outs += started(((wc.at[rest], wc_out.at[rest]),), sems, 8)
    wait(outs)


def owner_sums(staged, told, sums_out, skeletons, narrow, sums, sems):
    lane = lax.broadcasted_iota(jnp.int32, (N_DEV, RANK), 1).astype(F32)
    member = jnp.where(lane == told[:, FAR1 : FAR1 + 1], 1.0, 0.0).astype(BF16)
    uplifts = jnp.concatenate([staged[:, i, RANK : 2 * RANK] for i in range(COLS)], axis=1).astype(BF16)
    total = dot(member, uplifts, ((0,), (0,)))
    for i in range(COLS):
        narrow[pl.ds(CPG * i, CPG), :] = total[:CPG, RANK * i : RANK * (i + 1)]
    out = narrow[...].astype(BF16)
    for g in range(N_GRP):
        sums[g] = out
    copies = started(((sums, sums_out),), sems)
    skeletons[...] = jnp.concatenate([staged[:, i, :RANK] for i in range(COLS)], axis=1).astype(BF16)
    wait(copies)


def sums_first_kernel(arrived, sums_out, told, skeletons, staged, narrow, sums, sems):
    staged[...] = arrived[...].astype(F32)
    told[...] = staged[:, 0, 2 * RANK :]
    owner_sums(staged, told[...], sums_out, skeletons, narrow, sums, sems)


def sums_kernel(arrived, told, sums_out, skeletons, staged, narrow, sums, sems):
    staged[...] = arrived[...].astype(F32)
    owner_sums(staged, told[...], sums_out, skeletons, narrow, sums, sems)


def partners_kernel(skeletons, told, sent, staged):
    lane = lax.broadcasted_iota(jnp.int32, (N_DEV, N_DEV), 1).astype(F32)
    pick = jnp.concatenate(
        [jnp.where(lane == told[:, k : k + 1], 1.0, 0.0) for k in range(FAR1)], axis=0
    ).astype(BF16)
    picked = dot(pick, skeletons[...])
    for k in range(FAR1):
        for i in range(COLS):
            staged[:, i, RANK * k : RANK * (k + 1)] = picked[
                N_DEV * k : N_DEV * (k + 1), RANK * i : RANK * (i + 1)
            ]
    sent[...] = staged[...].astype(BF16)


def couple_kernel(picks, all_sums, blocks, told, partners, sent_out, staged, sent, sems):
    copies = started(((partners, sent_out.at[:, :, pl.ds(0, FAR1 * RANK)]),), sems)
    rows = COLS * CPG
    picked = dot(picks[...], all_sums[...].reshape(N_GRP * rows, RANK)).astype(BF16)
    total = jnp.zeros((CPG * RANK, rows), F32)
    for k in range(FAR2):
        block = blocks[:, k].reshape(CPG * RANK, RANK)
        total += dot(block, picked[rows * k : rows * (k + 1)], ((1,), (1,)))
    own = lax.broadcasted_iota(jnp.int32, (RANK, rows), 1) % CPG
    coupled = jnp.zeros((RANK, rows), F32)
    for c in range(CPG):
        coupled += jnp.where(own == c, total[RANK * c : RANK * (c + 1)], 0.0)
    coupled = coupled.T.astype(BF16)
    lane = lax.broadcasted_iota(jnp.int32, (N_DEV, rows), 1).astype(F32)
    pick = jnp.concatenate(
        [jnp.where(lane == told[:, FAR1 : FAR1 + 1] + CPG * i, 1.0, 0.0) for i in range(COLS)], axis=0
    ).astype(BF16)
    out = dot(pick, coupled)
    for i in range(COLS):
        staged[:, i, :] = out[N_DEV * i : N_DEV * (i + 1)]
    sent[...] = staged[...].astype(BF16)
    wait(copies + started(((sent, sent_out.at[:, :, pl.ds(FAR1 * RANK, RANK)]),), sems, 1))


def local_field(arrived, couplings, transfer, staged):
    staged[...] = arrived[...].astype(F32)
    local = jnp.zeros((OUT, RANK), F32)
    for k in range(FAR1 + 1):
        skeleton = jnp.concatenate(
            [staged[:, i, RANK * k : RANK * (k + 1)] for i in range(COLS)], axis=0
        ).astype(BF16)
        local += dot(skeleton, couplings[0, k] if k < FAR1 else transfer[0], ((1,), (1,)))
    return local.T.astype(BF16)


def middle_kernel(
    arrived, couplings, transfer, basis, residual, direction, factor, w, sent_out, r1, sent, staged, staged_out, sems
):
    local = local_field(arrived, couplings, transfer, staged)
    for r in range(0, LEAF, ROWS):
        part = slice(r, r + ROWS)
        far = dot(basis[part], local)
        r1[part] = residual[part] - far
        w[part] = (direction[part] - factor[:1, :1] * far).astype(BF16)
    to_owners(w[...], basis[...], transfer[0], staged_out)
    sent[...] = staged_out[...].astype(BF16)
    wait(started(((sent, sent_out),), sems))


def end_kernel(
    arrived, couplings, transfer, basis, before_r, before_s, factor, solution_out, residual_out,
    solution, residual, staged, sems,
):
    local = local_field(arrived, couplings, transfer, staged)
    outs = []
    for n, r in enumerate(range(0, LEAF, ROWS)):
        part = slice(r, r + ROWS)
        far = dot(basis[part], local)
        residual[part] = before_r[part] - far
        solution[part] = before_s[part] - factor[:1, :1] * far
        at = pl.ds(r, ROWS)
        outs += started(
            ((residual.at[at], residual_out.at[at]), (solution.at[at], solution_out.at[at])), sems, 2 * n
        )
    wait(outs)


def coordinates(held):
    parts = jnp.concatenate([held[: 2 * DIM], held[2 * DIM :]], axis=1)
    high, low = parts[:DIM], parts[DIM:]
    points = high.astype(F32) + low.astype(F32)
    return high, low, jnp.sum(points * points, axis=0, keepdims=True) * KERNEL_LOG2


def listed(near_list, offset):
    leaf = lax.axis_index("grp") * N_DEV + lax.axis_index("dev")
    hit = near_list[0, 0] == leaf + offset
    for k in range(1, NEAR):
        hit = hit | (near_list[0, k] == leaf + offset)
    return hit


def block_times(here, there, values, total, fresh):
    high, low, norm = here
    left = jnp.concatenate([high, high, low, low], axis=0)
    column = jnp.broadcast_to(norm, (RANK, LEAF)).T[:, :1]
    high, low, across = there
    right = jnp.concatenate([high, low, high, low], axis=0)
    step = 128
    for r in range(0, LEAF, step):
        part = slice(r, r + step)
        inner = dot(left[:, part], right, ((0,), (0,)))
        entries = jnp.exp2((column[part] + across) - (2.0 * KERNEL_LOG2) * inner).astype(BF16)
        product = dot(entries, values)
        total[part] = product if fresh else total[part] + product


def near_products(distance, near_list, mine, places, values, total):
    ahead = distance * (1 - 2 * (lax.axis_index("dev") % 2))
    for i, offset in enumerate((ahead, -ahead)):

        @pl.when(listed(near_list, offset))
        def _():
            block_times(mine, coordinates(places[1 + i]), values[i], total, False)


def near_pairs(places_in, p1, v1, p2, v2, places, values):
    pairs = [(p.at[pl.ds(LEAF, 4 * DIM)], places.at[i]) for i, p in enumerate((places_in, p1, p2))]
    return pairs + [(v.at[pl.ds(0, LEAF)], values.at[i]) for i, v in enumerate((v1, v2))]


def near_1_kernel(near_list, places_in, own, p1, v1, p2, v2, _, total, places, values, sems):
    pairs = near_pairs(places_in, p1, v1, p2, v2, places, values)
    wait(started([*pairs, (own.at[pl.ds(0, LEAF)], values.at[2])], sems))
    mine = coordinates(places[0])
    block_times(mine, mine, values[2], total, True)
    near_products(1, near_list, mine, places, values, total)


def near_2_kernel(
    last, ridge, near_list, places_in, before, p1, v1, p2, v2, rs_in, r1, residual, other, factor,
    total, places, values, rs, sems,
):
    pairs = near_pairs(places_in, p1, v1, p2, v2, places, values)
    copies = started([*pairs, (before, total), (rs_in, rs)], sems)
    if last:
        copies += started(((r1, residual),), sems, 7)
    wait(copies)
    near_products(2, near_list, coordinates(places[0]), places, values, total)
    ridge, centre, first, second = chebyshev(ridge[0])
    d1 = rs[...] / centre
    if last:
        d2 = first[0] * d1 + first[1] * residual[...]
        left = residual[...] - (ridge * d2 + total[...])
        other[...] = d1 + d2 + (second[0] * d2 + second[1] * left)
        factor[...] = jnp.broadcast_to(second[1], factor.shape)
    else:
        left = rs[...] - (ridge * d1 + total[...])
        other[...] = first[0] * d1 + first[1] * left
        factor[...] = jnp.broadcast_to(first[1], factor.shape)
    residual[...] = left


def prepare_kernel(far_clusters, picks):
    rows = COLS * CPG
    row = lax.broadcasted_iota(jnp.int32, (rows, N_GRP * rows), 0)
    lane = lax.broadcasted_iota(jnp.int32, (rows, N_GRP * rows), 1)
    column, cluster = row // CPG, row % CPG
    for k in range(FAR2):
        target = CPG * column
        for c in range(CPG):
            f = far_clusters[c, k]
            target += jnp.where(cluster == c, rows * (f // CPG) + f % CPG, 0)
        picks[rows * k : rows * (k + 1)] = jnp.where(lane == target, 1.0, 0.0).astype(BF16)


def swapped(one, two):
    inner = [(i, i ^ 1) for i in range(N_DEV)]
    outer = [(i, ((i + 1) ^ 1) - 1) for i in range(1, N_DEV - 1)]
    return lax.ppermute(one, "dev", inner), lax.ppermute(two, "dev", outer)


def exchanged(blocks, axis):
    return lax.all_to_all(blocks, axis, split_axis=0, concat_axis=0, tiled=True)


def body(
    coords,
    right_side,
    leaf_perm,
    near_list,
    far_leaves,
    couplings,
    transfer,
    leaf_basis,
    cluster_of,
    far_clusters,
    cluster_couplings,
    ridge_weight,
):
    ridge = ridge_weight.reshape(1)
    field, dma = (LEAF, OUT), pltpu.SemaphoreType.DMA
    payload, partner = (N_DEV, COLS, (FAR1 + 1) * RANK), (N_DEV, COLS, FAR1 * RANK)
    wide = pltpu.VMEM(payload, F32)
    told_too, upward = (N_DEV, COLS, 3 * RANK), (N_DEV, COLS, 2 * RANK)
    sums_shape = (N_GRP, COLS * CPG, RANK)
    narrow = [pltpu.VMEM((COLS * CPG, RANK), F32), pltpu.VMEM(sums_shape, BF16), dma((1,))]

    wc, sent, basis = call(
        start_kernel,
        "start",
        [
            ((LEAF + 4 * DIM, OUT), BF16, HBM),
            (told_too, BF16, HBM),
            ((LEAF, RANK), BF16, VMEM),
        ],
        [SMEM] * 2 + [HBM] * 6,
        (ridge, cluster_of, far_leaves, right_side, coords.T, leaf_perm, leaf_basis, transfer),
        [
            pltpu.SMEM((1, FAR1), jnp.int32),
            pltpu.VMEM(field, F32),
            pltpu.VMEM((DIM, LEAF), F32),
            pltpu.VMEM((1, LEAF), jnp.int32),
            pltpu.VMEM((LEAF, RANK), BF16),
            pltpu.VMEM((1, RANK, RANK), BF16),
            pltpu.VMEM((LEAF + 4 * DIM, OUT), BF16),
            pltpu.VMEM(told_too, BF16),
            pltpu.VMEM(told_too, F32),
            dma((9,)),
        ],
        SHORT,
    )

    def near_1(own, first, fields, after):
        (near,) = call(
            near_1_kernel,
            "near_1",
            [(field, F32, VMEM)],
            [SMEM, HBM] + [ANY] * 5 + [HBM],
            (near_list, wc, own, first[0], fields[0], first[1], fields[1], after),
            [pltpu.VMEM((3, 4 * DIM, OUT), BF16), pltpu.VMEM((3, *field), BF16), dma((6,))],
            MID,
        )
        return near

    def near_2(last, near, first, fields, r1):
        return call(
            lambda *refs: near_2_kernel(last, *refs),
            "near_2",
            [(field, F32, VMEM), (field, F32, VMEM), ((8, RANK), F32, VMEM)],
            [SMEM, SMEM, HBM] + [ANY] * 5 + [HBM, ANY],
            (ridge, near_list, wc, near, first[0], fields[0], first[1], fields[1], right_side, r1),
            [
                pltpu.VMEM(field, F32),
                pltpu.VMEM((3, 4 * DIM, OUT), BF16),
                pltpu.VMEM((2, *field), BF16),
                pltpu.VMEM(field, F32),
                dma((8,)),
            ],
            LONG,
        )

    def through_owners(sums, skeletons):
        all_sums = exchanged(sums, "grp")
        (partners,) = call(
            partners_kernel,
            "partners",
            [(partner, BF16, VMEM)],
            [VMEM] * 2,
            (skeletons, told),
            [pltpu.VMEM(partner, F32)],
            SHORT,
        )
        (sent,) = call(
            couple_kernel,
            "couple",
            [(payload, BF16, HBM)],
            [VMEM] * 5,
            (picks, all_sums, cluster_couplings, told, partners),
            [pltpu.VMEM((N_DEV, COLS, RANK), F32), pltpu.VMEM((N_DEV, COLS, RANK), BF16), dma((2,))],
            SHORT,
        )
        return sent, exchanged(sent, "dev")

    arrived = exchanged(sent, "dev")
    (picks,) = call(
        prepare_kernel,
        "prepare",
        [((FAR2 * COLS * CPG, N_GRP * COLS * CPG), BF16, VMEM)],
        [SMEM],
        (far_clusters,),
        flops=SHORT,
    )
    first1 = swapped(wc, wc)
    sums, told, skeletons = call(
        sums_first_kernel,
        "sums_first",
        [(sums_shape, BF16, HBM), ((N_DEV, RANK), F32, VMEM), ((N_DEV, COLS * RANK), BF16, VMEM)],
        [VMEM],
        (arrived,),
        [pltpu.VMEM(told_too, F32), *narrow],
        SHORT,
    )
    sent, arrived = through_owners(sums, skeletons)
    first2 = swapped(*first1[::-1])
    near = near_1(wc, first1, first1, sent)
    residual, direction, factor = near_2(False, near, first2, first2, near)
    w, sent, r1 = call(
        middle_kernel,
        "middle",
        [(field, BF16, VMEM), (upward, BF16, HBM), (field, F32, VMEM)],
        [VMEM] * 7,
        (arrived, couplings, transfer, basis, residual, direction, factor),
        [pltpu.VMEM(upward, BF16), wide, pltpu.VMEM(upward, F32), dma((1,))],
        SHORT,
    )
    arrived = exchanged(sent, "dev")
    fields1 = swapped(w, w)
    sums, skeletons = call(
        sums_kernel,
        "sums",
        [(sums_shape, BF16, HBM), ((N_DEV, COLS * RANK), BF16, VMEM)],
        [VMEM, VMEM],
        (arrived, told),
        [pltpu.VMEM(upward, F32), *narrow],
        SHORT,
    )
    sent, arrived = through_owners(sums, skeletons)
    fields2 = swapped(*fields1[::-1])
    near = near_1(w, first1, fields1, sent)
    residual, total, factor = near_2(True, near, first2, fields2, r1)
    return tuple(
        call(
            end_kernel,
            "end",
            [(field, F32, HBM), (field, F32, HBM)],
            [VMEM] * 7,
            (arrived, couplings, transfer, basis, residual, total, factor),
            [pltpu.VMEM(field, F32)] * 2 + [wide, dma((8,))],
            SHORT,
        )
    )


def solution(mesh):
    placed = (
        P(("grp", "dev"), None),
        P(("grp", "dev"), None),
        P(("grp", "dev"), None),
        P(("grp", "dev"), None),
        P(("grp", "dev"), None),
        P(("grp", "dev"), None, None, None),
        P(("grp", "dev"), None, None),
        P(("grp", "dev"), None),
        P(("grp", "dev")),
        P("grp", None),
        P("grp", None, None, None),
        P(),
    )
    return jax.shard_map(
        body,
        mesh=mesh,
        in_specs=placed,
        out_specs=(P(("grp", "dev"), None), P(("grp", "dev"), None)),
        check_vma=False,
    )
```

```python
import jax
import jax.numpy as jnp
from jax import lax
from jax.experimental import pallas as pl
from jax.experimental.pallas import tpu as pltpu
from jax.sharding import PartitionSpec as P

LEAF, DIM, OUT, RANK = 512, 64, 256, 128
N_GRP, N_DEV, CPG = 8, 64, 4
FAR1, FAR2 = 4, 4
COLS = OUT // N_DEV
NEAR = 4

KERNEL_LOG2 = -1.4426950408889634 / 32.0
GAP, TOP = 0.5, 8.0

F32, BF16 = jnp.float32, jnp.bfloat16
VMEM = pl.BlockSpec(memory_space=pltpu.VMEM)
SMEM = pl.BlockSpec(memory_space=pltpu.SMEM)
ANY = pl.BlockSpec(memory_space=pl.ANY)
HBM = pl.BlockSpec(memory_space=pltpu.HBM)
LIMIT = 32 * 2**20
SHORT, MID, LONG = 10**7, 10**10, 10**10
ROWS = 128


def dot(a, b, dims=((1,), (0,))):
    return lax.dot_general(a, b, (dims, ((), ())), preferred_element_type=F32)


def call(kernel, name, outs, ins, args, scratch=(), flops=0):
    shapes = [(pltpu.HBM if spec is HBM else jax.ShapeDtypeStruct)(shape, kind) for shape, kind, spec in outs]
    args = [
        pltpu.with_memory_space_constraint(arg, pltpu.HBM) if spec is HBM else arg for arg, spec in zip(args, ins)
    ]
    return pl.pallas_call(
        kernel,
        name=name,
        out_shape=shapes,
        in_specs=ins,
        out_specs=[spec for _, _, spec in outs],
        scratch_shapes=list(scratch),
        compiler_params=pltpu.CompilerParams(vmem_limit_bytes=LIMIT),
        cost_estimate=pl.CostEstimate(flops=flops, bytes_accessed=0, transcendentals=0),
    )(*args)


def started(pairs, sems, first=0):
    copies = [pltpu.make_async_copy(a, b, sems.at[first + i]) for i, (a, b) in enumerate(pairs)]
    for copy in copies:
        copy.start()
    return copies


def wait(copies):
    for copy in copies:
        copy.wait()


def chebyshev(ridge):
    ridge = jnp.full((1, 1), ridge, F32)
    bottom, top = ridge + GAP, ridge + TOP
    centre, spread = (top + bottom) / 2.0, (top - bottom) / 2.0
    sigma = centre / spread
    rho0 = 1.0 / sigma
    rho1 = 1.0 / (2.0 * sigma - rho0)
    rho2 = 1.0 / (2.0 * sigma - rho1)
    first = (rho1 * rho0, 2.0 * rho1 / spread)
    second = (rho2 * rho1, 2.0 * rho2 / spread)
    return ridge, centre, first, second


def to_owners(values, basis, transfer, staged):
    skeleton = dot(values, basis, ((0,), (0,))).astype(BF16)
    uplift = dot(skeleton, transfer)
    skeleton = skeleton.astype(F32)
    for i in range(COLS):
        part = slice(N_DEV * i, N_DEV * (i + 1))
        staged[:, i, :RANK] = skeleton[part]
        staged[:, i, RANK : 2 * RANK] = uplift[part]


def start_kernel(
    ridge, cluster, far_in, rs_in, coords_in, perm_in, basis_in, transfer_in, wc_out, sent_out, placed,
    far, rs, coords, perm, basis, transfer, wc, sent, staged, sems,
):
    copies = started(
        (
            (perm_in, perm), (basis_in, basis), (rs_in, rs), (transfer_in, transfer),
            (coords_in, coords), (far_in, far),
        ),
        sems,
    )
    _, centre, _, _ = chebyshev(ridge[0])
    wait(copies[:2])
    point = lax.broadcasted_iota(jnp.int32, (LEAF, LEAF), 0)
    pick = jnp.where(point == perm[...], 1.0, 0.0).astype(BF16)
    basis_here = dot(pick, basis[...]).astype(BF16)
    placed[...] = basis_here
    wait(copies[2:3])
    values = (rs[...] / centre).astype(BF16)
    wc[:LEAF] = values
    outs = started(((wc.at[pl.ds(0, LEAF)], wc_out.at[pl.ds(0, LEAF)]),), sems, 6)
    wait(copies[3:])
    to_owners(values, basis_here, transfer[0], staged)
    lane = lax.broadcasted_iota(jnp.int32, (N_DEV, RANK), 1)
    told = jnp.where(lane == FAR1, (cluster[0] % CPG).astype(F32), 0.0)
    for k in range(FAR1):
        told = jnp.where(lane == k, (far[0, k] % N_DEV).astype(F32), told)
    for i in range(COLS):
        staged[:, i, 2 * RANK :] = told
    sent[...] = staged[...].astype(BF16)
    outs += started(((sent, sent_out),), sems, 7)
    high = coords[...].astype(BF16)
    low = (coords[...] - high.astype(F32)).astype(BF16)
    both = jnp.concatenate([high, low], axis=0)
    wc[LEAF : LEAF + 2 * DIM] = both[:, :OUT]
    wc[LEAF + 2 * DIM :] = both[:, OUT:]
    rest = pl.ds(LEAF, 4 * DIM)
    outs += started(((wc.at[rest], wc_out.at[rest]),), sems, 8)
    wait(outs)


def owner_sums(staged, told, sums, skeletons, narrow):
    lane = lax.broadcasted_iota(jnp.int32, (N_DEV, RANK), 1).astype(F32)
    member = jnp.where(lane == told[:, FAR1 : FAR1 + 1], 1.0, 0.0).astype(BF16)
    uplifts = jnp.concatenate([staged[:, i, RANK : 2 * RANK] for i in range(COLS)], axis=1).astype(BF16)
    total = dot(member, uplifts, ((0,), (0,)))
    for i in range(COLS):
        narrow[pl.ds(CPG * i, CPG), :] = total[:CPG, RANK * i : RANK * (i + 1)]
    out = narrow[...].astype(BF16)
    for g in range(N_GRP):
        sums[g] = out
    skeletons[...] = jnp.concatenate([staged[:, i, :RANK] for i in range(COLS)], axis=1).astype(BF16)


def sums_first_kernel(arrived, _, sums, told, skeletons, staged, narrow):
    staged[...] = arrived[...].astype(F32)
    told[...] = staged[:, 0, 2 * RANK :]
    owner_sums(staged, told[...], sums, skeletons, narrow)


def sums_kernel(arrived, told, sums, skeletons, staged, narrow):
    staged[...] = arrived[...].astype(F32)
    owner_sums(staged, told[...], sums, skeletons, narrow)


def partners_kernel(skeletons, told, sent, staged):
    lane = lax.broadcasted_iota(jnp.int32, (N_DEV, N_DEV), 1).astype(F32)
    pick = jnp.concatenate(
        [jnp.where(lane == told[:, k : k + 1], 1.0, 0.0) for k in range(FAR1)], axis=0
    ).astype(BF16)
    picked = dot(pick, skeletons[...])
    for k in range(FAR1):
        for i in range(COLS):
            staged[:, i, RANK * k : RANK * (k + 1)] = picked[
                N_DEV * k : N_DEV * (k + 1), RANK * i : RANK * (i + 1)
            ]
    sent[...] = staged[...].astype(BF16)


def couple_kernel(picks, all_sums, blocks, told, partners, sent_out, staged, sent, sems):
    copies = started(((partners, sent_out.at[:, :, pl.ds(0, FAR1 * RANK)]),), sems)
    rows = COLS * CPG
    picked = dot(picks[...], all_sums[...].reshape(N_GRP * rows, RANK)).astype(BF16)
    total = jnp.zeros((CPG * RANK, rows), F32)
    for k in range(FAR2):
        block = blocks[:, k].reshape(CPG * RANK, RANK)
        total += dot(block, picked[rows * k : rows * (k + 1)], ((1,), (1,)))
    own = lax.broadcasted_iota(jnp.int32, (RANK, rows), 1) % CPG
    coupled = jnp.zeros((RANK, rows), F32)
    for c in range(CPG):
        coupled += jnp.where(own == c, total[RANK * c : RANK * (c + 1)], 0.0)
    coupled = coupled.T.astype(BF16)
    lane = lax.broadcasted_iota(jnp.int32, (N_DEV, rows), 1).astype(F32)
    pick = jnp.concatenate(
        [jnp.where(lane == told[:, FAR1 : FAR1 + 1] + CPG * i, 1.0, 0.0) for i in range(COLS)], axis=0
    ).astype(BF16)
    out = dot(pick, coupled)
    for i in range(COLS):
        staged[:, i, :] = out[N_DEV * i : N_DEV * (i + 1)]
    sent[...] = staged[...].astype(BF16)
    wait(copies + started(((sent, sent_out.at[:, :, pl.ds(FAR1 * RANK, RANK)]),), sems, 1))


def local_field(arrived, couplings, transfer, staged):
    staged[...] = arrived[...].astype(F32)
    local = jnp.zeros((OUT, RANK), F32)
    for k in range(FAR1 + 1):
        skeleton = jnp.concatenate(
            [staged[:, i, RANK * k : RANK * (k + 1)] for i in range(COLS)], axis=0
        ).astype(BF16)
        local += dot(skeleton, couplings[0, k] if k < FAR1 else transfer[0], ((1,), (1,)))
    return local.T.astype(BF16)


def middle_kernel(
    arrived, couplings, transfer, basis, residual, direction, factor, w, sent_out, r1, sent, staged, staged_out, sems
):
    local = local_field(arrived, couplings, transfer, staged)
    for r in range(0, LEAF, ROWS):
        part = slice(r, r + ROWS)
        far = dot(basis[part], local)
        r1[part] = residual[part] - far
        w[part] = (direction[part] - factor[:1, :1] * far).astype(BF16)
    to_owners(w[...], basis[...], transfer[0], staged_out)
    sent[...] = staged_out[...].astype(BF16)
    wait(started(((sent, sent_out),), sems))


def end_kernel(
    arrived, couplings, transfer, basis, before_r, before_s, factor, solution_out, residual_out,
    solution, residual, staged, sems,
):
    local = local_field(arrived, couplings, transfer, staged)
    outs = []
    for n, r in enumerate(range(0, LEAF, ROWS)):
        part = slice(r, r + ROWS)
        far = dot(basis[part], local)
        residual[part] = before_r[part] - far
        solution[part] = before_s[part] - factor[:1, :1] * far
        at = pl.ds(r, ROWS)
        outs += started(
            ((residual.at[at], residual_out.at[at]), (solution.at[at], solution_out.at[at])), sems, 2 * n
        )
    wait(outs)


def coordinates(held):
    parts = jnp.concatenate([held[: 2 * DIM], held[2 * DIM :]], axis=1)
    high, low = parts[:DIM], parts[DIM:]
    points = high.astype(F32) + low.astype(F32)
    return high, low, jnp.sum(points * points, axis=0, keepdims=True) * KERNEL_LOG2


def listed(near_list, offset):
    leaf = lax.axis_index("grp") * N_DEV + lax.axis_index("dev")
    hit = near_list[0, 0] == leaf + offset
    for k in range(1, NEAR):
        hit = hit | (near_list[0, k] == leaf + offset)
    return hit


def block_times(here, there, values, total, fresh):
    high, low, norm = here
    left = jnp.concatenate([high, high, low, low], axis=0)
    column = jnp.broadcast_to(norm, (RANK, LEAF)).T[:, :1]
    high, low, across = there
    right = jnp.concatenate([high, low, high, low], axis=0)
    step = 128
    for r in range(0, LEAF, step):
        part = slice(r, r + step)
        inner = dot(left[:, part], right, ((0,), (0,)))
        entries = jnp.exp2((column[part] + across) - (2.0 * KERNEL_LOG2) * inner).astype(BF16)
        product = dot(entries, values)
        total[part] = product if fresh else total[part] + product


def near_products(distance, near_list, mine, places, values, total):
    ahead = distance * (1 - 2 * (lax.axis_index("dev") % 2))
    for i, offset in enumerate((ahead, -ahead)):

        @pl.when(listed(near_list, offset))
        def _():
            block_times(mine, coordinates(places[1 + i]), values[i], total, False)


def near_pairs(places_in, p1, v1, p2, v2, places, values):
    pairs = [(p.at[pl.ds(LEAF, 4 * DIM)], places.at[i]) for i, p in enumerate((places_in, p1, p2))]
    return pairs + [(v.at[pl.ds(0, LEAF)], values.at[i]) for i, v in enumerate((v1, v2))]


def near_1_kernel(near_list, places_in, own, p1, v1, p2, v2, _, total, places, values, sems):
    pairs = near_pairs(places_in, p1, v1, p2, v2, places, values)
    wait(started([*pairs, (own.at[pl.ds(0, LEAF)], values.at[2])], sems))
    mine = coordinates(places[0])
    block_times(mine, mine, values[2], total, True)
    near_products(1, near_list, mine, places, values, total)


def near_2_kernel(
    last, ridge, near_list, places_in, before, p1, v1, p2, v2, rs_in, r1, residual, other, factor,
    total, places, values, rs, sems,
):
    pairs = near_pairs(places_in, p1, v1, p2, v2, places, values)
    copies = started([*pairs, (before, total), (rs_in, rs)], sems)
    if last:
        copies += started(((r1, residual),), sems, 7)
    wait(copies)
    near_products(2, near_list, coordinates(places[0]), places, values, total)
    ridge, centre, first, second = chebyshev(ridge[0])
    d1 = rs[...] / centre
    if last:
        d2 = first[0] * d1 + first[1] * residual[...]
        left = residual[...] - (ridge * d2 + total[...])
        other[...] = d1 + d2 + (second[0] * d2 + second[1] * left)
        factor[...] = jnp.broadcast_to(second[1], factor.shape)
    else:
        left = rs[...] - (ridge * d1 + total[...])
        other[...] = first[0] * d1 + first[1] * left
        factor[...] = jnp.broadcast_to(first[1], factor.shape)
    residual[...] = left


def prepare_kernel(far_clusters, picks):
    rows = COLS * CPG
    row = lax.broadcasted_iota(jnp.int32, (rows, N_GRP * rows), 0)
    lane = lax.broadcasted_iota(jnp.int32, (rows, N_GRP * rows), 1)
    column, cluster = row // CPG, row % CPG
    for k in range(FAR2):
        target = CPG * column
        for c in range(CPG):
            f = far_clusters[c, k]
            target += jnp.where(cluster == c, rows * (f // CPG) + f % CPG, 0)
        picks[rows * k : rows * (k + 1)] = jnp.where(lane == target, 1.0, 0.0).astype(BF16)


def swapped(one, two):
    inner = [(i, i ^ 1) for i in range(N_DEV)]
    outer = [(i, ((i + 1) ^ 1) - 1) for i in range(1, N_DEV - 1)]
    return lax.ppermute(one, "dev", inner), lax.ppermute(two, "dev", outer)


def exchanged(blocks, axis):
    return lax.all_to_all(blocks, axis, split_axis=0, concat_axis=0, tiled=True)


def body(
    coords,
    right_side,
    leaf_perm,
    near_list,
    far_leaves,
    couplings,
    transfer,
    leaf_basis,
    cluster_of,
    far_clusters,
    cluster_couplings,
    ridge_weight,
):
    ridge = ridge_weight.reshape(1)
    field, dma = (LEAF, OUT), pltpu.SemaphoreType.DMA
    payload, partner = (N_DEV, COLS, (FAR1 + 1) * RANK), (N_DEV, COLS, FAR1 * RANK)
    wide = pltpu.VMEM(payload, F32)
    told_too, upward = (N_DEV, COLS, 3 * RANK), (N_DEV, COLS, 2 * RANK)
    sums_shape = (N_GRP, COLS * CPG, RANK)
    narrow = pltpu.VMEM((COLS * CPG, RANK), F32)

    wc, sent, basis = call(
        start_kernel,
        "start",
        [
            ((LEAF + 4 * DIM, OUT), BF16, HBM),
            (told_too, BF16, HBM),
            ((LEAF, RANK), BF16, VMEM),
        ],
        [SMEM] * 2 + [HBM] * 6,
        (ridge, cluster_of, far_leaves, right_side, coords.T, leaf_perm, leaf_basis, transfer),
        [
            pltpu.SMEM((1, FAR1), jnp.int32),
            pltpu.VMEM(field, F32),
            pltpu.VMEM((DIM, LEAF), F32),
            pltpu.VMEM((1, LEAF), jnp.int32),
            pltpu.VMEM((LEAF, RANK), BF16),
            pltpu.VMEM((1, RANK, RANK), BF16),
            pltpu.VMEM((LEAF + 4 * DIM, OUT), BF16),
            pltpu.VMEM(told_too, BF16),
            pltpu.VMEM(told_too, F32),
            dma((9,)),
        ],
        SHORT,
    )

    def near_1(own, first, fields, after):
        (near,) = call(
            near_1_kernel,
            "near_1",
            [(field, F32, VMEM)],
            [SMEM, HBM] + [ANY] * 5 + [HBM],
            (near_list, wc, own, first[0], fields[0], first[1], fields[1], after),
            [pltpu.VMEM((3, 4 * DIM, OUT), BF16), pltpu.VMEM((3, *field), BF16), dma((6,))],
            MID,
        )
        return near

    def near_2(last, near, first, fields, r1):
        return call(
            lambda *refs: near_2_kernel(last, *refs),
            "near_2",
            [(field, F32, VMEM), (field, F32, VMEM), ((8, RANK), F32, VMEM)],
            [SMEM, SMEM, HBM] + [ANY] * 5 + [HBM, ANY],
            (ridge, near_list, wc, near, first[0], fields[0], first[1], fields[1], right_side, r1),
            [
                pltpu.VMEM(field, F32),
                pltpu.VMEM((3, 4 * DIM, OUT), BF16),
                pltpu.VMEM((2, *field), BF16),
                pltpu.VMEM(field, F32),
                dma((8,)),
            ],
            LONG,
        )

    def through_owners(sums, skeletons):
        all_sums = exchanged(sums, "grp")
        (partners,) = call(
            partners_kernel,
            "partners",
            [(partner, BF16, VMEM)],
            [VMEM] * 2,
            (skeletons, told),
            [pltpu.VMEM(partner, F32)],
            SHORT,
        )
        (sent,) = call(
            couple_kernel,
            "couple",
            [(payload, BF16, HBM)],
            [VMEM] * 5,
            (picks, all_sums, cluster_couplings, told, partners),
            [pltpu.VMEM((N_DEV, COLS, RANK), F32), pltpu.VMEM((N_DEV, COLS, RANK), BF16), dma((2,))],
            SHORT,
        )
        return sent, exchanged(sent, "dev")

    arrived = exchanged(sent, "dev")
    (picks,) = call(
        prepare_kernel,
        "prepare",
        [((FAR2 * COLS * CPG, N_GRP * COLS * CPG), BF16, VMEM)],
        [SMEM],
        (far_clusters,),
        flops=SHORT,
    )
    first1 = swapped(wc, wc)
    sums, told, skeletons = call(
        sums_first_kernel,
        "sums_first",
        [(sums_shape, BF16, VMEM), ((N_DEV, RANK), F32, VMEM), ((N_DEV, COLS * RANK), BF16, VMEM)],
        [VMEM, ANY],
        (arrived, picks),
        [pltpu.VMEM(told_too, F32), narrow],
        SHORT,
    )
    sent, arrived = through_owners(sums, skeletons)
    first2 = swapped(*first1[::-1])
    near = near_1(wc, first1, first1, sent)
    residual, direction, factor = near_2(False, near, first2, first2, near)
    w, sent, r1 = call(
        middle_kernel,
        "middle",
        [(field, BF16, VMEM), (upward, BF16, HBM), (field, F32, VMEM)],
        [VMEM] * 7,
        (arrived, couplings, transfer, basis, residual, direction, factor),
        [pltpu.VMEM(upward, BF16), wide, pltpu.VMEM(upward, F32), dma((1,))],
        SHORT,
    )
    arrived = exchanged(sent, "dev")
    fields1 = swapped(w, w)
    sums, skeletons = call(
        sums_kernel,
        "sums",
        [(sums_shape, BF16, VMEM), ((N_DEV, COLS * RANK), BF16, VMEM)],
        [VMEM, VMEM],
        (arrived, told),
        [pltpu.VMEM(upward, F32), narrow],
        SHORT,
    )
    sent, arrived = through_owners(sums, skeletons)
    fields2 = swapped(*fields1[::-1])
    near = near_1(w, first1, fields1, sent)
    residual, total, factor = near_2(True, near, first2, fields2, r1)
    return tuple(
        call(
            end_kernel,
            "end",
            [(field, F32, HBM), (field, F32, HBM)],
            [VMEM] * 7,
            (arrived, couplings, transfer, basis, residual, total, factor),
            [pltpu.VMEM(field, F32)] * 2 + [wide, dma((8,))],
            SHORT,
        )
    )


def solution(mesh):
    placed = (
        P(("grp", "dev"), None),
        P(("grp", "dev"), None),
        P(("grp", "dev"), None),
        P(("grp", "dev"), None),
        P(("grp", "dev"), None),
        P(("grp", "dev"), None, None, None),
        P(("grp", "dev"), None, None),
        P(("grp", "dev"), None),
        P(("grp", "dev")),
        P("grp", None),
        P("grp", None, None, None),
        P(),
    )
    return jax.shard_map(
        body,
        mesh=mesh,
        in_specs=placed,
        out_specs=(P(("grp", "dev"), None), P(("grp", "dev"), None)),
        check_vma=False,
    )
```

```python
import jax
import jax.numpy as jnp
from jax import lax
from jax.experimental import pallas as pl
from jax.experimental.pallas import tpu as pltpu
from jax.sharding import PartitionSpec as P

LEAF, DIM, OUT, RANK = 512, 64, 256, 128
N_GRP, N_DEV, CPG = 8, 64, 4
FAR1, FAR2 = 4, 4
COLS = OUT // N_DEV
NEAR = 4

KERNEL_LOG2 = -1.4426950408889634 / 32.0
GAP, TOP = 0.5, 8.0

F32, BF16 = jnp.float32, jnp.bfloat16
VMEM = pl.BlockSpec(memory_space=pltpu.VMEM)
SMEM = pl.BlockSpec(memory_space=pltpu.SMEM)
ANY = pl.BlockSpec(memory_space=pl.ANY)
HBM = pl.BlockSpec(memory_space=pltpu.HBM)
LIMIT = 32 * 2**20
SHORT, MID, LONG = 10**7, 10**10, 10**10
LATER, LAST = 10**10, 10**7
ROWS = 128


def dot(a, b, dims=((1,), (0,))):
    return lax.dot_general(a, b, (dims, ((), ())), preferred_element_type=F32)


def call(kernel, name, outs, ins, args, scratch=(), flops=0):
    shapes = [(pltpu.HBM if spec is HBM else jax.ShapeDtypeStruct)(shape, kind) for shape, kind, spec in outs]
    args = [
        pltpu.with_memory_space_constraint(arg, pltpu.HBM) if spec is HBM else arg for arg, spec in zip(args, ins)
    ]
    return pl.pallas_call(
        kernel,
        name=name,
        out_shape=shapes,
        in_specs=ins,
        out_specs=[spec for _, _, spec in outs],
        scratch_shapes=list(scratch),
        compiler_params=pltpu.CompilerParams(vmem_limit_bytes=LIMIT),
        cost_estimate=pl.CostEstimate(flops=flops, bytes_accessed=0, transcendentals=0),
    )(*args)


def started(pairs, sems, first=0):
    copies = [pltpu.make_async_copy(a, b, sems.at[first + i]) for i, (a, b) in enumerate(pairs)]
    for copy in copies:
        copy.start()
    return copies


def wait(copies):
    for copy in copies:
        copy.wait()


def chebyshev(ridge):
    ridge = jnp.full((1, 1), ridge, F32)
    bottom, top = ridge + GAP, ridge + TOP
    centre, spread = (top + bottom) / 2.0, (top - bottom) / 2.0
    sigma = centre / spread
    rho0 = 1.0 / sigma
    rho1 = 1.0 / (2.0 * sigma - rho0)
    rho2 = 1.0 / (2.0 * sigma - rho1)
    first = (rho1 * rho0, 2.0 * rho1 / spread)
    second = (rho2 * rho1, 2.0 * rho2 / spread)
    return ridge, centre, first, second


def to_owners(values, basis, transfer, staged):
    skeleton = dot(values, basis, ((0,), (0,))).astype(BF16)
    uplift = dot(skeleton, transfer)
    skeleton = skeleton.astype(F32)
    for i in range(COLS):
        part = slice(N_DEV * i, N_DEV * (i + 1))
        staged[:, i, :RANK] = skeleton[part]
        staged[:, i, RANK : 2 * RANK] = uplift[part]


def start_kernel(
    ridge, cluster, far_in, rs_in, coords_in, perm_in, basis_in, transfer_in, wc_out, sent_out, placed,
    far, rs, coords, perm, basis, transfer, wc, sent, staged, sems,
):
    copies = started(
        (
            (perm_in, perm), (basis_in, basis), (rs_in, rs), (transfer_in, transfer),
            (coords_in, coords), (far_in, far),
        ),
        sems,
    )
    _, centre, _, _ = chebyshev(ridge[0])
    wait(copies[:2])
    point = lax.broadcasted_iota(jnp.int32, (LEAF, LEAF), 0)
    pick = jnp.where(point == perm[...], 1.0, 0.0).astype(BF16)
    basis_here = dot(pick, basis[...]).astype(BF16)
    placed[...] = basis_here
    wait(copies[2:3])
    values = (rs[...] / centre).astype(BF16)
    wc[:LEAF] = values
    outs = started(((wc.at[pl.ds(0, LEAF)], wc_out.at[pl.ds(0, LEAF)]),), sems, 6)
    wait(copies[3:])
    to_owners(values, basis_here, transfer[0], staged)
    lane = lax.broadcasted_iota(jnp.int32, (N_DEV, RANK), 1)
    told = jnp.where(lane == FAR1, (cluster[0] % CPG).astype(F32), 0.0)
    for k in range(FAR1):
        told = jnp.where(lane == k, (far[0, k] % N_DEV).astype(F32), told)
    for i in range(COLS):
        staged[:, i, 2 * RANK :] = told
    sent[...] = staged[...].astype(BF16)
    outs += started(((sent, sent_out),), sems, 7)
    high = coords[...].astype(BF16)
    low = (coords[...] - high.astype(F32)).astype(BF16)
    both = jnp.concatenate([high, low], axis=0)
    wc[LEAF : LEAF + 2 * DIM] = both[:, :OUT]
    wc[LEAF + 2 * DIM :] = both[:, OUT:]
    rest = pl.ds(LEAF, 4 * DIM)
    outs += started(((wc.at[rest], wc_out.at[rest]),), sems, 8)
    wait(outs)


def owner_sums(staged, told, sums, skeletons, narrow):
    lane = lax.broadcasted_iota(jnp.int32, (N_DEV, RANK), 1).astype(F32)
    member = jnp.where(lane == told[:, FAR1 : FAR1 + 1], 1.0, 0.0).astype(BF16)
    uplifts = jnp.concatenate([staged[:, i, RANK : 2 * RANK] for i in range(COLS)], axis=1).astype(BF16)
    total = dot(member, uplifts, ((0,), (0,)))
    for i in range(COLS):
        narrow[pl.ds(CPG * i, CPG), :] = total[:CPG, RANK * i : RANK * (i + 1)]
    out = narrow[...].astype(BF16)
    for g in range(N_GRP):
        sums[g] = out
    skeletons[...] = jnp.concatenate([staged[:, i, :RANK] for i in range(COLS)], axis=1).astype(BF16)


def sums_first_kernel(arrived, _, sums, told, skeletons, staged, narrow):
    staged[...] = arrived[...].astype(F32)
    told[...] = staged[:, 0, 2 * RANK :]
    owner_sums(staged, told[...], sums, skeletons, narrow)


def sums_kernel(arrived, told, sums, skeletons, staged, narrow):
    staged[...] = arrived[...].astype(F32)
    owner_sums(staged, told[...], sums, skeletons, narrow)


def partners_kernel(skeletons, told, sent, staged):
    lane = lax.broadcasted_iota(jnp.int32, (N_DEV, N_DEV), 1).astype(F32)
    pick = jnp.concatenate(
        [jnp.where(lane == told[:, k : k + 1], 1.0, 0.0) for k in range(FAR1)], axis=0
    ).astype(BF16)
    picked = dot(pick, skeletons[...])
    for k in range(FAR1):
        for i in range(COLS):
            staged[:, i, RANK * k : RANK * (k + 1)] = picked[
                N_DEV * k : N_DEV * (k + 1), RANK * i : RANK * (i + 1)
            ]
    sent[...] = staged[...].astype(BF16)


def couple_kernel(picks, all_sums, blocks, told, partners, sent_out, staged, sent, sems):
    copies = started(((partners, sent_out.at[:, :, pl.ds(0, FAR1 * RANK)]),), sems)
    rows = COLS * CPG
    picked = dot(picks[...], all_sums[...].reshape(N_GRP * rows, RANK)).astype(BF16)
    total = jnp.zeros((CPG * RANK, rows), F32)
    for k in range(FAR2):
        block = blocks[:, k].reshape(CPG * RANK, RANK)
        total += dot(block, picked[rows * k : rows * (k + 1)], ((1,), (1,)))
    own = lax.broadcasted_iota(jnp.int32, (RANK, rows), 1) % CPG
    coupled = jnp.zeros((RANK, rows), F32)
    for c in range(CPG):
        coupled += jnp.where(own == c, total[RANK * c : RANK * (c + 1)], 0.0)
    coupled = coupled.T.astype(BF16)
    lane = lax.broadcasted_iota(jnp.int32, (N_DEV, rows), 1).astype(F32)
    pick = jnp.concatenate(
        [jnp.where(lane == told[:, FAR1 : FAR1 + 1] + CPG * i, 1.0, 0.0) for i in range(COLS)], axis=0
    ).astype(BF16)
    out = dot(pick, coupled)
    for i in range(COLS):
        staged[:, i, :] = out[N_DEV * i : N_DEV * (i + 1)]
    sent[...] = staged[...].astype(BF16)
    wait(copies + started(((sent, sent_out.at[:, :, pl.ds(FAR1 * RANK, RANK)]),), sems, 1))


def local_field(arrived, couplings, transfer, staged):
    staged[...] = arrived[...].astype(F32)
    local = jnp.zeros((OUT, RANK), F32)
    for k in range(FAR1 + 1):
        skeleton = jnp.concatenate(
            [staged[:, i, RANK * k : RANK * (k + 1)] for i in range(COLS)], axis=0
        ).astype(BF16)
        local += dot(skeleton, couplings[0, k] if k < FAR1 else transfer[0], ((1,), (1,)))
    return local.T.astype(BF16)


def middle_kernel(
    arrived, couplings, transfer, basis, residual, direction, factor, w, sent_out, r1, sent, staged, staged_out, sems
):
    local = local_field(arrived, couplings, transfer, staged)
    for r in range(0, LEAF, ROWS):
        part = slice(r, r + ROWS)
        far = dot(basis[part], local)
        r1[part] = residual[part] - far
        w[part] = (direction[part] - factor[:1, :1] * far).astype(BF16)
    to_owners(w[...], basis[...], transfer[0], staged_out)
    sent[...] = staged_out[...].astype(BF16)
    wait(started(((sent, sent_out),), sems))


def end_kernel(
    arrived, couplings, transfer, basis, before_r, before_s, factor, solution_out, residual_out,
    solution, residual, staged, sems,
):
    local = local_field(arrived, couplings, transfer, staged)
    outs = []
    for n, r in enumerate(range(0, LEAF, ROWS)):
        part = slice(r, r + ROWS)
        far = dot(basis[part], local)
        residual[part] = before_r[part] - far
        solution[part] = before_s[part] - factor[:1, :1] * far
        at = pl.ds(r, ROWS)
        outs += started(
            ((residual.at[at], residual_out.at[at]), (solution.at[at], solution_out.at[at])), sems, 2 * n
        )
    wait(outs)


def coordinates(held):
    parts = jnp.concatenate([held[: 2 * DIM], held[2 * DIM :]], axis=1)
    high, low = parts[:DIM], parts[DIM:]
    points = high.astype(F32) + low.astype(F32)
    return high, low, jnp.sum(points * points, axis=0, keepdims=True) * KERNEL_LOG2


def listed(near_list, offset):
    leaf = lax.axis_index("grp") * N_DEV + lax.axis_index("dev")
    hit = near_list[0, 0] == leaf + offset
    for k in range(1, NEAR):
        hit = hit | (near_list[0, k] == leaf + offset)
    return hit


def block_times(here, there, values, total, fresh):
    high, low, norm = here
    left = jnp.concatenate([high, high, low, low], axis=0)
    column = jnp.broadcast_to(norm, (RANK, LEAF)).T[:, :1]
    high, low, across = there
    right = jnp.concatenate([high, low, high, low], axis=0)
    step = 128
    for r in range(0, LEAF, step):
        part = slice(r, r + step)
        inner = dot(left[:, part], right, ((0,), (0,)))
        entries = jnp.exp2((column[part] + across) - (2.0 * KERNEL_LOG2) * inner).astype(BF16)
        product = dot(entries, values)
        total[part] = product if fresh else total[part] + product


def add_near(offsets, near_list, mine, places, values, total):
    for i, offset in enumerate(offsets):

        @pl.when(listed(near_list, offset))
        def _():
            block_times(mine, coordinates(places[1 + i]), values[i], total, False)


def offsets_of(swaps):
    ahead = 1 - 2 * (lax.axis_index("dev") % 2)
    return [ahead * way for way in swaps]


def near_1_kernel(swaps, near_list, places_in, own, *refs):
    n = len(swaps)
    total, places, values, sems = refs[2 * n + 1 :]
    pairs = [(p.at[pl.ds(LEAF, 4 * DIM)], places.at[i]) for i, p in enumerate((places_in, *refs[: 2 * n : 2]))]
    pairs += [(v.at[pl.ds(0, LEAF)], values.at[i]) for i, v in enumerate((*refs[1 : 2 * n : 2], own))]
    wait(started(pairs, sems))
    mine = coordinates(places[0])
    block_times(mine, mine, values[n], total, True)
    add_near(offsets_of(swaps), near_list, mine, places, values, total)


def near_2_kernel(swaps, last, ridge, near_list, places_in, before, *refs):
    n = len(swaps)
    rs_in, r1, residual, other, factor, total, places, values, rs, sems = refs[2 * n :]
    pairs = [(p.at[pl.ds(LEAF, 4 * DIM)], places.at[i]) for i, p in enumerate((places_in, *refs[: 2 * n : 2]))]
    pairs += [(v.at[pl.ds(0, LEAF)], values.at[i]) for i, v in enumerate(refs[1 : 2 * n : 2])]
    pairs += [(before, total), (rs_in, rs)] + ([(r1, residual)] if last else [])
    wait(started(pairs, sems))
    add_near(offsets_of(swaps), near_list, coordinates(places[0]), places, values, total)
    ridge, centre, first, second = chebyshev(ridge[0])
    d1 = rs[...] / centre
    if last:
        d2 = first[0] * d1 + first[1] * residual[...]
        left = residual[...] - (ridge * d2 + total[...])
        other[...] = d1 + d2 + (second[0] * d2 + second[1] * left)
        factor[...] = jnp.broadcast_to(second[1], factor.shape)
    else:
        left = rs[...] - (ridge * d1 + total[...])
        other[...] = first[0] * d1 + first[1] * left
        factor[...] = jnp.broadcast_to(first[1], factor.shape)
    residual[...] = left


def prepare_kernel(far_clusters, picks):
    rows = COLS * CPG
    row = lax.broadcasted_iota(jnp.int32, (rows, N_GRP * rows), 0)
    lane = lax.broadcasted_iota(jnp.int32, (rows, N_GRP * rows), 1)
    column, cluster = row // CPG, row % CPG
    for k in range(FAR2):
        target = CPG * column
        for c in range(CPG):
            f = far_clusters[c, k]
            target += jnp.where(cluster == c, rows * (f // CPG) + f % CPG, 0)
        picks[rows * k : rows * (k + 1)] = jnp.where(lane == target, 1.0, 0.0).astype(BF16)


def swapped(one, two):
    inner = [(i, i ^ 1) for i in range(N_DEV)]
    outer = [(i, ((i + 1) ^ 1) - 1) for i in range(1, N_DEV - 1)]
    return lax.ppermute(one, "dev", inner), lax.ppermute(two, "dev", outer)


def exchanged(blocks, axis):
    return lax.all_to_all(blocks, axis, split_axis=0, concat_axis=0, tiled=True)


def body(
    coords,
    right_side,
    leaf_perm,
    near_list,
    far_leaves,
    couplings,
    transfer,
    leaf_basis,
    cluster_of,
    far_clusters,
    cluster_couplings,
    ridge_weight,
):
    ridge = ridge_weight.reshape(1)
    field, dma = (LEAF, OUT), pltpu.SemaphoreType.DMA
    payload, partner = (N_DEV, COLS, (FAR1 + 1) * RANK), (N_DEV, COLS, FAR1 * RANK)
    wide = pltpu.VMEM(payload, F32)
    told_too, upward = (N_DEV, COLS, 3 * RANK), (N_DEV, COLS, 2 * RANK)
    sums_shape = (N_GRP, COLS * CPG, RANK)
    narrow = pltpu.VMEM((COLS * CPG, RANK), F32)

    wc, sent, basis = call(
        start_kernel,
        "start",
        [
            ((LEAF + 4 * DIM, OUT), BF16, HBM),
            (told_too, BF16, HBM),
            ((LEAF, RANK), BF16, VMEM),
        ],
        [SMEM] * 2 + [HBM] * 6,
        (ridge, cluster_of, far_leaves, right_side, coords.T, leaf_perm, leaf_basis, transfer),
        [
            pltpu.SMEM((1, FAR1), jnp.int32),
            pltpu.VMEM(field, F32),
            pltpu.VMEM((DIM, LEAF), F32),
            pltpu.VMEM((1, LEAF), jnp.int32),
            pltpu.VMEM((LEAF, RANK), BF16),
            pltpu.VMEM((1, RANK, RANK), BF16),
            pltpu.VMEM((LEAF + 4 * DIM, OUT), BF16),
            pltpu.VMEM(told_too, BF16),
            pltpu.VMEM(told_too, F32),
            dma((9,)),
        ],
        SHORT,
    )

    def near_1(swaps, own, first, fields, after, flops):
        n = len(swaps)
        (near,) = call(
            lambda *refs: near_1_kernel(swaps, *refs),
            "near_1",
            [(field, F32, VMEM)],
            [SMEM, HBM] + [ANY] * (1 + 2 * n) + [HBM],
            (near_list, wc, own, *[x for pair in zip(first, fields) for x in pair], after),
            [pltpu.VMEM((1 + n, 4 * DIM, OUT), BF16), pltpu.VMEM((1 + n, *field), BF16), dma((2 + 2 * n,))],
            flops,
        )
        return near

    def near_2(swaps, last, near, first, fields, r1, flops):
        n = len(swaps)
        return call(
            lambda *refs: near_2_kernel(swaps, last, *refs),
            "near_2",
            [(field, F32, VMEM), (field, F32, VMEM), ((8, RANK), F32, VMEM)],
            [SMEM, SMEM, HBM] + [ANY] * (1 + 2 * n) + [HBM, ANY],
            (ridge, near_list, wc, near, *[x for pair in zip(first, fields) for x in pair], right_side, r1),
            [
                pltpu.VMEM(field, F32),
                pltpu.VMEM((1 + n, 4 * DIM, OUT), BF16),
                pltpu.VMEM((n, *field), BF16),
                pltpu.VMEM(field, F32),
                dma((4 + 2 * n,)),
            ],
            flops,
        )

    def through_owners(sums, skeletons):
        all_sums = exchanged(sums, "grp")
        (partners,) = call(
            partners_kernel,
            "partners",
            [(partner, BF16, VMEM)],
            [VMEM] * 2,
            (skeletons, told),
            [pltpu.VMEM(partner, F32)],
            SHORT,
        )
        (sent,) = call(
            couple_kernel,
            "couple",
            [(payload, BF16, HBM)],
            [VMEM] * 5,
            (picks, all_sums, cluster_couplings, told, partners),
            [pltpu.VMEM((N_DEV, COLS, RANK), F32), pltpu.VMEM((N_DEV, COLS, RANK), BF16), dma((2,))],
            SHORT,
        )
        return sent, exchanged(sent, "dev")

    arrived = exchanged(sent, "dev")
    (picks,) = call(
        prepare_kernel,
        "prepare",
        [((FAR2 * COLS * CPG, N_GRP * COLS * CPG), BF16, VMEM)],
        [SMEM],
        (far_clusters,),
        flops=SHORT,
    )
    first1 = swapped(wc, wc)
    sums, told, skeletons = call(
        sums_first_kernel,
        "sums_first",
        [(sums_shape, BF16, VMEM), ((N_DEV, RANK), F32, VMEM), ((N_DEV, COLS * RANK), BF16, VMEM)],
        [VMEM, ANY],
        (arrived, picks),
        [pltpu.VMEM(told_too, F32), narrow],
        SHORT,
    )
    sent, arrived = through_owners(sums, skeletons)
    first2 = swapped(*first1[::-1])
    near = near_1((1, -1), wc, first1, first1, sent, MID)
    residual, direction, factor = near_2((2, -2), False, near, first2, first2, near, LONG)
    w, sent, r1 = call(
        middle_kernel,
        "middle",
        [(field, BF16, VMEM), (upward, BF16, HBM), (field, F32, VMEM)],
        [VMEM] * 7,
        (arrived, couplings, transfer, basis, residual, direction, factor),
        [pltpu.VMEM(upward, BF16), wide, pltpu.VMEM(upward, F32), dma((1,))],
        SHORT,
    )
    arrived = exchanged(sent, "dev")
    fields1 = swapped(w, w)
    sums, skeletons = call(
        sums_kernel,
        "sums",
        [(sums_shape, BF16, VMEM), ((N_DEV, COLS * RANK), BF16, VMEM)],
        [VMEM, VMEM],
        (arrived, told),
        [pltpu.VMEM(upward, F32), narrow],
        SHORT,
    )
    sent, arrived = through_owners(sums, skeletons)
    fields2 = swapped(*fields1[::-1])
    near = near_1((1, -1, 2), w, (*first1, first2[0]), (*fields1, fields2[0]), sent, LATER)
    residual, total, factor = near_2((-2,), True, near, first2[1:], fields2[1:], r1, LAST)
    return tuple(
        call(
            end_kernel,
            "end",
            [(field, F32, HBM), (field, F32, HBM)],
            [VMEM] * 7,
            (arrived, couplings, transfer, basis, residual, total, factor),
            [pltpu.VMEM(field, F32)] * 2 + [wide, dma((8,))],
            SHORT,
        )
    )


def solution(mesh):
    placed = (
        P(("grp", "dev"), None),
        P(("grp", "dev"), None),
        P(("grp", "dev"), None),
        P(("grp", "dev"), None),
        P(("grp", "dev"), None),
        P(("grp", "dev"), None, None, None),
        P(("grp", "dev"), None, None),
        P(("grp", "dev"), None),
        P(("grp", "dev")),
        P("grp", None),
        P("grp", None, None, None),
        P(),
    )
    return jax.shard_map(
        body,
        mesh=mesh,
        in_specs=placed,
        out_specs=(P(("grp", "dev"), None), P(("grp", "dev"), None)),
        check_vma=False,
    )
```

```python
import jax
import jax.numpy as jnp
from jax import lax
from jax.experimental import pallas as pl
from jax.experimental.pallas import tpu as pltpu
from jax.sharding import PartitionSpec as P

LEAF, DIM, OUT, RANK = 512, 64, 256, 128
N_GRP, N_DEV, CPG = 8, 64, 4
FAR1, FAR2 = 4, 4
COLS = OUT // N_DEV
NEAR = 4

KERNEL_LOG2 = -1.4426950408889634 / 32.0
GAP, TOP = 0.5, 8.0

F32, BF16 = jnp.float32, jnp.bfloat16
VMEM = pl.BlockSpec(memory_space=pltpu.VMEM)
SMEM = pl.BlockSpec(memory_space=pltpu.SMEM)
ANY = pl.BlockSpec(memory_space=pl.ANY)
HBM = pl.BlockSpec(memory_space=pltpu.HBM)
LIMIT = 32 * 2**20
SHORT = 10**7
LATER, LAST = 10**10, 10**7
ROWS = 128


def dot(a, b, dims=((1,), (0,))):
    return lax.dot_general(a, b, (dims, ((), ())), preferred_element_type=F32)


def call(kernel, name, outs, ins, args, scratch=(), flops=0):
    shapes = [(pltpu.HBM if spec is HBM else jax.ShapeDtypeStruct)(shape, kind) for shape, kind, spec in outs]
    args = [
        pltpu.with_memory_space_constraint(arg, pltpu.HBM) if spec is HBM else arg for arg, spec in zip(args, ins)
    ]
    return pl.pallas_call(
        kernel,
        name=name,
        out_shape=shapes,
        in_specs=ins,
        out_specs=[spec for _, _, spec in outs],
        scratch_shapes=list(scratch),
        compiler_params=pltpu.CompilerParams(vmem_limit_bytes=LIMIT),
        cost_estimate=pl.CostEstimate(flops=flops, bytes_accessed=0, transcendentals=0),
    )(*args)


def started(pairs, sems, first=0):
    copies = [pltpu.make_async_copy(a, b, sems.at[first + i]) for i, (a, b) in enumerate(pairs)]
    for copy in copies:
        copy.start()
    return copies


def wait(copies):
    for copy in copies:
        copy.wait()


def chebyshev(ridge):
    ridge = jnp.full((1, 1), ridge, F32)
    bottom, top = ridge + GAP, ridge + TOP
    centre, spread = (top + bottom) / 2.0, (top - bottom) / 2.0
    sigma = centre / spread
    rho0 = 1.0 / sigma
    rho1 = 1.0 / (2.0 * sigma - rho0)
    rho2 = 1.0 / (2.0 * sigma - rho1)
    first = (rho1 * rho0, 2.0 * rho1 / spread)
    second = (rho2 * rho1, 2.0 * rho2 / spread)
    return ridge, centre, first, second


def to_owners(values, basis, transfer, staged):
    skeleton = dot(values, basis, ((0,), (0,))).astype(BF16)
    uplift = dot(skeleton, transfer)
    skeleton = skeleton.astype(F32)
    for i in range(COLS):
        part = slice(N_DEV * i, N_DEV * (i + 1))
        staged[:, i, :RANK] = skeleton[part]
        staged[:, i, RANK : 2 * RANK] = uplift[part]


def start_kernel(
    ridge, cluster, far_in, rs_in, coords_in, perm_in, basis_in, transfer_in, wc_out, sent_out, placed,
    far, rs, coords, perm, basis, transfer, wc, sent, staged, sems,
):
    copies = started(
        (
            (perm_in, perm), (basis_in, basis), (rs_in, rs), (transfer_in, transfer),
            (coords_in, coords), (far_in, far),
        ),
        sems,
    )
    _, centre, _, _ = chebyshev(ridge[0])
    wait(copies[:2])
    point = lax.broadcasted_iota(jnp.int32, (LEAF, LEAF), 0)
    pick = jnp.where(point == perm[...], 1.0, 0.0).astype(BF16)
    basis_here = dot(pick, basis[...]).astype(BF16)
    placed[...] = basis_here
    wait(copies[2:3])
    values = (rs[...] / centre).astype(BF16)
    wc[:LEAF] = values
    outs = started(((wc.at[pl.ds(0, LEAF)], wc_out.at[pl.ds(0, LEAF)]),), sems, 6)
    wait(copies[3:])
    to_owners(values, basis_here, transfer[0], staged)
    lane = lax.broadcasted_iota(jnp.int32, (N_DEV, RANK), 1)
    told = jnp.where(lane == FAR1, (cluster[0] % CPG).astype(F32), 0.0)
    for k in range(FAR1):
        told = jnp.where(lane == k, (far[0, k] % N_DEV).astype(F32), told)
    for i in range(COLS):
        staged[:, i, 2 * RANK :] = told
    sent[...] = staged[...].astype(BF16)
    outs += started(((sent, sent_out),), sems, 7)
    high = coords[...].astype(BF16)
    low = (coords[...] - high.astype(F32)).astype(BF16)
    both = jnp.concatenate([high, low], axis=0)
    wc[LEAF : LEAF + 2 * DIM] = both[:, :OUT]
    wc[LEAF + 2 * DIM :] = both[:, OUT:]
    rest = pl.ds(LEAF, 4 * DIM)
    outs += started(((wc.at[rest], wc_out.at[rest]),), sems, 8)
    wait(outs)


def owner_sums(staged, told, sums, skeletons, narrow):
    lane = lax.broadcasted_iota(jnp.int32, (N_DEV, RANK), 1).astype(F32)
    member = jnp.where(lane == told[:, FAR1 : FAR1 + 1], 1.0, 0.0).astype(BF16)
    uplifts = jnp.concatenate([staged[:, i, RANK : 2 * RANK] for i in range(COLS)], axis=1).astype(BF16)
    total = dot(member, uplifts, ((0,), (0,)))
    for i in range(COLS):
        narrow[pl.ds(CPG * i, CPG), :] = total[:CPG, RANK * i : RANK * (i + 1)]
    out = narrow[...].astype(BF16)
    for g in range(N_GRP):
        sums[g] = out
    skeletons[...] = jnp.concatenate([staged[:, i, :RANK] for i in range(COLS)], axis=1).astype(BF16)


def sums_first_kernel(arrived, _, sums, told, skeletons, staged, narrow):
    staged[...] = arrived[...].astype(F32)
    told[...] = staged[:, 0, 2 * RANK :]
    owner_sums(staged, told[...], sums, skeletons, narrow)


def sums_kernel(arrived, told, sums, skeletons, staged, narrow):
    staged[...] = arrived[...].astype(F32)
    owner_sums(staged, told[...], sums, skeletons, narrow)


def partners_kernel(skeletons, told, sent, staged):
    lane = lax.broadcasted_iota(jnp.int32, (N_DEV, N_DEV), 1).astype(F32)
    pick = jnp.concatenate(
        [jnp.where(lane == told[:, k : k + 1], 1.0, 0.0) for k in range(FAR1)], axis=0
    ).astype(BF16)
    picked = dot(pick, skeletons[...])
    for k in range(FAR1):
        for i in range(COLS):
            staged[:, i, RANK * k : RANK * (k + 1)] = picked[
                N_DEV * k : N_DEV * (k + 1), RANK * i : RANK * (i + 1)
            ]
    sent[...] = staged[...].astype(BF16)


def couple_kernel(picks, all_sums, blocks, told, partners, sent_out, staged, sent, sems):
    copies = started(((partners, sent_out.at[:, :, pl.ds(0, FAR1 * RANK)]),), sems)
    rows = COLS * CPG
    picked = dot(picks[...], all_sums[...].reshape(N_GRP * rows, RANK)).astype(BF16)
    total = jnp.zeros((CPG * RANK, rows), F32)
    for k in range(FAR2):
        block = blocks[:, k].reshape(CPG * RANK, RANK)
        total += dot(block, picked[rows * k : rows * (k + 1)], ((1,), (1,)))
    own = lax.broadcasted_iota(jnp.int32, (RANK, rows), 1) % CPG
    coupled = jnp.zeros((RANK, rows), F32)
    for c in range(CPG):
        coupled += jnp.where(own == c, total[RANK * c : RANK * (c + 1)], 0.0)
    coupled = coupled.T.astype(BF16)
    lane = lax.broadcasted_iota(jnp.int32, (N_DEV, rows), 1).astype(F32)
    pick = jnp.concatenate(
        [jnp.where(lane == told[:, FAR1 : FAR1 + 1] + CPG * i, 1.0, 0.0) for i in range(COLS)], axis=0
    ).astype(BF16)
    out = dot(pick, coupled)
    for i in range(COLS):
        staged[:, i, :] = out[N_DEV * i : N_DEV * (i + 1)]
    sent[...] = staged[...].astype(BF16)
    wait(copies + started(((sent, sent_out.at[:, :, pl.ds(FAR1 * RANK, RANK)]),), sems, 1))


def local_field(arrived, couplings, transfer, staged):
    staged[...] = arrived[...].astype(F32)
    local = jnp.zeros((OUT, RANK), F32)
    for k in range(FAR1 + 1):
        skeleton = jnp.concatenate(
            [staged[:, i, RANK * k : RANK * (k + 1)] for i in range(COLS)], axis=0
        ).astype(BF16)
        local += dot(skeleton, couplings[0, k] if k < FAR1 else transfer[0], ((1,), (1,)))
    return local.T.astype(BF16)


def middle_kernel(
    arrived, couplings, transfer, basis, residual, direction, factor, w, sent_out, r1, sent, staged, staged_out, sems
):
    local = local_field(arrived, couplings, transfer, staged)
    for r in range(0, LEAF, ROWS):
        part = slice(r, r + ROWS)
        far = dot(basis[part], local)
        r1[part] = residual[part] - far
        w[part] = (direction[part] - factor[:1, :1] * far).astype(BF16)
    to_owners(w[...], basis[...], transfer[0], staged_out)
    sent[...] = staged_out[...].astype(BF16)
    wait(started(((sent, sent_out),), sems))


def end_kernel(
    arrived, couplings, transfer, basis, before_r, before_s, factor, solution_out, residual_out,
    solution, residual, staged, sems,
):
    local = local_field(arrived, couplings, transfer, staged)
    outs = []
    for n, r in enumerate(range(0, LEAF, ROWS)):
        part = slice(r, r + ROWS)
        far = dot(basis[part], local)
        residual[part] = before_r[part] - far
        solution[part] = before_s[part] - factor[:1, :1] * far
        at = pl.ds(r, ROWS)
        outs += started(
            ((residual.at[at], residual_out.at[at]), (solution.at[at], solution_out.at[at])), sems, 2 * n
        )
    wait(outs)


def coordinates(held):
    parts = jnp.concatenate([held[: 2 * DIM], held[2 * DIM :]], axis=1)
    high, low = parts[:DIM], parts[DIM:]
    points = high.astype(F32) + low.astype(F32)
    return high, low, jnp.sum(points * points, axis=0, keepdims=True) * KERNEL_LOG2


def listed(near_list, offset):
    leaf = lax.axis_index("grp") * N_DEV + lax.axis_index("dev")
    hit = near_list[0, 0] == leaf + offset
    for k in range(1, NEAR):
        hit = hit | (near_list[0, k] == leaf + offset)
    return hit


def block_times(here, there, values, total, fresh):
    high, low, norm = here
    left = jnp.concatenate([high, high, low, low], axis=0)
    column = jnp.broadcast_to(norm, (RANK, LEAF)).T[:, :1]
    high, low, across = there
    right = jnp.concatenate([high, low, high, low], axis=0)
    step = 128
    for r in range(0, LEAF, step):
        part = slice(r, r + step)
        inner = dot(left[:, part], right, ((0,), (0,)))
        entries = jnp.exp2((column[part] + across) - (2.0 * KERNEL_LOG2) * inner).astype(BF16)
        product = dot(entries, values)
        total[part] = product if fresh else total[part] + product


def add_near(offsets, near_list, mine, places, values, total):
    for i, offset in enumerate(offsets):

        @pl.when(listed(near_list, offset))
        def _():
            block_times(mine, coordinates(places[1 + i]), values[i], total, False)


def offsets_of(swaps):
    ahead = 1 - 2 * (lax.axis_index("dev") % 2)
    return [ahead * way for way in swaps]


def near_1_kernel(swaps, near_list, places_in, own, *refs):
    n = len(swaps)
    total, places, values, sems = refs[2 * n + 1 :]
    pairs = [(p.at[pl.ds(LEAF, 4 * DIM)], places.at[i]) for i, p in enumerate((places_in, *refs[: 2 * n : 2]))]
    pairs += [(v.at[pl.ds(0, LEAF)], values.at[i]) for i, v in enumerate((*refs[1 : 2 * n : 2], own))]
    wait(started(pairs, sems))
    mine = coordinates(places[0])
    block_times(mine, mine, values[n], total, True)
    add_near(offsets_of(swaps), near_list, mine, places, values, total)


def near_2_kernel(swaps, last, ridge, near_list, places_in, before, *refs):
    n = len(swaps)
    rs_in, r1, residual, other, factor, total, places, values, rs, sems = refs[2 * n :]
    pairs = [(p.at[pl.ds(LEAF, 4 * DIM)], places.at[i]) for i, p in enumerate((places_in, *refs[: 2 * n : 2]))]
    pairs += [(v.at[pl.ds(0, LEAF)], values.at[i]) for i, v in enumerate(refs[1 : 2 * n : 2])]
    pairs += [(before, total), (rs_in, rs)] + ([(r1, residual)] if last else [])
    wait(started(pairs, sems))
    add_near(offsets_of(swaps), near_list, coordinates(places[0]), places, values, total)
    ridge, centre, first, second = chebyshev(ridge[0])
    d1 = rs[...] / centre
    if last:
        d2 = first[0] * d1 + first[1] * residual[...]
        left = residual[...] - (ridge * d2 + total[...])
        other[...] = d1 + d2 + (second[0] * d2 + second[1] * left)
        factor[...] = jnp.broadcast_to(second[1], factor.shape)
    else:
        left = rs[...] - (ridge * d1 + total[...])
        other[...] = first[0] * d1 + first[1] * left
        factor[...] = jnp.broadcast_to(first[1], factor.shape)
    residual[...] = left


def prepare_kernel(far_clusters, picks):
    rows = COLS * CPG
    row = lax.broadcasted_iota(jnp.int32, (rows, N_GRP * rows), 0)
    lane = lax.broadcasted_iota(jnp.int32, (rows, N_GRP * rows), 1)
    column, cluster = row // CPG, row % CPG
    for k in range(FAR2):
        target = CPG * column
        for c in range(CPG):
            f = far_clusters[c, k]
            target += jnp.where(cluster == c, rows * (f // CPG) + f % CPG, 0)
        picks[rows * k : rows * (k + 1)] = jnp.where(lane == target, 1.0, 0.0).astype(BF16)


def swapped(one, two):
    inner = [(i, i ^ 1) for i in range(N_DEV)]
    outer = [(i, ((i + 1) ^ 1) - 1) for i in range(1, N_DEV - 1)]
    return lax.ppermute(one, "dev", inner), lax.ppermute(two, "dev", outer)


def exchanged(blocks, axis):
    return lax.all_to_all(blocks, axis, split_axis=0, concat_axis=0, tiled=True)


def body(
    coords,
    right_side,
    leaf_perm,
    near_list,
    far_leaves,
    couplings,
    transfer,
    leaf_basis,
    cluster_of,
    far_clusters,
    cluster_couplings,
    ridge_weight,
):
    ridge = ridge_weight.reshape(1)
    field, dma = (LEAF, OUT), pltpu.SemaphoreType.DMA
    payload, partner = (N_DEV, COLS, (FAR1 + 1) * RANK), (N_DEV, COLS, FAR1 * RANK)
    wide = pltpu.VMEM(payload, F32)
    told_too, upward = (N_DEV, COLS, 3 * RANK), (N_DEV, COLS, 2 * RANK)
    sums_shape = (N_GRP, COLS * CPG, RANK)
    narrow = pltpu.VMEM((COLS * CPG, RANK), F32)

    wc, sent, basis = call(
        start_kernel,
        "start",
        [
            ((LEAF + 4 * DIM, OUT), BF16, HBM),
            (told_too, BF16, HBM),
            ((LEAF, RANK), BF16, VMEM),
        ],
        [SMEM] * 2 + [HBM] * 6,
        (ridge, cluster_of, far_leaves, right_side, coords.T, leaf_perm, leaf_basis, transfer),
        [
            pltpu.SMEM((1, FAR1), jnp.int32),
            pltpu.VMEM(field, F32),
            pltpu.VMEM((DIM, LEAF), F32),
            pltpu.VMEM((1, LEAF), jnp.int32),
            pltpu.VMEM((LEAF, RANK), BF16),
            pltpu.VMEM((1, RANK, RANK), BF16),
            pltpu.VMEM((LEAF + 4 * DIM, OUT), BF16),
            pltpu.VMEM(told_too, BF16),
            pltpu.VMEM(told_too, F32),
            dma((9,)),
        ],
        SHORT,
    )

    def near_1(swaps, own, first, fields, after, flops):
        n = len(swaps)
        (near,) = call(
            lambda *refs: near_1_kernel(swaps, *refs),
            "near_1",
            [(field, F32, VMEM)],
            [SMEM, HBM] + [ANY] * (1 + 2 * n) + [HBM],
            (near_list, wc, own, *[x for pair in zip(first, fields) for x in pair], after),
            [pltpu.VMEM((1 + n, 4 * DIM, OUT), BF16), pltpu.VMEM((1 + n, *field), BF16), dma((2 + 2 * n,))],
            flops,
        )
        return near

    def near_2(swaps, last, near, first, fields, r1, flops):
        n = len(swaps)
        return call(
            lambda *refs: near_2_kernel(swaps, last, *refs),
            "near_2",
            [(field, F32, VMEM), (field, F32, VMEM), ((8, RANK), F32, VMEM)],
            [SMEM, SMEM, HBM] + [ANY] * (1 + 2 * n) + [HBM, ANY],
            (ridge, near_list, wc, near, *[x for pair in zip(first, fields) for x in pair], right_side, r1),
            [
                pltpu.VMEM(field, F32),
                pltpu.VMEM((1 + n, 4 * DIM, OUT), BF16),
                pltpu.VMEM((n, *field), BF16),
                pltpu.VMEM(field, F32),
                dma((4 + 2 * n,)),
            ],
            flops,
        )

    def through_owners(sums, skeletons):
        all_sums = exchanged(sums, "grp")
        (partners,) = call(
            partners_kernel,
            "partners",
            [(partner, BF16, VMEM)],
            [VMEM] * 2,
            (skeletons, told),
            [pltpu.VMEM(partner, F32)],
            SHORT,
        )
        (sent,) = call(
            couple_kernel,
            "couple",
            [(payload, BF16, HBM)],
            [VMEM] * 5,
            (picks, all_sums, cluster_couplings, told, partners),
            [pltpu.VMEM((N_DEV, COLS, RANK), F32), pltpu.VMEM((N_DEV, COLS, RANK), BF16), dma((2,))],
            SHORT,
        )
        return sent, exchanged(sent, "dev")

    arrived = exchanged(sent, "dev")
    (picks,) = call(
        prepare_kernel,
        "prepare",
        [((FAR2 * COLS * CPG, N_GRP * COLS * CPG), BF16, VMEM)],
        [SMEM],
        (far_clusters,),
        flops=SHORT,
    )
    first1 = swapped(wc, wc)
    sums, told, skeletons = call(
        sums_first_kernel,
        "sums_first",
        [(sums_shape, BF16, VMEM), ((N_DEV, RANK), F32, VMEM), ((N_DEV, COLS * RANK), BF16, VMEM)],
        [VMEM, ANY],
        (arrived, picks),
        [pltpu.VMEM(told_too, F32), narrow],
        SHORT,
    )
    sent, arrived = through_owners(sums, skeletons)
    first2 = swapped(*first1[::-1])
    near = near_1((1, -1, 2), wc, (*first1, first2[0]), (*first1, first2[0]), sent, LATER)
    residual, direction, factor = near_2((-2,), False, near, first2[1:], first2[1:], near, LAST)
    w, sent, r1 = call(
        middle_kernel,
        "middle",
        [(field, BF16, VMEM), (upward, BF16, HBM), (field, F32, VMEM)],
        [VMEM] * 7,
        (arrived, couplings, transfer, basis, residual, direction, factor),
        [pltpu.VMEM(upward, BF16), wide, pltpu.VMEM(upward, F32), dma((1,))],
        SHORT,
    )
    arrived = exchanged(sent, "dev")
    fields1 = swapped(w, w)
    sums, skeletons = call(
        sums_kernel,
        "sums",
        [(sums_shape, BF16, VMEM), ((N_DEV, COLS * RANK), BF16, VMEM)],
        [VMEM, VMEM],
        (arrived, told),
        [pltpu.VMEM(upward, F32), narrow],
        SHORT,
    )
    sent, arrived = through_owners(sums, skeletons)
    fields2 = swapped(*fields1[::-1])
    near = near_1((1, -1, 2), w, (*first1, first2[0]), (*fields1, fields2[0]), sent, LATER)
    residual, total, factor = near_2((-2,), True, near, first2[1:], fields2[1:], r1, LAST)
    return tuple(
        call(
            end_kernel,
            "end",
            [(field, F32, HBM), (field, F32, HBM)],
            [VMEM] * 7,
            (arrived, couplings, transfer, basis, residual, total, factor),
            [pltpu.VMEM(field, F32)] * 2 + [wide, dma((8,))],
            SHORT,
        )
    )


def solution(mesh):
    placed = (
        P(("grp", "dev"), None),
        P(("grp", "dev"), None),
        P(("grp", "dev"), None),
        P(("grp", "dev"), None),
        P(("grp", "dev"), None),
        P(("grp", "dev"), None, None, None),
        P(("grp", "dev"), None, None),
        P(("grp", "dev"), None),
        P(("grp", "dev")),
        P("grp", None),
        P("grp", None, None, None),
        P(),
    )
    return jax.shard_map(
        body,
        mesh=mesh,
        in_specs=placed,
        out_specs=(P(("grp", "dev"), None), P(("grp", "dev"), None)),
        check_vma=False,
    )
```
